32 devices in a mesh: dp: 8 (over z, y), head: 4 (over x, core).
Axes of the slice: x: 2, y: 2, z: 4, core: 2. Of those that a mesh axis runs over, the one named last changes fastest.
Arguments:
- tokens: bfloat16 [50176, 384], P(('dp', 'head')), may hold values from -6 to 6
- crop_ids: int32 [50176], P('dp'), may hold values from 0 to 1023, as said below
- grad_out: bfloat16 [50176, 384], P(('dp', 'head')), may hold values from -6 to 6
- query_key_value: float32 [3, 384, 384], P(None, 'dp', 'head'), may hold values from -0.3125 to 0.3125
- output_weight: float32 [384, 384], P('head', 'dp'), may hold values from -1.25 to 1.25
- expand_weight: float32 [384, 1536], P('dp', 'head'), may hold values from -0.3125 to 0.3125
- contract_weight: float32 [1536, 384], P('head', 'dp'), may hold values from -0.15625 to 0.15625
- query_value_bias: float32 [2, 384], P(None, 'head'), may hold values from -3 to 3
- expand_bias: float32 [1536], P('head'), may hold values from -3 to 3
- position_table: float32 [169, 12], P(None, 'head'), may hold values from -4 to 4
- norm_params: float32 [6, 384], replicated, may hold values from -0.5 to 1.4
- query_key_value_moment: float32 [3, 384, 384], P(None, 'dp', 'head'), may hold values from -80 to 80
- query_key_value_square: float32 [3, 384, 384], P(None, 'dp', 'head'), may hold values from 6.272 to 100.352
- output_weight_moment: float32 [384, 384], P('head', 'dp'), may hold values from -80 to 80
- output_weight_square: float32 [384, 384], P('head', 'dp'), may hold values from 6.272 to 100.352
- expand_weight_moment: float32 [384, 1536], P('dp', 'head'), may hold values from -80 to 80
- expand_weight_square: float32 [384, 1536], P('dp', 'head'), may hold values from 6.272 to 100.352
- contract_weight_moment: float32 [1536, 384], P('head', 'dp'), may hold values from -80 to 80
- contract_weight_square: float32 [1536, 384], P('head', 'dp'), may hold values from 6.272 to 100.352
- query_value_bias_moment: float32 [2, 384], P(None, 'head'), may hold values from -80 to 80
- query_value_bias_square: float32 [2, 384], P(None, 'head'), may hold values from 6.272 to 100.352
- expand_bias_moment: float32 [1536], P('head'), may hold values from -80 to 80
- expand_bias_square: float32 [1536], P('head'), may hold values from 6.272 to 100.352
- position_table_moment: float32 [169, 12], P(None, 'head'), may hold values from -80 to 80
- position_table_square: float32 [169, 12], P(None, 'head'), may hold values from 6.272 to 100.352
- norm_params_moment: float32 [6, 384], replicated, may hold values from -160 to 160
- norm_params_square: float32 [6, 384], replicated, may hold values from 25.088 to 401.408
Outputs:
- block_out: bfloat16 [50176, 384], P(('dp', 'head'))
- grad_tokens: float32 [50176, 384], P(('dp', 'head'))
- query_key_value_updated: float32 [3, 384, 384], P(None, 'dp', 'head')
- query_key_value_moment_next: float32 [3, 384, 384], P(None, 'dp', 'head')
- query_key_value_square_next: float32 [3, 384, 384], P(None, 'dp', 'head')
- output_weight_updated: float32 [384, 384], P('head', 'dp')
- output_weight_moment_next: float32 [384, 384], P('head', 'dp')
- output_weight_square_next: float32 [384, 384], P('head', 'dp')
- expand_weight_updated: float32 [384, 1536], P('dp', 'head')
- expand_weight_moment_next: float32 [384, 1536], P('dp', 'head')
- expand_weight_square_next: float32 [384, 1536], P('dp', 'head')
- contract_weight_updated: float32 [1536, 384], P('head', 'dp')
- contract_weight_moment_next: float32 [1536, 384], P('head', 'dp')
- contract_weight_square_next: float32 [1536, 384], P('head', 'dp')
- query_value_bias_updated: float32 [2, 384], P(None, 'head')
- query_value_bias_moment_next: float32 [2, 384], P(None, 'head')
- query_value_bias_square_next: float32 [2, 384], P(None, 'head')
- expand_bias_updated: float32 [1536], P('head')
- expand_bias_moment_next: float32 [1536], P('head')
- expand_bias_square_next: float32 [1536], P('head')
- position_table_updated: float32 [169, 12], P(None, 'head')
- position_table_moment_next: float32 [169, 12], P(None, 'head')
- position_table_square_next: float32 [169, 12], P(None, 'head')
- norm_params_updated: float32 [6, 384], replicated
- norm_params_moment_next: float32 [6, 384], replicated
- norm_params_square_next: float32 [6, 384], replicated
The draws below stay inside these ranges and needn't reach their ends.
Inputs may be any that keep to these rules, and one draw needn't show every extreme that they name: `crop_ids`: each canvas is cut by one row and one column, each drawn from 4 to 10, into four rectangular crops; crop numbers are 4 * canvas + quadrant.
All inputs are finite; a program needn't handle non-finite values.
Results may differ from the reference program's by a relative error of at most 0.015.
Values may be sent and summed in bfloat16 or wider, within the bound.
No kernel may reach another device: no remote copies, remote signals or barrier semaphores. Data moves between devices by JAX's collectives and lax.ppermute only.
A program may use at most 128 MiB of HBM per device.

```python
import math
import jax
import jax.numpy as jnp
from jax import lax

WIDTH = 384
HEADS = 12
HEAD_DIM = 32
HIDDEN_SIZE = 1536
WINDOW = 7
SIDE = 14
SHIFT = 3
STEP = 10
TABLE = 169
CANVASES = 256
TOKENS = 50176


def draw_crop_ids(key, part):
    key = jax.random.fold_in(key, 11)
    row_key, col_key = jax.random.split(key)
    cut_rows = jax.random.randint(row_key, (CANVASES, 1, 1), 4, 11)
    cut_cols = jax.random.randint(col_key, (CANVASES, 1, 1), 4, 11)
    coords = jnp.arange(SIDE, dtype=jnp.int32)
    lower = (coords[None, :, None] >= cut_rows).astype(jnp.int32)
    righter = (coords[None, None, :] >= cut_cols).astype(jnp.int32)
    base_ids = jnp.arange(CANVASES, dtype=jnp.int32)[:, None, None] * 4
    return (base_ids + 2 * lower + righter).reshape(TOKENS)


def draw_norm_params(key, part):
    key = jax.random.fold_in(key, 7)
    spread = jax.random.uniform(key, (6, WIDTH), jnp.float32, -1.0, 1.0)
    row_ids = jnp.arange(6)[:, None]
    is_gain = (row_ids == 0) | (row_ids == 2)
    return jnp.where(is_gain, 1.0 + 0.4 * spread, 0.5 * spread)


def level_of(rng, shape, cuts, least, top_value):
    factor_of = 1.0
    for dim, parts in cuts:
        draws = jax.random.uniform(jax.random.fold_in(jax.random.fold_in(rng, 6), dim), (parts,), jnp.float32, least / len(cuts), top_value / len(cuts))
        factor_of = factor_of * jnp.repeat(jnp.exp(draws), shape[dim] // parts).reshape((-1,) + (1,) * (len(shape) - 1 - dim))
    return factor_of


def scatter_about(stream_key, shape, scale, limit, cuts=(), kind=jnp.bfloat16):
    array = jax.random.normal(stream_key, shape, jnp.float32) * scale
    if len(cuts) > 0:
        array = level_of(stream_key, shape, cuts, -0.22, 0.18) * array
    return jnp.clip(array, min=-limit, max=limit).astype(kind)


def setup_inputs(seed: int = 0) -> dict:
    seeds = jax.random.split(jax.random.key(seed), 28)
    return {
        "tokens": scatter_about(seeds[0], (TOKENS, WIDTH), 1.0, 6.0, ((0, 32),)),
        "crop_ids": draw_crop_ids(jax.random.fold_in(seeds[27], 71), 0),
        "grad_out": scatter_about(seeds[2], (TOKENS, WIDTH), 1.0, 6.0, ((0, 32),)),
        "query_key_value": scatter_about(seeds[3], (3, WIDTH, WIDTH), WIDTH ** -0.5, 0.3125, ((1, 8), (2, 4)), jnp.float32),
        "output_weight": scatter_about(seeds[4], (WIDTH, WIDTH), (WIDTH // 16) ** -0.5, 1.25, ((0, 4), (1, 8)), jnp.float32),
        "expand_weight": scatter_about(seeds[5], (WIDTH, HIDDEN_SIZE), WIDTH ** -0.5, 0.3125, ((0, 8), (1, 4)), jnp.float32),
        "contract_weight": scatter_about(seeds[6], (HIDDEN_SIZE, WIDTH), HIDDEN_SIZE ** -0.5, 0.15625, ((0, 4), (1, 8)), jnp.float32),
        "query_value_bias": scatter_about(seeds[7], (2, WIDTH), 0.5, 3.0, ((1, 4),), jnp.float32),
        "expand_bias": scatter_about(seeds[8], (HIDDEN_SIZE,), 0.5, 3.0, ((0, 4),), jnp.float32),
        "position_table": scatter_about(seeds[9], (TABLE, HEADS), 1.0, 4.0, ((1, 4),), jnp.float32),
        "norm_params": draw_norm_params(jax.random.fold_in(seeds[27], 71), 0),
        "query_key_value_moment": scatter_about(seeds[11], (3, WIDTH, WIDTH), (0.055 * TOKENS ** 0.5), 80.0, ((1, 8), (2, 4)), jnp.float32),
        "query_key_value_square": jnp.clip(jnp.exp(math.log(100.352) - 2.7725887 * jax.random.uniform(seeds[12], (3, WIDTH, WIDTH), jnp.float32) ** level_of(seeds[12], (3, WIDTH, WIDTH), ((1, 8), (2, 4)), -0.2, 0.2)), 6.272, 100.352),
        "output_weight_moment": scatter_about(seeds[13], (WIDTH, WIDTH), (0.055 * TOKENS ** 0.5), 80.0, ((0, 4), (1, 8)), jnp.float32),
        "output_weight_square": jnp.clip(jnp.exp(math.log(100.352) - 2.7725887 * jax.random.uniform(seeds[14], (WIDTH, WIDTH), jnp.float32) ** level_of(seeds[14], (WIDTH, WIDTH), ((0, 4), (1, 8)), -0.2, 0.2)), 6.272, 100.352),
        "expand_weight_moment": scatter_about(seeds[15], (WIDTH, HIDDEN_SIZE), (0.055 * TOKENS ** 0.5), 80.0, ((0, 8), (1, 4)), jnp.float32),
        "expand_weight_square": jnp.clip(jnp.exp(math.log(100.352) - 2.7725887 * jax.random.uniform(seeds[16], (WIDTH, HIDDEN_SIZE), jnp.float32) ** level_of(seeds[16], (WIDTH, HIDDEN_SIZE), ((0, 8), (1, 4)), -0.2, 0.2)), 6.272, 100.352),
        "contract_weight_moment": scatter_about(seeds[17], (HIDDEN_SIZE, WIDTH), (0.055 * TOKENS ** 0.5), 80.0, ((0, 4), (1, 8)), jnp.float32),
        "contract_weight_square": jnp.clip(jnp.exp(math.log(100.352) - 2.7725887 * jax.random.uniform(seeds[18], (HIDDEN_SIZE, WIDTH), jnp.float32) ** level_of(seeds[18], (HIDDEN_SIZE, WIDTH), ((0, 4), (1, 8)), -0.2, 0.2)), 6.272, 100.352),
        "query_value_bias_moment": scatter_about(seeds[19], (2, WIDTH), (0.055 * TOKENS ** 0.5), 80.0, ((1, 4),), jnp.float32),
        "query_value_bias_square": jnp.clip(jnp.exp(math.log(100.352) - 2.7725887 * jax.random.uniform(seeds[20], (2, WIDTH), jnp.float32) ** level_of(seeds[20], (2, WIDTH), ((1, 4),), -0.2, 0.2)), 6.272, 100.352),
        "expand_bias_moment": scatter_about(seeds[21], (HIDDEN_SIZE,), (0.055 * TOKENS ** 0.5), 80.0, ((0, 4),), jnp.float32),
        "expand_bias_square": jnp.clip(jnp.exp(math.log(100.352) - 2.7725887 * jax.random.uniform(seeds[22], (HIDDEN_SIZE,), jnp.float32) ** level_of(seeds[22], (HIDDEN_SIZE,), ((0, 4),), -0.2, 0.2)), 6.272, 100.352),
        "position_table_moment": scatter_about(seeds[23], (TABLE, HEADS), (0.055 * TOKENS ** 0.5), 80.0, ((1, 4),), jnp.float32),
        "position_table_square": jnp.clip(jnp.exp(math.log(100.352) - 2.7725887 * jax.random.uniform(seeds[24], (TABLE, HEADS), jnp.float32) ** level_of(seeds[24], (TABLE, HEADS), ((1, 4),), -0.2, 0.2)), 6.272, 100.352),
        "norm_params_moment": scatter_about(seeds[25], (6, WIDTH), (0.11 * TOKENS ** 0.5), 160.0, (), jnp.float32),
        "norm_params_square": jnp.clip(jnp.exp(jax.random.uniform(seeds[26], (6, WIDTH), jnp.float32, math.log(25.088), math.log(401.408))), 25.088, 401.408),
    }


@jax.custom_vjp
def low(v):
    return lax.optimization_barrier(v.astype(jnp.bfloat16)).astype(jnp.float32)

@jax.custom_vjp
def low_back(v):
    return v

def low_keep(v):
    return (low(v), None)

def low_pass(kept, grad):
    return (grad,)

def back_keep(v):
    return (v, None)

def back_low(kept, grad):
    return (low(grad),)
low.defvjp(low_keep, low_pass)
low_back.defvjp(back_keep, back_low)
NORM_EPS = 1e-05
BETA_ONE = 0.9
BETA_TWO = 0.999
ADAM_EPS = 1e-08
RATE_MATRIX = 0.1
RATE_SMALL = 0.5
DECAY_MATRIX = 0.05
MASKED = -1e+30
HIGHEST = lax.Precision.HIGHEST

def matmul(left, right):
    return jnp.dot(left, right, precision=HIGHEST)

def layer_norm(values, gain_row, offset):
    centred = values - lax.optimization_barrier(jnp.mean(values, axis=-1, keepdims=True))
    inv_std = lax.rsqrt(lax.optimization_barrier(jnp.mean(centred * centred, axis=-1, keepdims=True)) + NORM_EPS)
    return centred * inv_std * gain_row + offset

def to_windows(values):
    canvas_count = values.shape[0] // (SIDE * SIDE)
    per_side = SIDE // WINDOW
    feature_count = values.shape[-1]
    grid = values.reshape(canvas_count, SIDE, SIDE, feature_count)
    grid = jnp.roll(grid, (-SHIFT, -SHIFT), axis=(1, 2))
    grid = grid.reshape(canvas_count, per_side, WINDOW, per_side, WINDOW, feature_count)
    grid = grid.transpose(0, 1, 3, 2, 4, 5)
    return grid.reshape(canvas_count * per_side * per_side, WINDOW * WINDOW, feature_count)

def from_windows(values):
    per_side = SIDE // WINDOW
    canvas_count = values.shape[0] // (per_side * per_side)
    feature_count = values.shape[-1]
    grid = values.reshape(canvas_count, per_side, per_side, WINDOW, WINDOW, feature_count)
    grid = grid.transpose(0, 1, 3, 2, 4, 5).reshape(canvas_count, SIDE, SIDE, feature_count)
    grid = jnp.roll(grid, (SHIFT, SHIFT), axis=(1, 2))
    return grid.reshape(canvas_count * SIDE * SIDE, feature_count)

def region_mask():
    coords = jnp.arange(SIDE)
    band_ids = jnp.where(coords < SIDE - WINDOW, 0, jnp.where(coords < SIDE - SHIFT, 1, 2))
    region = band_ids[:, None] * 3 + band_ids[None, :]
    per_side = SIDE // WINDOW
    region = region.reshape(per_side, WINDOW, per_side, WINDOW).transpose(0, 2, 1, 3)
    region = region.reshape(per_side * per_side, WINDOW * WINDOW)
    return region[:, :, None] == region[:, None, :]

def relative_index():
    places = jnp.arange(WINDOW * WINDOW)
    row_place = places // WINDOW
    col_place = places % WINDOW
    row_diff = row_place[:, None] - row_place[None, :] + WINDOW - 1
    col_diff = col_place[:, None] - col_place[None, :] + WINDOW - 1
    return (row_diff * (2 * WINDOW - 1) + col_diff).astype(jnp.int32)

def attend(queries, key_rows, value_rows, crop_rows, table_w):
    windows_q = to_windows(queries)
    window_count = windows_q.shape[0]
    window_shape = (window_count, WINDOW * WINDOW, HEADS, HEAD_DIM)
    query_w = windows_q.reshape(window_shape)
    key_w = to_windows(key_rows).reshape(window_shape)
    value_w = to_windows(value_rows).reshape(window_shape)
    bias_heads = jnp.transpose(table_w[relative_index()], (2, 0, 1))
    raw_scores = jnp.einsum('wqhd,wkhd->whqk', query_w, key_w, precision=HIGHEST)
    scores = low_back(raw_scores * HEAD_DIM ** (-0.5) + bias_heads[None])
    crop_windows = to_windows(crop_rows[:, None])[:, :, 0]
    same_crop = crop_windows[:, :, None] == crop_windows[:, None, :]
    per_canvas = SIDE // WINDOW * (SIDE // WINDOW)
    allowed = same_crop & jnp.tile(region_mask(), (window_count // per_canvas, 1, 1))
    probabilities = low(jax.nn.softmax(jnp.where(allowed[:, None], scores, MASKED), axis=-1))
    mixed_rows = jnp.einsum('whqk,wkhd->wqhd', probabilities, value_w, precision=HIGHEST)
    return from_windows(mixed_rows.reshape(window_count, WINDOW * WINDOW, WIDTH))

def block_forward(params, tokens_block, crops_block):
    attn_in, attn_out, expand_w, contract_w, qv_bias, expand_b, table_w, norm_set = params
    normed_one = low(layer_norm(tokens_block, norm_set[0], norm_set[1]))
    queries = low(low_back(matmul(normed_one, attn_in[0]) + qv_bias[0]))
    key_rows = low(low_back(matmul(normed_one, attn_in[1])))
    value_rows = low(low_back(matmul(normed_one, attn_in[2]) + qv_bias[1]))
    merged = low(low_back(attend(queries, key_rows, value_rows, crops_block, table_w)))
    middle = tokens_block + low_back(matmul(merged, attn_out)) + norm_set[4]
    normed_two = low(layer_norm(middle, norm_set[2], norm_set[3]))
    pre_act = low_back(matmul(normed_two, expand_w) + expand_b)
    hidden = low(jax.nn.gelu(pre_act, approximate=False))
    return middle + matmul(hidden, contract_w) + norm_set[5]

def adamw_step(master, grad_value, moment, square, step_rate, decay_rate):
    moment_new = BETA_ONE * moment + (1.0 - BETA_ONE) * grad_value
    square_new = BETA_TWO * square + (1.0 - BETA_TWO) * grad_value * grad_value
    moment_hat = moment_new / (1.0 - BETA_ONE ** STEP)
    square_hat = square_new / (1.0 - BETA_TWO ** STEP)
    updated = master - step_rate * (moment_hat / (jnp.sqrt(square_hat) + ADAM_EPS) + decay_rate * master)
    return (updated, moment_new, square_new)

def reference(tokens, crop_ids, grad_out, query_key_value, output_weight, expand_weight, contract_weight, query_value_bias, expand_bias, position_table, norm_params, query_key_value_moment, query_key_value_square, output_weight_moment, output_weight_square, expand_weight_moment, expand_weight_square, contract_weight_moment, contract_weight_square, query_value_bias_moment, query_value_bias_square, expand_bias_moment, expand_bias_square, position_table_moment, position_table_square, norm_params_moment, norm_params_square):
    masters = (query_key_value, output_weight, expand_weight, contract_weight, query_value_bias, expand_bias, position_table, norm_params)
    per_block = math.gcd(CANVASES, 16)
    block_rows = per_block * SIDE * SIDE
    block_count = CANVASES // per_block
    token_blocks = tokens.astype(jnp.float32).reshape(block_count, block_rows, WIDTH)
    crop_blocks = crop_ids.reshape(block_count, block_rows)

    def forward(params, inputs):
        rounded = tuple((low(member) for member in params[:7])) + (params[7],)

        def one_block(pair_in):
            return block_forward(rounded, pair_in[0], pair_in[1])
        return lax.map(jax.checkpoint(one_block), (inputs, crop_blocks))
    outputs, pullback = jax.vjp(forward, masters, token_blocks)
    grad_list, grad_blocks = pullback(grad_out.astype(jnp.float32).reshape(outputs.shape))
    moments = (query_key_value_moment, output_weight_moment, expand_weight_moment, contract_weight_moment, query_value_bias_moment, expand_bias_moment, position_table_moment, norm_params_moment)
    squares = (query_key_value_square, output_weight_square, expand_weight_square, contract_weight_square, query_value_bias_square, expand_bias_square, position_table_square, norm_params_square)
    rates = (RATE_MATRIX,) * 4 + (RATE_SMALL,) * 4
    decays = (DECAY_MATRIX,) * 4 + (0.0,) * 4
    news = [adamw_step(masters[index_p], grad_list[index_p], moments[index_p], squares[index_p], rates[index_p], decays[index_p]) for index_p in range(8)]
    block_out = outputs.reshape(TOKENS, WIDTH).astype(jnp.bfloat16)
    grad_tokens = grad_blocks.reshape(TOKENS, WIDTH)
    return (block_out, grad_tokens, news[0][0], news[0][1], news[0][2], news[1][0], news[1][1], news[1][2], news[2][0], news[2][1], news[2][2], news[3][0], news[3][1], news[3][2], news[4][0], news[4][1], news[4][2], news[5][0], news[5][1], news[5][2], news[6][0], news[6][1], news[6][2], news[7][0], news[7][1], news[7][2])
```

```python
import functools
import math

import jax
import jax.numpy as jnp
import numpy as np
from jax import lax
from jax.experimental import pallas as pl
from jax.experimental.pallas import tpu as pltpu
from jax.sharding import PartitionSpec as P

HEAD_DIM = 32
WINDOW = 7
SIDE = 14
SHIFT = 3
STEP = 10
CANVAS = SIDE * SIDE
PLACES = WINDOW * WINDOW
SLOT = 64
QUAD_ROWS = 4 * CANVAS
SPAN = 208
WIDTH = 384
GROUPS = 3
PACK = 4
HIDDEN = 1536
CHUNK = 512

NORM_EPS = 1e-05
BETA_ONE = 0.9
BETA_TWO = 0.999
ADAM_EPS = 1e-08
RATE_MATRIX = 0.1
RATE_SMALL = 0.5
DECAY_MATRIX = 0.05
MASKED = -1e30
LOG2E = math.log2(math.e)
SCALE = HEAD_DIM**-0.5
ROOT_HALF = 0.7071067811865476
INV_ROOT_TWO_PI = 1.0 / 2.5066282746310002
BF = jnp.bfloat16
F32 = jnp.float32


def slot_rows():
    rows = -np.ones((4, SLOT), np.int64)
    for win in range(4):
        for place in range(PLACES):
            row = (win // 2) * WINDOW + place // WINDOW
            col = (win % 2) * WINDOW + place % WINDOW
            rows[win, place] = ((row + SHIFT) % SIDE) * SIDE + (col + SHIFT) % SIDE
    return rows.reshape(-1)


def permutations():
    rows = slot_rows()
    to_slots = np.zeros((4, 4 * SLOT, SPAN), np.float32)
    for i in range(4):
        for slot, row in enumerate(rows):
            if row >= 0:
                to_slots[i, slot, 4 * i + row] = 1.0
    return to_slots, to_slots.transpose(0, 2, 1).copy()


def region_codes():
    def band(v):
        return 0 if v < SIDE - WINDOW else (1 if v < SIDE - SHIFT else 2)

    codes = np.full((4, SLOT), 999.0, np.float32)
    for win in range(4):
        for place in range(PLACES):
            row = (win // 2) * WINDOW + place // WINDOW
            col = (win % 2) * WINDOW + place % WINDOW
            codes[win, place] = 4 * (3 * band(row) + band(col))
    return codes.reshape(-1)


def pair_onehot(rows):
    out = np.zeros((rows, SLOT, SLOT), np.float32)
    for key in range(PLACES):
        for query in range(PLACES):
            up = query // WINDOW - key // WINDOW + WINDOW - 1
            side = query % WINDOW - key % WINDOW + WINDOW - 1
            out[up * (2 * WINDOW - 1) + side, key, query] = 1.0
    return out


def dot_nn(a, b):
    return jnp.dot(a, b, preferred_element_type=F32)


def dot_nt(a, b):
    return lax.dot_general(a, b, (((1,), (1,)), ((), ())), preferred_element_type=F32)


def stats(values):
    centred = values - jnp.mean(values, axis=-1, keepdims=True)
    inv_std = lax.rsqrt(jnp.mean(centred * centred, axis=-1, keepdims=True) + NORM_EPS)
    return centred * inv_std, inv_std


def norm_back(grad_norm, hat, inv_std, gain_row):
    grad_hat = grad_norm * gain_row
    inner = grad_hat - jnp.mean(grad_hat, axis=-1, keepdims=True)
    return inv_std * (inner - hat * jnp.mean(grad_hat * hat, axis=-1, keepdims=True))


def owners(idx):
    z, y, x, c = idx[0], idx[1], idx[2], idx[3]
    for e in range(2):
        for k in range(4):
            for s in range(4):
                row = ((z ^ s) * 2 + (y ^ (k >> 1))) * 48
                yield e, k, s, pl.multiple_of(row, 16), (x ^ (k & 1)) * 2 + (c ^ e)


def spread(block):
    four = jnp.concatenate([block] * PACK, axis=1)
    rows = lax.broadcasted_iota(jnp.int32, four.shape, 0) // HEAD_DIM
    lanes = lax.broadcasted_iota(jnp.int32, four.shape, 1) // SLOT
    return jnp.where(rows == lanes, four, jnp.zeros_like(four))


def attention_forward(
    idx, p0, p1, p2, p3, p4, p5, p6, p7, tok, quad, ut, u, reg_row, reg_col, bias, tb, par,
    mrg, qt, kt, vv, pt, mt, n1t, wnat, outt, wout,
    wbuf, waug, wt, n1aug, vt,
):
    step = pl.program_id(0)

    @pl.when(step == 0)
    def _():
        refs = (p0, p1, p2, p3, p4, p5, p6, p7)
        for e, k, s, row, head in owners(idx):
            wbuf[head, pl.ds(row, 48), :] = refs[e * 4 + k][s * 48 : (s + 1) * 48, :]
        for j in range(3):
            waug[0:WIDTH, j * WIDTH : (j + 1) * WIDTH] = jnp.concatenate(
                [wbuf[h, :, 96 * j : 96 * (j + 1)] for h in range(4)], axis=1
            )
        out_t = jnp.concatenate([wbuf[h, :, 288:384] for h in range(4)], axis=1)
        outt[...] = out_t
        wout[...] = out_t.T
        waug[WIDTH : WIDTH + 16, :] = bias[...]
        waug[WIDTH + 16 : 512, :] = jnp.zeros((112, 3 * WIDTH), BF)
        wnat[...] = waug[0:WIDTH, :]
        wt[...] = waug[...].T
        lane = lax.broadcasted_iota(jnp.int32, (4 * SLOT, 128), 1)
        n1aug[:, WIDTH:512] = jnp.where(lane == 0, 1.0, 0.0).astype(BF)

    start = pl.multiple_of((step // 4) * QUAD_ROWS + (step % 4) * 192, 16)
    hat, _ = stats(tok[pl.ds(start, SPAN), :].astype(F32))
    n1 = (hat * par[0:1, :] + par[1:2, :]).astype(BF)
    n1aug[:, 0:WIDTH] = dot_nn(ut[0], n1).astype(BF)
    na = n1aug[...]
    n1t[0] = na.T[0:400, :]
    all_t = dot_nt(wt[...], na).astype(BF)
    qt[0] = all_t[0:WIDTH]
    kt[0] = all_t[WIDTH : 2 * WIDTH]
    vt[...] = all_t[2 * WIDTH :]
    kv = dot_nt(na, wt[WIDTH:, :]).astype(BF)
    vv[0] = kv[:, WIDTH:]
    code_row = dot_nt(quad[0], ut[0]) + reg_row[...]
    code_col = dot_nt(ut[0], quad[0]) + reg_col[...]
    for win in range(4):
        lo, hi = win * SLOT, (win + 1) * SLOT
        same = code_col[lo:hi, 0:1] == jnp.concatenate([code_row[0:1, lo:hi]] * PACK, axis=1)
        mask = jnp.where(same, 0.0, MASKED)
        for g in range(GROUPS):
            fa, fb = g * 128, (g + 1) * 128
            scores = dot_nn(kv[lo:hi, fa:fb], spread(qt[0, fa:fb, lo:hi]))
            scores = scores * (SCALE * LOG2E) + (tb[g] + mask)
            top = jnp.max(scores, axis=0, keepdims=True)
            grown = jnp.exp2(scores - top)
            probs = (grown * (1.0 / jnp.sum(grown, axis=0, keepdims=True))).astype(BF)
            pt[0, win * GROUPS + g] = probs
            mixed = dot_nn(vt[fa:fb, lo:hi], probs)
            for h in range(PACK):
                r = fa + h * HEAD_DIM
                mt[0, r : r + HEAD_DIM, lo:hi] = mixed[
                    h * HEAD_DIM : (h + 1) * HEAD_DIM, h * SLOT : (h + 1) * SLOT
                ].astype(BF)
    back = dot_nt(u[0], mt[0]).astype(BF)

    @pl.when(step % 4 == 0)
    def _():
        mrg[pl.ds(start, 16), :] = back[0:16]

    @pl.when(step % 4 != 0)
    def _():
        mrg[pl.ds(start, 16), :] = mrg[pl.ds(start, 16), :] + back[0:16]

    mrg[pl.ds(pl.multiple_of(start + 16, 16), SPAN - 16), :] = back[16:]


def mlp(
    idx, p0, p1, p2, p3, p4, p5, p6, p7, tok, gout, mrg, outt, eb, par,
    blk, gmid, keep, send, sums, ebg,
    eaug, ct, n2, mid, n2t, got, hid, gpr, acc_m, acc_g, cg, eg,
):
    step = pl.program_id(0)
    last = pl.num_programs(0) - 1
    rows_all = tok.shape[0]
    tile = 224
    tiles = rows_all // tile

    @pl.when(step == 0)
    def _():
        refs = (p0, p1, p2, p3, p4, p5, p6, p7)
        for e, k, s, row, head in owners(idx):
            lanes = pl.ds(pl.multiple_of(head * WIDTH, 128), WIDTH)
            eaug[pl.ds(row, 48), lanes] = refs[e * 4 + k][s * 48 : (s + 1) * 48, 0:WIDTH]
            ct[pl.ds(row, 48), lanes] = refs[e * 4 + k][s * 48 : (s + 1) * 48, WIDTH:]
        eaug[WIDTH : WIDTH + 16, :] = eb[...]
        eaug[WIDTH + 16 : 512, :] = jnp.zeros((112, HIDDEN), BF)
        lane = lax.broadcasted_iota(jnp.int32, (tile, 128), 1)
        ones = jnp.where(lane == 0, 1.0, 0.0).astype(BF)

        def head_rows(t, carry):
            rows = pl.ds(pl.multiple_of(t * tile, 16), tile)
            attn = dot_nt(mrg[rows, :], outt[...])
            middle = tok[rows, :].astype(F32) + attn + par[4:5, :]
            mid[rows, :] = middle
            hat, _ = stats(middle)
            n2[rows, 0:WIDTH] = (hat * par[2:3, :] + par[3:4, :]).astype(BF)
            n2[rows, WIDTH:512] = ones
            acc_m[rows, :] = jnp.zeros((tile, WIDTH), F32)
            acc_g[rows, :] = jnp.zeros((tile, WIDTH), F32)
            return carry

        lax.fori_loop(0, tiles, head_rows, 0)
        n2t[...] = n2[...].T[0:400, :]
        got[...] = gout[...].T

    cols = pl.ds(pl.multiple_of(step * CHUNK, 128), CHUNK)

    def unit_rows(t, carry):
        rows = pl.ds(pl.multiple_of(t * tile, 16), tile)
        pre = dot_nn(n2[rows, :], eaug[:, cols])
        grad_hidden = dot_nn(gout[rows, :], ct[:, cols])
        phi = 0.5 + 0.5 * lax.erf(pre * ROOT_HALF)
        bell = jnp.exp2(pre * pre * (-0.5 * LOG2E)) * INV_ROOT_TWO_PI
        hidden = (pre * phi).astype(BF)
        grad_pre = (grad_hidden * (phi + pre * bell)).astype(BF)
        hid[rows, :] = hidden
        gpr[rows, :] = grad_pre
        acc_m[rows, :] += dot_nt(hidden, ct[:, cols])
        acc_g[rows, :] += dot_nt(grad_pre, eaug[0:WIDTH, cols])
        return carry

    lax.fori_loop(0, tiles, unit_rows, 0)
    cg[:, cols] = dot_nn(got[...], hid[...]).astype(BF)
    grads = dot_nn(n2t[...], gpr[...])
    eg[:, cols] = grads[0:WIDTH].astype(BF)
    ebg[:, cols] = grads[WIDTH : WIDTH + 8]

    @pl.when(step == last)
    def _():
        for e, k, s, row, head in owners(idx):
            dst = (keep, send)[e]
            lanes = pl.ds(pl.multiple_of(head * WIDTH, 128), WIDTH)
            base = (k * 4 + s) * 48
            dst[base : base + 48, 0:WIDTH] = eg[pl.ds(row, 48), lanes]
            dst[base : base + 48, WIDTH:] = cg[pl.ds(row, 48), lanes]

        def tail_rows(t, carry):
            rows = pl.ds(pl.multiple_of(t * tile, 16), tile)
            middle = mid[rows, :]
            blk[rows, :] = (middle + acc_m[rows, :] + par[5:6, :]).astype(BF)
            hat, inv = stats(middle)
            g = acc_g[rows, :]
            top = gout[rows, :].astype(F32)
            grad_mid = top + norm_back(g, hat, inv, par[2:3, :])
            gmid[rows, :] = grad_mid
            parts = (g * hat, g, grad_mid, top)
            return tuple(c + jnp.sum(p, axis=0, keepdims=True) for c, p in zip(carry, parts))

        zero = jnp.zeros((1, WIDTH), F32)
        totals = lax.fori_loop(0, tiles, tail_rows, (zero,) * 4)
        sums[...] = jnp.concatenate([zero, zero, *totals, zero, zero], axis=0)


def attention_backward(
    idx, tok, gmid, qt, kt, vv, pt, mt, n1t, wnat, wout, ut, u, par, sums_in,
    gtok, keep, send, table,
    gtall, ntall, wacc, oacc, csum, gt,
):
    step = pl.program_id(0)
    last = pl.num_programs(0) - 1

    @pl.when(step == 0)
    def _():
        table[...] = jnp.zeros(table.shape, F32)
        oacc[...] = jnp.zeros(oacc.shape, F32)
        wacc[...] = jnp.zeros(wacc.shape, F32)
        csum[...] = sums_in[...]

    start = pl.multiple_of((step // 4) * QUAD_ROWS + (step % 4) * 192, 16)
    rows = pl.ds(start, SPAN)
    grad_mid = gmid[rows, :]
    gmw = dot_nn(ut[0], grad_mid.astype(BF)).astype(BF)
    gmt = dot_nt(wout[...], gmw).astype(BF)
    oacc[...] += dot_nn(mt[0], gmw)
    for win in range(4):
        lo, hi = win * SLOT, (win + 1) * SLOT
        for g in range(GROUPS):
            fa, fb = g * 128, (g + 1) * 128
            gm_s = spread(gmt[fa:fb, lo:hi])
            q_s = spread(qt[0, fa:fb, lo:hi])
            probs_b = pt[0, win * GROUPS + g]
            probs = probs_b.astype(F32)
            gp = dot_nn(vv[0, lo:hi, fa:fb], gm_s)
            delta = jnp.sum(probs * gp, axis=0, keepdims=True)
            gs = (probs * (gp - delta)).astype(BF)
            table[g] += gs.astype(F32)
            gq = dot_nn(kt[0, fa:fb, lo:hi], gs) * SCALE
            for h in range(PACK):
                r = fa + h * HEAD_DIM
                gt[r : r + HEAD_DIM, lo:hi] = gq[
                    h * HEAD_DIM : (h + 1) * HEAD_DIM, h * SLOT : (h + 1) * SLOT
                ].astype(BF)
            gt[WIDTH + fa : WIDTH + fb, lo:hi] = (dot_nt(q_s, gs) * SCALE).astype(BF)
            gt[2 * WIDTH + fa : 2 * WIDTH + fb, lo:hi] = dot_nt(gm_s, probs_b).astype(BF)
    gta = gt[...]
    wacc[...] += dot_nt(n1t[0], gta)
    g1t = dot_nn(wnat[...], gta)
    high = g1t.astype(BF)
    low = (g1t - high.astype(F32)).astype(BF)
    g1 = dot_nt(u[0], high) + dot_nt(u[0], low)
    hat, inv = stats(tok[rows, :].astype(F32))
    csum[0:1, :] += jnp.sum(g1 * hat, axis=0, keepdims=True)
    csum[1:2, :] += jnp.sum(g1, axis=0, keepdims=True)
    part = norm_back(g1, hat, inv, par[0:1, :])

    @pl.when(step % 4 == 0)
    def _():
        gtok[pl.ds(start, 16), :] = grad_mid[0:16] + part[0:16]

    @pl.when(step % 4 != 0)
    def _():
        gtok[pl.ds(start, 16), :] += part[0:16]

    gtok[pl.ds(pl.multiple_of(start + 16, 16), SPAN - 16), :] = grad_mid[16:] + part[16:]

    @pl.when(step == last)
    def _():
        out_t = oacc[...].T
        for h in range(4):
            pieces = [wacc[0:WIDTH, j * WIDTH + 96 * h : j * WIDTH + 96 * (h + 1)] for j in range(3)]
            pieces.append(out_t[:, 96 * h : 96 * (h + 1)])
            ntall[h] = jnp.concatenate(pieces, axis=1).astype(BF)
        for e, k, s, row, head in owners(idx):
            dst = (keep, send)[e]
            base = (k * 4 + s) * 48
            dst[base : base + 48, :] = ntall[head, pl.ds(row, 48), :]
        bias_rows = [wacc[WIDTH : WIDTH + 1, j * WIDTH : (j + 1) * WIDTH] for j in (0, 2)]
        small = jnp.concatenate([csum[0:6, :], *bias_rows], axis=0)
        small = jnp.concatenate([small, jnp.zeros((8, WIDTH), F32)], axis=0).astype(BF)
        keep[768:784, :] = small
        send[768:784, :] = small


def adamw_step(master, grad_value, moment, square, step_rate, decay_rate):
    moment_new = BETA_ONE * moment + (1.0 - BETA_ONE) * grad_value
    square_new = BETA_TWO * square + (1.0 - BETA_TWO) * grad_value * grad_value
    moment_hat = moment_new / (1.0 - BETA_ONE**STEP)
    square_hat = square_new / (1.0 - BETA_TWO**STEP)
    updated = master - step_rate * (
        moment_hat / (jnp.sqrt(square_hat) + ADAM_EPS) + decay_rate * master
    )
    return (updated, moment_new, square_new)


class Links:
    def __init__(self, sizes):
        self.sizes = sizes
        self.outer = sizes["dp"] // 8

    def perm(self, z=0, y=0, x=0, c=0):
        pairs = []
        for flat in range(self.sizes["dp"] * self.sizes["head"]):
            head, dp = flat % 4, flat // 4
            inner, place = dp // self.outer, dp % self.outer
            inner ^= z * 2 + y
            pairs.append((flat, (inner * self.outer + place) * 4 + (head ^ (x * 2 + c))))
        return pairs

    def send(self, value, **flips):
        return lax.ppermute(value, ("dp", "head"), self.perm(**flips))

    def groups(self):
        return [[i * self.outer + j for j in range(self.outer)] for i in range(8)]

    def gather(self, shard):
        if self.outer > 1:
            shard = lax.all_gather(
                shard, "dp", axis=0, tiled=True, axis_index_groups=self.groups()
            )
        line = jnp.concatenate([shard] + [self.send(shard, z=s) for s in range(1, 4)], axis=0)
        plane = [line] + [self.send(line, x=k & 1, y=k >> 1) for k in range(1, 4)]
        return plane + [self.send(part, c=1) for part in plane]

    def outer_sum(self, value):
        if self.outer > 1:
            value = lax.psum_scatter(
                value, "dp", scatter_dimension=0, tiled=True, axis_index_groups=self.groups()
            )
        return value


def whole(shape):
    zeros = (0,) * len(shape)
    return pl.BlockSpec(shape, lambda i: zeros)


def slab(shape):
    zeros = (0,) * (len(shape) - 1)
    return pl.BlockSpec((1, *shape[1:]), lambda i: (i, *zeros))


def turn(shape):
    zeros = (0,) * (len(shape) - 1)
    return pl.BlockSpec((1, *shape[1:]), lambda i: (i % 4, *zeros))


SMEM = pl.BlockSpec(memory_space=pltpu.SMEM)


def per_device(links, *args):
    (
        tokens, crop_ids, grad_out, qkv_w, out_w, exp_w, con_w, qv_b, exp_b, table_w, norm_p,
        qkv_m, qkv_s, out_m, out_s, exp_m, exp_s, con_m, con_s,
        qv_m, qv_s, eb_m, eb_s, tab_m, tab_s, norm_m, norm_s,
    ) = args
    rows_all = tokens.shape[0]
    canvases = rows_all // CANVAS
    head = lax.axis_index("head")
    dp = lax.axis_index("dp") // links.outer
    idx = jnp.stack([dp // 2, dp % 2, head // 2, head % 2]).astype(jnp.int32)

    first = jnp.concatenate([qkv_w[0], qkv_w[1], qkv_w[2], out_w.T], axis=1).astype(BF)
    second = jnp.concatenate([exp_w, con_w.T], axis=1).astype(BF)
    firsts = links.gather(first)
    seconds = links.gather(second)
    own = jnp.concatenate([qv_b.reshape(-1), exp_b, table_w.T.reshape(-1)]).astype(BF)
    own = own.reshape(1, -1)
    pair = jnp.where(idx[3] == 0, 1, 0)
    other = links.send(own, c=1)
    both = jnp.where(pair == 1, jnp.concatenate([own, other]), jnp.concatenate([other, own]))
    other = links.send(both, x=1)
    four = jnp.where(
        idx[2] == 0, jnp.concatenate([both, other]), jnp.concatenate([other, both])
    )
    bias_qv = four[:, 0:192].reshape(4, 2, 96).transpose(1, 0, 2).reshape(2, WIDTH)
    bias_row = jnp.concatenate([bias_qv[0], jnp.zeros((WIDTH,), BF), bias_qv[1]])
    bias16 = jnp.pad(bias_row[None], ((0, 15), (0, 0)))
    eb16 = jnp.pad(four[:, 192:576].reshape(1, HIDDEN), ((0, 15), (0, 0)))
    table_rows = table_w.shape[0]
    table_t = four[:, 576:].reshape(12, table_rows)
    pairs = jnp.asarray(pair_onehot(table_rows), BF)
    bias_t = jnp.einsum("ht,tkq->hkq", table_t, pairs, preferred_element_type=F32) * LOG2E
    bias_t = bias_t.reshape(GROUPS, PACK, SLOT, SLOT).transpose(0, 2, 1, 3)
    bias_t = bias_t.reshape(GROUPS, SLOT, PACK * SLOT)

    crop_rows = lax.dynamic_slice_in_dim(crop_ids, head * rows_all, rows_all, 0)
    quads = (crop_rows & 3).astype(BF)
    quads = jnp.stack(
        [quads[(c // 4) * QUAD_ROWS + 192 * (c % 4) :][:SPAN] for c in range(canvases)]
    )
    quads = jnp.broadcast_to(quads[:, None, :], (canvases, 8, SPAN))
    to_slots, from_slots = permutations()
    to_slots, from_slots = jnp.asarray(to_slots, BF), jnp.asarray(from_slots, BF)
    codes = region_codes()
    reg_row = jnp.asarray(np.broadcast_to(codes[None, :], (8, 4 * SLOT)).copy())
    reg_col = jnp.asarray(np.broadcast_to(codes[:, None], (4 * SLOT, 8)).copy())
    par = jnp.pad(norm_p, ((0, 2), (0, 0)))

    slots = 4 * SLOT
    fm = (canvases, WIDTH, slots)
    tm = (canvases, slots, WIDTH)
    big = (canvases, 12, SLOT, slots)
    nt = (canvases, 400, slots)
    shapes = [
        ((rows_all, WIDTH), BF), (fm, BF), (fm, BF), (tm, BF), (big, BF), (fm, BF), (nt, BF),
        ((WIDTH, 3 * WIDTH), BF), ((WIDTH, WIDTH), BF), ((WIDTH, WIDTH), BF),
    ]
    merged, qt, kt, vv, pt, mt, n1t, wnat, outt, wout = pl.pallas_call(
        attention_forward,
        grid=(canvases,),
        in_specs=[SMEM]
        + [whole((192, WIDTH))] * 8
        + [
            whole((rows_all, WIDTH)), slab(quads.shape), turn(to_slots.shape),
            turn(from_slots.shape), whole(reg_row.shape), whole(reg_col.shape),
            whole(bias16.shape), whole(bias_t.shape), whole(par.shape),
        ],
        out_specs=[whole(shapes[0][0])]
        + [slab(s) for s, _ in shapes[1:7]]
        + [whole(s) for s, _ in shapes[7:]],
        out_shape=[jax.ShapeDtypeStruct(s, d) for s, d in shapes],
        scratch_shapes=[
            pltpu.VMEM((4, WIDTH, WIDTH), BF), pltpu.VMEM((512, 3 * WIDTH), BF),
            pltpu.VMEM((3 * WIDTH, 512), BF), pltpu.VMEM((slots, 512), BF),
            pltpu.VMEM((WIDTH, slots), BF),
        ],
        compiler_params=pltpu.CompilerParams(vmem_limit_bytes=50 * 2**20),
        name="attention_forward",
    )(idx, *firsts, tokens, quads, to_slots, from_slots, reg_row, reg_col, bias16, bias_t, par)

    wide = (rows_all, WIDTH)
    block_out, grad_mid, keep_r, send_r, sums, eb_grad = pl.pallas_call(
        mlp,
        grid=(HIDDEN // CHUNK,),
        in_specs=[SMEM]
        + [whole((192, 2 * WIDTH))] * 8
        + [
            whole(wide), whole(wide), whole(wide), whole((WIDTH, WIDTH)), whole(eb16.shape),
            whole(par.shape),
        ],
        out_specs=[
            whole(wide), whole(wide), whole((768, 2 * WIDTH)), whole((768, 2 * WIDTH)),
            whole((8, WIDTH)), whole((8, HIDDEN)),
        ],
        out_shape=[
            jax.ShapeDtypeStruct(wide, BF), jax.ShapeDtypeStruct(wide, F32),
            jax.ShapeDtypeStruct((768, 2 * WIDTH), BF), jax.ShapeDtypeStruct((768, 2 * WIDTH), BF),
            jax.ShapeDtypeStruct((8, WIDTH), F32), jax.ShapeDtypeStruct((8, HIDDEN), F32),
        ],
        scratch_shapes=[
            pltpu.VMEM((512, HIDDEN), BF), pltpu.VMEM((WIDTH, HIDDEN), BF),
            pltpu.VMEM((rows_all, 512), BF), pltpu.VMEM(wide, F32),
            pltpu.VMEM((400, rows_all), BF), pltpu.VMEM((WIDTH, rows_all), BF),
            pltpu.VMEM((rows_all, CHUNK), BF), pltpu.VMEM((rows_all, CHUNK), BF),
            pltpu.VMEM(wide, F32), pltpu.VMEM(wide, F32),
            pltpu.VMEM((WIDTH, HIDDEN), BF), pltpu.VMEM((WIDTH, HIDDEN), BF),
        ],
        compiler_params=pltpu.CompilerParams(vmem_limit_bytes=58 * 2**20),
        name="mlp",
    )(idx, *seconds, tokens, grad_out, merged, outt, eb16, par)

    grad_tokens, keep_q, send_q, table_sum = pl.pallas_call(
        attention_backward,
        grid=(canvases,),
        in_specs=[SMEM]
        + [
            whole(wide), whole(wide), slab(fm), slab(fm), slab(tm), slab(big), slab(fm), slab(nt),
            whole((WIDTH, 3 * WIDTH)), whole((WIDTH, WIDTH)), turn(to_slots.shape),
            turn(from_slots.shape), whole(par.shape), whole((8, WIDTH)),
        ],
        out_specs=[
            whole(wide), whole((784, WIDTH)), whole((784, WIDTH)), whole((GROUPS, SLOT, slots)),
        ],
        out_shape=[
            jax.ShapeDtypeStruct(wide, F32), jax.ShapeDtypeStruct((784, WIDTH), BF),
            jax.ShapeDtypeStruct((784, WIDTH), BF),
            jax.ShapeDtypeStruct((GROUPS, SLOT, slots), F32),
        ],
        scratch_shapes=[
            pltpu.VMEM((8, 128), BF), pltpu.VMEM((4, WIDTH, WIDTH), BF),
            pltpu.VMEM((400, 3 * WIDTH), F32), pltpu.VMEM((WIDTH, WIDTH), F32),
            pltpu.VMEM((8, WIDTH), F32), pltpu.VMEM((3 * WIDTH, slots), BF),
        ],
        compiler_params=pltpu.CompilerParams(vmem_limit_bytes=50 * 2**20),
        name="attention_backward",
    )(
        idx, tokens, grad_mid, qt, kt, vv, pt, mt, n1t, wnat, wout, to_slots, from_slots, par, sums
    )

    table_part = table_sum.reshape(GROUPS, SLOT, PACK, SLOT).transpose(0, 2, 1, 3)
    table_part = table_part.reshape(12, SLOT * SLOT)
    table_grad = jnp.dot(
        table_part, pairs.reshape(table_rows, -1).astype(F32).T, precision=lax.Precision.HIGHEST
    )
    extra = jnp.concatenate([eb_grad[0], table_grad.reshape(-1)])
    extra_rows = -(-extra.shape[0] // (16 * WIDTH)) * 16
    extra = jnp.pad(extra, (0, extra_rows * WIDTH - extra.shape[0])).reshape(extra_rows, WIDTH)

    def reduced(keep, send, small, small_sent):
        columns = keep.shape[1]
        total = keep.astype(F32) + links.send(send, c=1).astype(F32)
        if small is not None:
            small = small.astype(F32) + links.send(small_sent, c=1).astype(F32)
        total = total.reshape(4, 192, columns)
        got = []
        for k in range(1, 4):
            out = total[k].astype(BF)
            if small is not None:
                out = jnp.concatenate([out, small.astype(BF)], axis=0)
            got.append(links.send(out, x=k & 1, y=k >> 1).astype(F32))
        total = total[0] + got[0][:192] + got[1][:192] + got[2][:192]
        if small is not None:
            small = small + got[0][192:] + got[1][192:] + got[2][192:]
        total = total.reshape(4, 48, columns)
        got = []
        for s in range(1, 4):
            out = total[s].astype(BF)
            if small is not None:
                out = jnp.concatenate([out, small.astype(BF)], axis=0)
            got.append(links.send(out, z=s).astype(F32))
        total = total[0] + got[0][:48] + got[1][:48] + got[2][:48]
        if small is not None:
            small = small + got[0][48:] + got[1][48:] + got[2][48:]
        if links.outer > 1 and small is not None:
            small = lax.psum(small, "dp", axis_index_groups=links.groups())
        return links.outer_sum(total), small

    total_r, _ = reduced(keep_r, send_r, None, None)
    total_q, _ = reduced(keep_q[:768], send_q[:768], None, None)
    small_own = jnp.concatenate([keep_q[768:].astype(F32), extra], axis=0)
    small_own = small_own.astype(BF)
    small = small_own.astype(F32)
    small = small + links.send(small.astype(BF), c=1).astype(F32)
    send_now = small.astype(BF)
    for k in range(1, 4):
        small = small + links.send(send_now, x=k & 1, y=k >> 1).astype(F32)
    send_now = small.astype(BF)
    for s in range(1, 4):
        small = small + links.send(send_now, z=s).astype(F32)
    if links.outer > 1:
        small = lax.psum(small, "dp", axis_index_groups=links.groups())

    qkv_grad = total_q[:, 0:288].reshape(-1, 3, 96).transpose(1, 0, 2)
    out_grad = total_q[:, 288:].T
    exp_grad = total_r[:, 0:WIDTH]
    con_grad = total_r[:, WIDTH:].T
    norm_grad = small[0:6]
    qv_grad = lax.dynamic_slice_in_dim(small[6:8], head * 96, 96, 1)
    flat = small[16:].reshape(-1)
    eb_grad = lax.dynamic_slice_in_dim(flat[:HIDDEN], head * WIDTH, WIDTH, 0)
    tab_grad = flat[HIDDEN : HIDDEN + 12 * table_rows].reshape(12, table_rows)
    tab_grad = lax.dynamic_slice_in_dim(tab_grad, head * 3, 3, 0).T

    news = (
        adamw_step(qkv_w, qkv_grad, qkv_m, qkv_s, RATE_MATRIX, DECAY_MATRIX)
        + adamw_step(out_w, out_grad, out_m, out_s, RATE_MATRIX, DECAY_MATRIX)
        + adamw_step(exp_w, exp_grad, exp_m, exp_s, RATE_MATRIX, DECAY_MATRIX)
        + adamw_step(con_w, con_grad, con_m, con_s, RATE_MATRIX, DECAY_MATRIX)
        + adamw_step(qv_b, qv_grad, qv_m, qv_s, RATE_SMALL, 0.0)
        + adamw_step(exp_b, eb_grad, eb_m, eb_s, RATE_SMALL, 0.0)
        + adamw_step(table_w, tab_grad, tab_m, tab_s, RATE_SMALL, 0.0)
        + adamw_step(norm_p, norm_grad, norm_m, norm_s, RATE_SMALL, 0.0)
    )
    return (block_out, grad_tokens, *news)


def solution(mesh):
    tokens = P(("dp", "head"), None)
    qkv, rows_head, rows_dp = P(None, "dp", "head"), P("head", "dp"), P("dp", "head")
    pair, unit, none = P(None, "head"), P("head"), P()
    matrices = (qkv, rows_head, rows_dp, rows_head)
    small = (pair, unit, pair, none)
    in_specs = (tokens, P("dp"), tokens, *matrices, *small)
    in_specs += tuple(s for spec in (*matrices, *small) for s in (spec, spec))
    out_specs = (tokens, tokens) + tuple(
        s for spec in (*matrices, *small) for s in (spec, spec, spec)
    )
    return jax.shard_map(
        functools.partial(per_device, Links(dict(mesh.shape))),
        mesh=mesh, in_specs=in_specs, out_specs=out_specs, check_vma=False,
    )
```

```python
import functools
import math

import jax
import jax.numpy as jnp
import numpy as np
from jax import lax
from jax.experimental import pallas as pl
from jax.experimental.pallas import tpu as pltpu
from jax.sharding import PartitionSpec as P

HEAD_DIM = 32
WINDOW = 7
SIDE = 14
SHIFT = 3
STEP = 10
CANVAS = SIDE * SIDE
PLACES = WINDOW * WINDOW
SLOT = 64
QUAD_ROWS = 4 * CANVAS
SPAN = 208
WIDTH = 384
GROUPS = 3
PACK = 4
HIDDEN = 1536
CHUNK = 512

NORM_EPS = 1e-05
BETA_ONE = 0.9
BETA_TWO = 0.999
ADAM_EPS = 1e-08
RATE_MATRIX = 0.1
RATE_SMALL = 0.5
DECAY_MATRIX = 0.05
MASKED = -1e30
LOG2E = math.log2(math.e)
SCALE = HEAD_DIM**-0.5
ROOT_HALF = 0.7071067811865476
INV_ROOT_TWO_PI = 1.0 / 2.5066282746310002
BF = jnp.bfloat16
F32 = jnp.float32


def slot_rows():
    rows = -np.ones((4, SLOT), np.int64)
    for win in range(4):
        for place in range(PLACES):
            row = (win // 2) * WINDOW + place // WINDOW
            col = (win % 2) * WINDOW + place % WINDOW
            rows[win, place] = ((row + SHIFT) % SIDE) * SIDE + (col + SHIFT) % SIDE
    return rows.reshape(-1)


def region_codes():
    def band(v):
        return 0 if v < SIDE - WINDOW else (1 if v < SIDE - SHIFT else 2)

    codes = np.full((4, SLOT), 999.0, np.float32)
    for win in range(4):
        for place in range(PLACES):
            row = (win // 2) * WINDOW + place // WINDOW
            col = (win % 2) * WINDOW + place % WINDOW
            codes[win, place] = 4 * (3 * band(row) + band(col))
    return codes.reshape(-1)


def tables():
    line = np.array([13 * (p // WINDOW) + p % WINDOW for p in range(PLACES)], np.float32)
    out = np.full((8, 4 * SLOT), -1000.0, np.float32)
    out[0] = slot_rows()
    out[0][out[0] < 0] = -1000.0
    out[1] = region_codes()
    out[2, :PLACES] = 43 + line
    out[3, :PLACES] = out[3, SLOT : SLOT + PLACES] = 84 - line
    out[4, :PLACES] = line
    return out, out.T.copy()


def onehot(shape, axis, places):
    index = lax.broadcasted_iota(jnp.int32, shape, axis).astype(F32)
    return jnp.where(index == places, 1.0, 0.0).astype(BF)


def dot_nn(a, b):
    return jnp.dot(a, b, preferred_element_type=F32)


def dot_nt(a, b):
    return lax.dot_general(a, b, (((1,), (1,)), ((), ())), preferred_element_type=F32)


def stats(values):
    centred = values - jnp.mean(values, axis=-1, keepdims=True)
    inv_std = lax.rsqrt(jnp.mean(centred * centred, axis=-1, keepdims=True) + NORM_EPS)
    return centred * inv_std, inv_std


def norm_back(grad_norm, hat, inv_std, gain_row):
    grad_hat = grad_norm * gain_row
    inner = grad_hat - jnp.mean(grad_hat, axis=-1, keepdims=True)
    return inv_std * (inner - hat * jnp.mean(grad_hat * hat, axis=-1, keepdims=True))


def owners(idx):
    z, y, x, c = idx[0], idx[1], idx[2], idx[3]
    for e in range(2):
        for k in range(4):
            for s in range(4):
                row = ((z ^ s) * 2 + (y ^ (k >> 1))) * 48
                yield e, k, s, pl.multiple_of(row, 16), (x ^ (k & 1)) * 2 + (c ^ e)


def spread(block):
    four = jnp.concatenate([block] * PACK, axis=1)
    rows = lax.broadcasted_iota(jnp.int32, four.shape, 0) // HEAD_DIM
    lanes = lax.broadcasted_iota(jnp.int32, four.shape, 1) // SLOT
    return jnp.where(rows == lanes, four, jnp.zeros_like(four))


def assemble(idx, refs, put):
    for e, k, s, row, head in owners(idx):
        put(row, head, refs[e * 4 + k][s * 48 : (s + 1) * 48, :])


UNITS = [(win, g) for win in range(4) for g in range(GROUPS)]


def window(win):
    return slice(win * SLOT, (win + 1) * SLOT)


def feats(g):
    return slice(g * 128, (g + 1) * 128)


def own_blocks(parts):
    rows = []
    for g in range(GROUPS):
        for h in range(PACK):
            rows.append(
                jnp.concatenate(
                    [
                        parts[win, g][
                            h * HEAD_DIM : (h + 1) * HEAD_DIM, h * SLOT : (h + 1) * SLOT
                        ]
                        for win in range(4)
                    ],
                    axis=1,
                )
            )
    return jnp.concatenate(rows, axis=0)


def canvas_start(step):
    return pl.multiple_of((step // 4) * QUAD_ROWS + (step % 4) * 192, 16)


def pack_attention(qkv, out_t, first):
    first[...] = jnp.concatenate([qkv[0], qkv[1], qkv[2], out_t[...]], axis=1).astype(BF)


def pack_mlp(expand, contract_t, qv, eb, table_t, second, own):
    second[:, 0:WIDTH] = expand[...].astype(BF)
    second[:, WIDTH:] = contract_t[...].astype(BF)
    own[...] = jnp.zeros(own.shape, BF)
    own[0:2, 0:96] = qv[...].astype(BF)
    own[2:3, :] = eb[...].reshape(1, -1).astype(BF)
    own[3:6, 0 : table_t.shape[1]] = table_t[...].astype(BF)


def prepare(
    idx, own, by_c, by_x, by_xc, tok, gout, crop, rows_c, cols_c, par_h,
    na, xt, ut, u, tokv, goutv, got, tb, bias, eb, code_row, code_col, par, down, across,
    sbuf,
):
    x, c = idx[2], idx[3]
    for ref, dx, dc in ((own, 0, 0), (by_c, 0, 1), (by_x, 1, 0), (by_xc, 1, 1)):
        sbuf[(x ^ dx) * 2 + (c ^ dc)] = ref[...].astype(F32)
    pad = jnp.zeros((1, WIDTH), F32)
    qv = [jnp.concatenate([sbuf[h, r : r + 1, 0:96] for h in range(4)], axis=1) for r in (0, 1)]
    bias[0:16, :] = jnp.concatenate(
        [jnp.concatenate([qv[0], pad, qv[1]], axis=1), jnp.zeros((15, 3 * WIDTH), F32)], axis=0
    ).astype(BF)
    eb[...] = jnp.concatenate(
        [
            jnp.concatenate([sbuf[h, 2:3, :] for h in range(4)], axis=1),
            jnp.zeros((15, HIDDEN), F32),
        ],
        axis=0,
    ).astype(BF)
    up = onehot((SLOT, 128), 1, cols_c[0:SLOT, 2:3])
    down[...] = onehot((128, 2 * SLOT), 0, rows_c[3:4, 0 : 2 * SLOT])
    over = onehot((256, SLOT), 0, rows_c[4:5, 0:SLOT])
    across[...] = over
    for g in range(GROUPS):
        blocks = []
        for h in range(g * PACK, (g + 1) * PACK):
            row = sbuf[h // 3, 3 + h % 3 : 4 + h % 3, 0:256]
            lines = pltpu.roll(
                jnp.broadcast_to(row, (128, 256)), 129, axis=1, stride=1, stride_axis=0
            )
            keyed = dot_nn(up, lines.astype(BF)).astype(BF)
            blocks.append(dot_nn(keyed, over))
        tb[g] = jnp.concatenate(blocks, axis=1) * LOG2E
    tokv[...] = tok[...]
    goutv[...] = gout[...]
    par[...] = jnp.concatenate([par_h[...], jnp.zeros((2, WIDTH), F32)], axis=0)
    lane = lax.broadcasted_iota(jnp.int32, (4 * SLOT, 128), 1)
    ones = jnp.where(lane == 0, 1.0, 0.0).astype(BF)
    to_slots = []
    for turn in range(4):
        ut[turn] = onehot((4 * SLOT, SPAN), 1, cols_c[:, 0:1] + 4.0 * turn)
        u[turn] = onehot((SPAN, 4 * SLOT), 0, rows_c[0:1, :] + 4.0 * turn)
        to_slots.append(ut[turn])
    head = idx[2] * 2 + idx[3]
    for block in range(na.shape[0] // 4):
        hat, _ = stats(tok[block * QUAD_ROWS : (block + 1) * QUAD_ROWS, :].astype(F32))
        n1 = (hat * par_h[0:1, :] + par_h[1:2, :]).astype(BF)
        sides = jnp.concatenate([n1, hat.astype(BF)], axis=1)
        crops = crop[pl.ds(head * (na.shape[0] // 4) + block, 1), :] & 3
        for turn in range(4):
            step, start = 4 * block + turn, 192 * turn
            both = dot_nn(to_slots[turn], sides[start : start + SPAN]).astype(BF)
            na[step] = jnp.concatenate([both[:, 0:WIDTH], ones], axis=1)
            xt[step] = jnp.concatenate([both[:, WIDTH:], ones], axis=1).T[0:400, :]
            quad = crops[:, start : start + SPAN]
            quad = jnp.broadcast_to(quad.astype(F32), (8, SPAN)).astype(BF)
            code_row[step] = dot_nt(quad, to_slots[turn]) + rows_c[1:2, :]
            code_col[step] = dot_nt(to_slots[turn], quad) + cols_c[:, 1:2]
    got[...] = gout[...].T


def attention_forward(
    idx, p0, p1, p2, p3, p4, p5, p6, p7, nas, codes_row, codes_col, u, bias, tb,
    mrg, qt, kt, vv, pt, mt, wnat, outt, wout,
    wbuf, waug, wt,
):
    def put(row, head, value):
        wbuf[head, pl.ds(row, 48), :] = value

    assemble(idx, (p0, p1, p2, p3, p4, p5, p6, p7), put)
    for j in range(3):
        waug[0:WIDTH, j * WIDTH : (j + 1) * WIDTH] = jnp.concatenate(
            [wbuf[h, :, 96 * j : 96 * (j + 1)] for h in range(4)], axis=1
        )
    out_t = jnp.concatenate([wbuf[h, :, 288:384] for h in range(4)], axis=1)
    outt[...] = out_t
    wout[...] = out_t.T
    waug[WIDTH : WIDTH + 16, :] = bias[...]
    waug[WIDTH + 16 : 512, :] = jnp.zeros((112, 3 * WIDTH), BF)
    wnat[...] = waug[0:WIDTH, :]
    wt[...] = waug[...].T

    def canvas(step, carry):
        turn = step % 4
        start = canvas_start(step)
        na = nas[step]
        all_t = dot_nt(wt[...], na).astype(BF)
        kv = dot_nt(na, wt[WIDTH:, :]).astype(BF)
        q_t, v_t = all_t[0:WIDTH], all_t[2 * WIDTH :]
        code_row, code_col = codes_row[step], codes_col[step]
        masks = []
        for win in range(4):
            row = jnp.concatenate([code_row[0:1, window(win)]] * PACK, axis=1)
            masks.append(jnp.where(code_col[window(win), 0:1] == row, 0.0, MASKED))
        scores = {
            (w, g): dot_nn(kv[window(w), feats(g)], spread(q_t[feats(g), window(w)]))
            for w, g in UNITS
        }
        probs = {}
        for w, g in UNITS:
            sc = scores[w, g] * (SCALE * LOG2E) + (tb[g] + masks[w])
            grown = jnp.exp2(sc - jnp.max(sc, axis=0, keepdims=True))
            probs[w, g] = (grown * (1.0 / jnp.sum(grown, axis=0, keepdims=True))).astype(BF)
        mixed = {(w, g): dot_nn(v_t[feats(g), window(w)], probs[w, g]) for w, g in UNITS}
        merged_t = own_blocks(mixed).astype(BF)
        back = dot_nt(u[turn], merged_t).astype(BF)
        for w, g in UNITS:
            pt[step, w * GROUPS + g] = probs[w, g]
        mt[step] = merged_t
        qt[step] = q_t
        kt[step] = all_t[WIDTH : 2 * WIDTH]
        vv[step] = kv[:, WIDTH:]
        begin = pl.ds(start, 16)
        mrg[begin, :] = back[0:16] + jnp.where(turn == 0, jnp.zeros((16, WIDTH), BF), mrg[begin, :])
        mrg[pl.ds(pl.multiple_of(start + 16, 16), SPAN - 16), :] = back[16:]
        return carry

    lax.fori_loop(0, nas.shape[0], canvas, 0)


TILE = 784


def mlp_begin(mrg, tok, outt, par, mid, n2, n2t):
    lane = lax.broadcasted_iota(jnp.int32, (TILE, 128), 1)
    ones = jnp.where(lane == 0, 1.0, 0.0).astype(BF)

    def head_rows(t, carry):
        rows = pl.ds(pl.multiple_of(t * TILE, 16), TILE)
        middle = tok[rows, :].astype(F32) + dot_nt(mrg[rows, :], outt[...]) + par[4:5, :]
        mid[rows, :] = middle
        hat, _ = stats(middle)
        n2[rows, 0:WIDTH] = (hat * par[2:3, :] + par[3:4, :]).astype(BF)
        n2[rows, WIDTH:512] = ones
        return carry

    lax.fori_loop(0, tok.shape[0] // TILE, head_rows, 0)
    n2t[...] = n2[...].T[0:400, :]


def mlp(
    idx, p0, p1, p2, p3, p4, p5, p6, p7, n2, n2t, got, gout, eb,
    acc_m, acc_g, keep, send, ebg,
    eaug, ct, hid, gpr, cg, eg,
):
    tiles = gout.shape[0] // TILE

    def put(row, head, value):
        lanes = pl.ds(pl.multiple_of(head * WIDTH, 128), WIDTH)
        eaug[pl.ds(row, 48), lanes] = value[:, 0:WIDTH]
        ct[pl.ds(row, 48), lanes] = value[:, WIDTH:]

    assemble(idx, (p0, p1, p2, p3, p4, p5, p6, p7), put)
    eaug[WIDTH : WIDTH + 16, :] = eb[...]
    eaug[WIDTH + 16 : 512, :] = jnp.zeros((112, HIDDEN), BF)
    acc_m[...] = jnp.zeros(acc_m.shape, F32)
    acc_g[...] = jnp.zeros(acc_g.shape, F32)

    def chunk(step, carry):
        cols = pl.ds(pl.multiple_of(step * CHUNK, 128), CHUNK)

        def unit_rows(t, carry):
            rows = pl.ds(pl.multiple_of(t * TILE, 16), TILE)
            pre = dot_nn(n2[rows, :], eaug[:, cols])
            grad_hidden = dot_nn(gout[rows, :], ct[:, cols])
            phi = 0.5 + 0.5 * lax.erf(pre * ROOT_HALF)
            bell = jnp.exp2(pre * pre * (-0.5 * LOG2E)) * INV_ROOT_TWO_PI
            hidden = (pre * phi).astype(BF)
            grad_pre = (grad_hidden * (phi + pre * bell)).astype(BF)
            hid[rows, :] = hidden
            gpr[rows, :] = grad_pre
            acc_m[rows, :] += dot_nt(hidden, ct[:, cols])
            acc_g[rows, :] += dot_nt(grad_pre, eaug[0:WIDTH, cols])
            return carry

        lax.fori_loop(0, tiles, unit_rows, 0)
        cg[:, cols] = dot_nn(got[...], hid[...]).astype(BF)
        grads = dot_nn(n2t[...], gpr[...])
        eg[:, cols] = grads[0:WIDTH].astype(BF)
        ebg[:, cols] = grads[WIDTH : WIDTH + 8]
        return carry

    lax.fori_loop(0, HIDDEN // CHUNK, chunk, 0)
    for e, k, s, row, head in owners(idx):
        dst = (keep, send)[e]
        lanes = pl.ds(pl.multiple_of(head * WIDTH, 128), WIDTH)
        base = (k * 4 + s) * 48
        dst[base : base + 48, 0:WIDTH] = eg[pl.ds(row, 48), lanes]
        dst[base : base + 48, WIDTH:] = cg[pl.ds(row, 48), lanes]


def mlp_end(mid, acc_m, acc_g, gout, par, blk, gmid, sums):
    def tail_rows(t, carry):
        rows = pl.ds(pl.multiple_of(t * TILE, 16), TILE)
        middle = mid[rows, :]
        blk[rows, :] = (middle + acc_m[rows, :] + par[5:6, :]).astype(BF)
        hat, inv = stats(middle)
        g = acc_g[rows, :]
        top = gout[rows, :].astype(F32)
        grad_mid = top + norm_back(g, hat, inv, par[2:3, :])
        gmid[rows, :] = grad_mid
        parts = (g * hat, g, grad_mid, top)
        return tuple(c + jnp.sum(p, axis=0, keepdims=True) for c, p in zip(carry, parts))

    zero = jnp.zeros((1, WIDTH), F32)
    totals = lax.fori_loop(0, mid.shape[0] // TILE, tail_rows, (zero,) * 4)
    sums[...] = jnp.concatenate([zero, zero, *totals, zero, zero], axis=0)


def attention_backward(
    idx, gmid, qt, kt, vv, pt, mt, xt, wout, ut, wnat, par, sums, ebg, down, across,
    keep, send, gta,
    ntall, wacc, oacc, table,
):
    table[...] = jnp.zeros(table.shape, F32)
    oacc[...] = jnp.zeros(oacc.shape, F32)
    wacc[...] = jnp.zeros(wacc.shape, F32)

    def canvas(step, carry):
        turn = step % 4
        rows = pl.ds(canvas_start(step), SPAN)
        gmw = dot_nn(ut[turn], gmid[rows, :].astype(BF)).astype(BF)
        gmt = dot_nt(wout[...], gmw).astype(BF)
        q_t, k_t, v_w = qt[step], kt[step], vv[step]
        gm_s = {(w, g): spread(gmt[feats(g), window(w)]) for w, g in UNITS}
        q_s = {(w, g): spread(q_t[feats(g), window(w)]) for w, g in UNITS}
        gp = {(w, g): dot_nn(v_w[window(w), feats(g)], gm_s[w, g]) for w, g in UNITS}
        probs_b = {(w, g): pt[step, w * GROUPS + g] for w, g in UNITS}
        gs = {}
        for w, g in UNITS:
            probs = probs_b[w, g].astype(F32)
            delta = jnp.sum(probs * gp[w, g], axis=0, keepdims=True)
            gs[w, g] = (probs * (gp[w, g] - delta)).astype(BF)
        gq = {(w, g): dot_nn(k_t[feats(g), window(w)], gs[w, g]) for w, g in UNITS}
        gk = {(w, g): dot_nt(q_s[w, g], gs[w, g]) for w, g in UNITS}
        gv = {(w, g): dot_nt(gm_s[w, g], probs_b[w, g]) for w, g in UNITS}

        def rows_of(parts):
            return jnp.concatenate(
                [
                    jnp.concatenate([parts[w, g] for w in range(4)], axis=1)
                    for g in range(GROUPS)
                ],
                axis=0,
            )

        g_all = jnp.concatenate(
            [
                (own_blocks(gq) * SCALE).astype(BF),
                (rows_of(gk) * SCALE).astype(BF),
                rows_of(gv).astype(BF),
            ],
            axis=0,
        )
        gta[step] = g_all
        wacc[...] += dot_nt(xt[step], g_all)
        oacc[...] += dot_nn(mt[step], gmw)
        for g in range(GROUPS):
            table[g] += sum(gs[w, g].astype(F32) for w in range(4))
        return carry

    lax.fori_loop(0, qt.shape[0], canvas, 0)
    columns = par[...].T
    gain, offset = columns[:, 0:1], columns[:, 1:2]
    totals = wacc[WIDTH : WIDTH + 1, :]
    weights = wnat[...].astype(F32)
    gain_sum = jnp.sum(weights * wacc[0:WIDTH, :], axis=1, keepdims=True)
    offset_sum = jnp.sum(weights * totals, axis=1, keepdims=True)
    norm_rows = jnp.concatenate([gain_sum, offset_sum, jnp.zeros((WIDTH, 6), F32)], axis=1).T
    grads = wacc[0:WIDTH, :] * gain + offset * totals
    out_t = oacc[...].T
    for h in range(4):
        pieces = [grads[:, j * WIDTH + 96 * h : j * WIDTH + 96 * (h + 1)] for j in range(3)]
        pieces.append(out_t[:, 96 * h : 96 * (h + 1)])
        ntall[h] = jnp.concatenate(pieces, axis=1).astype(BF)
    for e, k, s, row, head in owners(idx):
        base = (k * 4 + s) * 48
        (keep, send)[e][base : base + 48, :] = ntall[head, pl.ds(row, 48), :]
    rows = [norm_rows[0:2, :], sums[2:6, :], totals[:, 0:WIDTH], totals[:, 2 * WIDTH :]]
    rows += [ebg[0:1, j * WIDTH : (j + 1) * WIDTH] for j in range(4)]
    for g in range(GROUPS):
        high = table[g].astype(BF)
        low = (table[g] - high.astype(F32)).astype(BF)
        both = jnp.concatenate([high, low], axis=0)
        for h in range(PACK):
            spaced = dot_nt(both[:, h * SLOT : (h + 1) * SLOT], across[...]).astype(BF)
            lines = dot_nn(down[...], spaced)
            lines = pltpu.roll(lines, 0, axis=1, stride=1, stride_axis=0)
            row = jnp.sum(lines, axis=0, keepdims=True)
            rows.append(jnp.concatenate([row, jnp.zeros((1, 128), F32)], axis=1))
    rows.append(jnp.zeros((8, WIDTH), F32))
    small = jnp.concatenate(rows, axis=0).astype(BF)
    keep[768:800, :] = small
    send[768:800, :] = small


def tokens_end(tok, gmid, gta, wnat, u, par, gtok):
    def block_rows(block, carry):
        ends = []
        for turn in range(4):
            g1t = dot_nn(wnat[...], gta[4 * block + turn])
            high = g1t.astype(BF)
            low = (g1t - high.astype(F32)).astype(BF)
            ends.append(dot_nt(u[turn], high) + dot_nt(u[turn], low))
        pieces = [ends[0][0:192]]
        for turn in range(1, 4):
            pieces += [ends[turn - 1][192:] + ends[turn][0:16], ends[turn][16:192]]
        g1 = jnp.concatenate([*pieces, ends[3][192:]], axis=0)
        rows = pl.ds(pl.multiple_of(block * QUAD_ROWS, 16), QUAD_ROWS)
        hat, inv = stats(tok[rows, :].astype(F32))
        gtok[rows, :] = gmid[rows, :] + norm_back(g1, hat, inv, par[0:1, :])
        return carry

    lax.fori_loop(0, gta.shape[0] // 4, block_rows, 0)


def plane_sum(keep, got, *refs):
    small = None
    if len(refs) > 4:
        small = keep[768:, :].astype(F32) + got[768:, :].astype(F32)
        refs[4][...] = small
    for k in range(4):
        block = slice(k * 192, (k + 1) * 192)
        value = keep[block, :].astype(F32) + got[block, :].astype(F32)
        if k == 0:
            refs[0][...] = value
        else:
            refs[k][0:192, :] = value.astype(BF)
            if small is not None:
                refs[k][192:, :] = small.astype(BF)


def line_sum(own, r1, r2, r3, *refs):
    small = None
    parts = (r1, r2, r3)
    if len(refs) > 4:
        mine, *refs = refs
        small = mine[...] + sum(r[192:, :].astype(F32) for r in parts)
        refs[4][...] = small
    for s in range(4):
        block = slice(s * 48, (s + 1) * 48)
        value = own[block, :] + sum(r[block, :].astype(F32) for r in parts)
        if s == 0:
            refs[0][...] = value
        else:
            refs[s][0:48, :] = value.astype(BF)
            if small is not None:
                refs[s][48:, :] = small.astype(BF)


def adamw(master, grad, moment, square, step_rate, decay_rate):
    moment_new = BETA_ONE * moment + (1.0 - BETA_ONE) * grad
    square_new = BETA_TWO * square + (1.0 - BETA_TWO) * grad * grad
    moment_hat = moment_new * (1.0 / (1.0 - BETA_ONE**STEP))
    square_hat = square_new * (1.0 / (1.0 - BETA_TWO**STEP))
    step = moment_hat / (jnp.sqrt(square_hat) + ADAM_EPS)
    if decay_rate:
        step = step + decay_rate * master
    return master - step_rate * step, moment_new, square_new


def update(refs, grad, outs, step_rate, decay_rate, at=...):
    master, moment, square = (r[at] for r in refs)
    news = adamw(master, grad, moment, square, step_rate, decay_rate)
    for out, new in zip(outs, news):
        out[at] = new


def step_mlp(n_parts, *refs):
    parts, refs = refs[:n_parts], refs[n_parts:]
    total = sum(r[...].astype(F32) for r in parts)
    update(refs[0:3], total[:, 0:WIDTH], refs[6:9], RATE_MATRIX, DECAY_MATRIX)
    update(refs[3:6], total[:, WIDTH:], refs[9:12], RATE_MATRIX, DECAY_MATRIX)


def step_attention(n_parts, rows, idx, *refs):
    parts, refs = refs[:n_parts], refs[n_parts:]
    total = sum(r[0:rows, :].astype(F32) for r in parts)
    small, refs = refs[0], refs[1:]
    small = small[...] + sum(r[rows:, :].astype(F32) for r in parts[1:])
    head = idx[2] * 2 + idx[3]

    def pick(blocks):
        return sum(jnp.where(head == h, block, 0.0) for h, block in enumerate(blocks))

    ins, outs = refs[:18], refs[18:]
    for j in range(3):
        update(
            ins[0:3], total[:, 96 * j : 96 * (j + 1)], outs[0:3], RATE_MATRIX, DECAY_MATRIX, at=j
        )
    update(ins[3:6], total[:, 288:384], outs[3:6], RATE_MATRIX, DECAY_MATRIX)
    qv = pick([small[6:8, 96 * h : 96 * (h + 1)] for h in range(4)])
    update(ins[6:9], qv, outs[6:9], RATE_SMALL, 0.0)
    eb = pick([small[8 + h : 9 + h, :] for h in range(4)])
    update(ins[9:12], eb.reshape(ins[9].shape), outs[9:12], RATE_SMALL, 0.0)
    table_rows = ins[12].shape[1]
    table = pick([small[12 + 3 * h : 15 + 3 * h, 0:table_rows] for h in range(4)])
    update(ins[12:15], table, outs[12:15], RATE_SMALL, 0.0)
    update(ins[15:18], small[0:6, :], outs[15:18], RATE_SMALL, 0.0)


class Links:
    def __init__(self, sizes):
        self.sizes = sizes
        self.outer = sizes["dp"] // 8

    def perm(self, z=0, y=0, x=0, c=0):
        pairs = []
        for flat in range(self.sizes["dp"] * self.sizes["head"]):
            head, dp = flat % 4, flat // 4
            inner, place = dp // self.outer, dp % self.outer
            inner ^= z * 2 + y
            pairs.append((flat, (inner * self.outer + place) * 4 + (head ^ (x * 2 + c))))
        return pairs

    def send(self, value, **flips):
        return lax.ppermute(value, ("dp", "head"), self.perm(**flips))

    def groups(self):
        return [[i * self.outer + j for j in range(self.outer)] for i in range(8)]

    def gather_line(self, shard):
        if self.outer > 1:
            shard = lax.all_gather(
                shard, "dp", axis=0, tiled=True, axis_index_groups=self.groups()
            )
        return jnp.concatenate([shard] + [self.send(shard, z=s) for s in range(1, 4)], axis=0)

    def gather_plane(self, line):
        return [line] + [self.send(line, x=k & 1, y=k >> 1) for k in range(1, 4)]

    def gather_core(self, plane):
        return list(plane) + [self.send(part, c=1) for part in plane]

    def to_plane(self, blocks):
        return [self.send(b, x=k & 1, y=k >> 1) for k, b in enumerate(blocks, 1)]

    def to_line(self, blocks):
        return [self.send(b, z=s) for s, b in enumerate(blocks, 1)]

    def outer_sum(self, value):
        if self.outer > 1:
            value = lax.psum_scatter(
                value, "dp", scatter_dimension=0, tiled=True, axis_index_groups=self.groups()
            )
        return value


SMEM = pl.BlockSpec(memory_space=pltpu.SMEM)
VMEM = pl.BlockSpec(memory_space=pltpu.VMEM)


class Far:
    def __init__(self, value):
        self.value = value


def placed(arg):
    if isinstance(arg, Far):
        return pltpu.with_memory_space_constraint(arg.value, pltpu.HBM)
    return pltpu.with_memory_space_constraint(arg, pltpu.VMEM)


def call(kernel, outs, *args, scratch=(), limit=16, scalars=None, far=(), time=1):
    lead = [] if scalars is None else [scalars]
    name = getattr(kernel, "__name__", None) or kernel.func.__name__
    return pl.pallas_call(
        kernel,
        in_specs=[SMEM] * len(lead) + [VMEM] * len(args),
        out_specs=[VMEM] * len(outs),
        out_shape=[(pltpu.HBM if i in far else pltpu.VMEM)(s, d) for i, (s, d) in enumerate(outs)],
        scratch_shapes=[pltpu.VMEM(s, d) for s, d in scratch],
        compiler_params=pltpu.CompilerParams(vmem_limit_bytes=limit * 2**20),
        cost_estimate=pl.CostEstimate(
            flops=int(time * 1.15e9), bytes_accessed=0, transcendentals=0
        ),
        name=name,
    )(*lead, *(placed(a) for a in args))


def per_device(links, *args):
    (
        tokens, crop_ids, grad_out, qkv_w, out_w, exp_w, con_w, qv_b, exp_b, table_w, norm_p,
        qkv_m, qkv_s, out_m, out_s, exp_m, exp_s, con_m, con_s,
        qv_m, qv_s, eb_m, eb_s, tab_m, tab_s, norm_m, norm_s,
    ) = args
    rows_all = tokens.shape[0]
    canvases = rows_all // CANVAS
    head = lax.axis_index("head")
    dp = lax.axis_index("dp") // links.outer
    idx = jnp.stack([dp // 2, dp % 2, head // 2, head % 2]).astype(jnp.int32)
    slots = 4 * SLOT
    wide = (rows_all, WIDTH)
    square = (WIDTH, WIDTH)
    fm = (canvases, WIDTH, slots)
    tm = (canvases, slots, WIDTH)

    rows_own = exp_w.shape[0]
    (first,) = call(pack_attention, [((rows_own, WIDTH), BF)], Far(qkv_w), Far(out_w.T))
    line = links.gather_line(first)
    firsts = links.gather_plane(line)
    second, own = call(
        pack_mlp, [((rows_own, 2 * WIDTH), BF), ((16, WIDTH), BF)],
        Far(exp_w), Far(con_w.T), Far(qv_b), Far(exp_b), Far(table_w.T),
    )
    by_c, by_x, by_xc = links.send(own, c=1), links.send(own, x=1), links.send(own, x=1, c=1)

    crop_rows = crop_ids.reshape(-1, QUAD_ROWS)
    rows_c, cols_c = (jnp.asarray(t) for t in tables())
    line, own = lax.optimization_barrier((line, own))
    to_slots = (4, slots, SPAN)
    prepared = call(
        prepare,
        [
            ((canvases, slots, 512), BF), ((canvases, 400, slots), BF), (to_slots, BF),
            ((4, SPAN, slots), BF), (wide, BF), (wide, BF), ((WIDTH, rows_all), BF),
            ((GROUPS, SLOT, slots), F32), ((16, 3 * WIDTH), BF), ((16, HIDDEN), BF),
            ((canvases, 8, slots), F32), ((canvases, slots, 8), F32), ((8, WIDTH), F32),
            ((128, 2 * SLOT), BF), ((256, SLOT), BF),
        ],
        own, by_c, by_x, by_xc, Far(tokens), Far(grad_out), Far(crop_rows), Far(rows_c),
        Far(cols_c), Far(norm_p),
        scratch=[((4, 16, WIDTH), F32)], limit=16, scalars=idx, time=5,
    )
    (second, *prepared) = lax.optimization_barrier((second, *prepared))
    nas, xt, ut, u, tok, gout, got, bias_t, bias16, eb16, code_row, code_col, par = prepared[:13]
    down, across = prepared[13:]
    line_s = links.gather_line(second)
    plane_s = links.gather_plane(line_s)
    firsts = list(lax.optimization_barrier((*firsts, nas))[:4])
    firsts = links.gather_core(firsts)
    firsts[0], line_s = lax.optimization_barrier((firsts[0], line_s))
    merged, qt, kt, vv, pt, mt, wnat, outt, wout = call(
        attention_forward,
        [
            (wide, BF), (fm, BF), (fm, BF), (tm, BF), ((canvases, 12, SLOT, slots), BF), (fm, BF),
            ((WIDTH, 3 * WIDTH), BF), (square, BF), (square, BF),
        ],
        *firsts, nas, code_row, code_col, u, bias16, bias_t,
        scratch=[
            ((4, WIDTH, WIDTH), BF), ((512, 3 * WIDTH), BF), ((3 * WIDTH, 512), BF),
        ],
        limit=10, scalars=idx, time=14,
    )
    merged, *plane_s = lax.optimization_barrier((merged, *plane_s))
    seconds = links.gather_core(plane_s)
    middle, n2, n2t = call(
        mlp_begin, [(wide, F32), ((rows_all, 512), BF), ((400, rows_all), BF)],
        merged, tok, outt, par, time=3,
    )
    acc_m, acc_g, keep_r, send_r, eb_grad = call(
        mlp,
        [
            (wide, F32), (wide, F32), ((768, 2 * WIDTH), BF), ((768, 2 * WIDTH), BF),
            ((8, HIDDEN), F32),
        ],
        *seconds, n2, n2t, got, gout, eb16,
        scratch=[
            ((512, HIDDEN), BF), ((WIDTH, HIDDEN), BF), ((rows_all, CHUNK), BF),
            ((rows_all, CHUNK), BF), ((WIDTH, HIDDEN), BF), ((WIDTH, HIDDEN), BF),
        ],
        limit=24, scalars=idx, time=18,
    )
    got_r = links.send(send_r, c=1)
    block_out, grad_mid, sums = call(
        mlp_end, [(wide, BF), (wide, F32), ((8, WIDTH), F32)], middle, acc_m, acc_g, gout, par,
        limit=16, far=(0,), time=3,
    )
    block_r = [((192, 2 * WIDTH), F32)] + [((192, 2 * WIDTH), BF)] * 3
    got_r, grad_mid = lax.optimization_barrier((got_r, grad_mid))
    own_r, *blocks_r = call(plane_sum, block_r, keep_r, got_r)
    grad_mid, *blocks_r = lax.optimization_barrier((grad_mid, *blocks_r))
    plane_r = links.to_plane(blocks_r)
    keep_q, send_q, g_all = call(
        attention_backward,
        [((800, WIDTH), BF), ((800, WIDTH), BF), ((canvases, 3 * WIDTH, slots), BF)],
        grad_mid, qt, kt, vv, pt, mt, xt, wout, ut, wnat, par, sums, eb_grad, down, across,
        scratch=[
            ((4, WIDTH, WIDTH), BF), ((400, 3 * WIDTH), F32), (square, F32),
            ((GROUPS, SLOT, slots), F32),
        ],
        limit=16, scalars=idx, time=20,
    )
    *plane_r, send_q = lax.optimization_barrier((*plane_r, send_q))
    got_q = links.send(send_q, c=1)
    block_q = [((192, WIDTH), F32)] + [((224, WIDTH), BF)] * 3 + [((32, WIDTH), F32)]
    own_q, *blocks_q, small = call(plane_sum, block_q, keep_q, got_q)
    plane_q = links.to_plane(blocks_q)
    plane_r = lax.optimization_barrier((*plane_r, *blocks_q))[:3]
    line_r = [((48, 2 * WIDTH), F32)] + [((48, 2 * WIDTH), BF)] * 3
    own_r, *blocks_r = call(line_sum, line_r, own_r, *plane_r)
    parts_r = links.to_line(blocks_r)
    g_all = lax.optimization_barrier((g_all, *blocks_r))[0]
    (grad_tokens,) = call(
        tokens_end, [(wide, F32)], tok, grad_mid, g_all, wnat, u, par, far=(0,), time=5,
    )
    *plane_q, grad_tokens = lax.optimization_barrier((*plane_q, grad_tokens))
    line_q = [((48, WIDTH), F32)] + [((80, WIDTH), BF)] * 3 + [((32, WIDTH), F32)]
    own_q, *blocks_q, small = call(line_sum, line_q, own_q, *plane_q, small)
    parts_q = links.to_line(blocks_q)
    parts_q, parts_r = [own_q, *parts_q], [own_r, *parts_r]
    rows = 48
    if links.outer > 1:
        small = small + sum(p[48:].astype(F32) for p in parts_q[1:])
        small = lax.psum(small, "dp", axis_index_groups=links.groups())
        parts_q = [links.outer_sum(sum(p[:48].astype(F32) for p in parts_q))]
        parts_r = [links.outer_sum(sum(p.astype(F32) for p in parts_r))]
        rows = parts_q[0].shape[0]

    mlp_state = [exp_w, exp_m, exp_s, con_w.T, con_m.T, con_s.T]
    third = call(
        functools.partial(step_mlp, len(parts_r)), [(a.shape, F32) for a in mlp_state],
        *parts_r, *(Far(a) for a in mlp_state), far=range(6), time=2,
    )
    state = [
        qkv_w, qkv_m, qkv_s, out_w.T, out_m.T, out_s.T, qv_b, qv_m, qv_s, exp_b, eb_m, eb_s,
        table_w.T, tab_m.T, tab_s.T, norm_p, norm_m, norm_s,
    ]
    fourth = call(
        functools.partial(step_attention, len(parts_q), rows), [(a.shape, F32) for a in state],
        *parts_q, small, *(Far(a) for a in state), scalars=idx, far=range(18), time=2,
    )
    return (
        block_out, grad_tokens, *fourth[0:3], *(a.T for a in fourth[3:6]), *third[0:3],
        *(a.T for a in third[3:6]), *fourth[6:12], *(a.T for a in fourth[12:15]), *fourth[15:],
    )


def solution(mesh):
    tokens = P(("dp", "head"), None)
    qkv, rows_head, rows_dp = P(None, "dp", "head"), P("head", "dp"), P("dp", "head")
    pair, unit, none = P(None, "head"), P("head"), P()
    matrices = (qkv, rows_head, rows_dp, rows_head)
    small = (pair, unit, pair, none)
    in_specs = (tokens, P("dp"), tokens, *matrices, *small)
    in_specs += tuple(s for spec in (*matrices, *small) for s in (spec, spec))
    out_specs = (tokens, tokens) + tuple(
        s for spec in (*matrices, *small) for s in (spec, spec, spec)
    )
    return jax.shard_map(
        functools.partial(per_device, Links(dict(mesh.shape))),
        mesh=mesh, in_specs=in_specs, out_specs=out_specs, check_vma=False,
    )
```

```python
import functools
import math

import jax
import jax.numpy as jnp
import numpy as np
from jax import lax
from jax.experimental import pallas as pl
from jax.experimental.pallas import tpu as pltpu
from jax.sharding import PartitionSpec as P

HEAD_DIM = 32
WINDOW = 7
SIDE = 14
SHIFT = 3
STEP = 10
CANVAS = SIDE * SIDE
PLACES = WINDOW * WINDOW
SLOT = 64
QUAD_ROWS = 4 * CANVAS
SPAN = 208
WIDTH = 384
GROUPS = 3
PACK = 4
HIDDEN = 1536
CHUNK = 512

NORM_EPS = 1e-05
BETA_ONE = 0.9
BETA_TWO = 0.999
ADAM_EPS = 1e-08
RATE_MATRIX = 0.1
RATE_SMALL = 0.5
DECAY_MATRIX = 0.05
MASKED = -1e30
LOG2E = math.log2(math.e)
SCALE = HEAD_DIM**-0.5
ROOT_HALF = 0.7071067811865476
INV_ROOT_TWO_PI = 1.0 / 2.5066282746310002
BF = jnp.bfloat16
F32 = jnp.float32


def slot_rows():
    rows = -np.ones((4, SLOT), np.int64)
    for win in range(4):
        for place in range(PLACES):
            row = (win // 2) * WINDOW + place // WINDOW
            col = (win % 2) * WINDOW + place % WINDOW
            rows[win, place] = ((row + SHIFT) % SIDE) * SIDE + (col + SHIFT) % SIDE
    return rows.reshape(-1)


def region_codes():
    def band(v):
        return 0 if v < SIDE - WINDOW else (1 if v < SIDE - SHIFT else 2)

    codes = np.full((4, SLOT), 999.0, np.float32)
    for win in range(4):
        for place in range(PLACES):
            row = (win // 2) * WINDOW + place // WINDOW
            col = (win % 2) * WINDOW + place % WINDOW
            codes[win, place] = 4 * (3 * band(row) + band(col))
    return codes.reshape(-1)


def tables():
    line = np.array([13 * (p // WINDOW) + p % WINDOW for p in range(PLACES)], np.float32)
    out = np.full((8, 4 * SLOT), -1000.0, np.float32)
    out[0] = slot_rows()
    out[0][out[0] < 0] = -1000.0
    out[1] = region_codes()
    out[2, :PLACES] = 43 + line
    out[3, :PLACES] = out[3, SLOT : SLOT + PLACES] = 84 - line
    out[4, :PLACES] = line
    return out, out.T.copy()


def onehot(shape, axis, places):
    index = lax.broadcasted_iota(jnp.int32, shape, axis).astype(F32)
    return jnp.where(index == places, 1.0, 0.0).astype(BF)


def dot_nn(a, b):
    return jnp.dot(a, b, preferred_element_type=F32)


def dot_nt(a, b):
    return lax.dot_general(a, b, (((1,), (1,)), ((), ())), preferred_element_type=F32)


def stats(values):
    centred = values - jnp.mean(values, axis=-1, keepdims=True)
    inv_std = lax.rsqrt(jnp.mean(centred * centred, axis=-1, keepdims=True) + NORM_EPS)
    return centred * inv_std, inv_std


def norm_back(grad_norm, hat, inv_std, gain_row):
    grad_hat = grad_norm * gain_row
    inner = grad_hat - jnp.mean(grad_hat, axis=-1, keepdims=True)
    return inv_std * (inner - hat * jnp.mean(grad_hat * hat, axis=-1, keepdims=True))


def owners(idx):
    z, y, x, c = idx[0], idx[1], idx[2], idx[3]
    for e in range(2):
        for k in range(4):
            for s in range(4):
                row = ((z ^ s) * 2 + (y ^ (k >> 1))) * 48
                yield e, k, s, pl.multiple_of(row, 16), (x ^ (k & 1)) * 2 + (c ^ e)


def spread(block):
    four = jnp.concatenate([block] * PACK, axis=1)
    rows = lax.broadcasted_iota(jnp.int32, four.shape, 0) // HEAD_DIM
    lanes = lax.broadcasted_iota(jnp.int32, four.shape, 1) // SLOT
    return jnp.where(rows == lanes, four, jnp.zeros_like(four))


def assemble(idx, refs, put, order=(0, 1, 2, 3)):
    for e, k, s, row, head in owners(idx):
        start = (k * 4 + order.index(s)) * 48
        put(row, head, refs[e][start : start + 48, :])


UNITS = [(win, g) for win in range(4) for g in range(GROUPS)]


def window(win):
    return slice(win * SLOT, (win + 1) * SLOT)


def feats(g):
    return slice(g * 128, (g + 1) * 128)


def own_blocks(parts):
    rows = []
    for g in range(GROUPS):
        for h in range(PACK):
            rows.append(
                jnp.concatenate(
                    [
                        parts[win, g][
                            h * HEAD_DIM : (h + 1) * HEAD_DIM, h * SLOT : (h + 1) * SLOT
                        ]
                        for win in range(4)
                    ],
                    axis=1,
                )
            )
    return jnp.concatenate(rows, axis=0)


def pack_attention(qkv, out_t, first):
    first[...] = jnp.concatenate([qkv[0], qkv[1], qkv[2], out_t[...]], axis=1).astype(BF)


def pack_mlp(after, expand, contract_t, qv, eb, table_t, second, own):
    second[:, 0:WIDTH] = expand[...].astype(BF)
    second[:, WIDTH:] = contract_t[...].astype(BF)
    own[...] = jnp.zeros(own.shape, BF)
    own[0:2, 0:96] = qv[...].astype(BF)
    own[2:3, :] = eb[...].reshape(1, -1).astype(BF)
    own[3:6, 0 : table_t.shape[1]] = table_t[...].astype(BF)


def prepare(
    idx, after, tok, gout, crop, rows_c, cols_c, par_h,
    na, xt, ut, u, tokv, goutv, got, code_row, code_col, par, down, across,
):
    down[...] = onehot((128, 2 * SLOT), 0, rows_c[3:4, 0 : 2 * SLOT])
    across[...] = onehot((256, SLOT), 0, rows_c[4:5, 0:SLOT])
    tokv[...] = tok[...]
    goutv[...] = gout[...]
    par[...] = jnp.concatenate([par_h[...], jnp.zeros((2, WIDTH), F32)], axis=0)
    lane = lax.broadcasted_iota(jnp.int32, (4 * SLOT, 128), 1)
    ones = jnp.where(lane == 0, 1.0, 0.0).astype(BF)
    to_slots = []
    for turn in range(4):
        ut[turn] = onehot((4 * SLOT, SPAN), 1, cols_c[:, 0:1] + 4.0 * turn)
        u[turn] = onehot((SPAN, 4 * SLOT), 0, rows_c[0:1, :] + 4.0 * turn)
        to_slots.append(ut[turn])
    head = idx[2] * 2 + idx[3]
    for block in range(na.shape[0] // 4):
        hat, _ = stats(tok[block * QUAD_ROWS : (block + 1) * QUAD_ROWS, :].astype(F32))
        n1 = (hat * par_h[0:1, :] + par_h[1:2, :]).astype(BF)
        sides = jnp.concatenate([n1, hat.astype(BF)], axis=1)
        crops = crop[pl.ds(head * (na.shape[0] // 4) + block, 1), :] & 3
        for turn in range(4):
            step, start = 4 * block + turn, 192 * turn
            both = dot_nn(to_slots[turn], sides[start : start + SPAN]).astype(BF)
            na[step] = jnp.concatenate([both[:, 0:WIDTH], ones], axis=1)
            xt[step] = jnp.concatenate([both[:, WIDTH:], ones], axis=1).T[0:400, :]
            quad = crops[:, start : start + SPAN]
            quad = jnp.broadcast_to(quad.astype(F32), (8, SPAN)).astype(BF)
            code_row[step] = dot_nt(quad, to_slots[turn]) + rows_c[1:2, :]
            code_col[step] = dot_nt(to_slots[turn], quad) + cols_c[:, 1:2]
    got[...] = gout[...].T


def spread_small(idx, own, by_c, cols_c, across, tb, bias, eb, sbuf):
    x, c = idx[2], idx[3]
    for ref, dc in ((own, 0), (by_c, 1)):
        for dx in range(2):
            sbuf[(x ^ dx) * 2 + (c ^ dc)] = ref[16 * dx : 16 * (dx + 1), :].astype(F32)
    pad = jnp.zeros((1, WIDTH), F32)
    qv = [jnp.concatenate([sbuf[h, r : r + 1, 0:96] for h in range(4)], axis=1) for r in (0, 1)]
    bias[0:16, :] = jnp.concatenate(
        [jnp.concatenate([qv[0], pad, qv[1]], axis=1), jnp.zeros((15, 3 * WIDTH), F32)], axis=0
    ).astype(BF)
    eb[...] = jnp.concatenate(
        [
            jnp.concatenate([sbuf[h, 2:3, :] for h in range(4)], axis=1),
            jnp.zeros((15, HIDDEN), F32),
        ],
        axis=0,
    ).astype(BF)
    up = onehot((SLOT, 128), 1, cols_c[0:SLOT, 2:3])
    for g in range(GROUPS):
        blocks = []
        for h in range(g * PACK, (g + 1) * PACK):
            row = sbuf[h // 3, 3 + h % 3 : 4 + h % 3, 0:256]
            lines = pltpu.roll(
                jnp.broadcast_to(row, (128, 256)), 129, axis=1, stride=1, stride_axis=0
            )
            keyed = dot_nn(up, lines.astype(BF)).astype(BF)
            blocks.append(dot_nn(keyed, across[...]))
        tb[g] = jnp.concatenate(blocks, axis=1) * LOG2E


BATCH = 4


def canvas_start(step):
    return pl.multiple_of((step // 4) * QUAD_ROWS + (step % 4) * 192, 16)


def attention_forward(
    idx, mine, other, nas, codes_row, codes_col, u, bias, tb,
    mrg, qt, kt, vv, pt, mt, wnat, outt, wout,
    wbuf, waug, wt,
):
    def put(row, head, value):
        wbuf[head, pl.ds(row, 48), :] = value

    assemble(idx, (mine, other), put)
    for j in range(3):
        waug[0:WIDTH, j * WIDTH : (j + 1) * WIDTH] = jnp.concatenate(
            [wbuf[h, :, 96 * j : 96 * (j + 1)] for h in range(4)], axis=1
        )
    out_t = jnp.concatenate([wbuf[h, :, 288:384] for h in range(4)], axis=1)
    outt[...] = out_t
    wout[...] = out_t.T
    waug[WIDTH : WIDTH + 16, :] = bias[...]
    waug[WIDTH + 16 : 512, :] = jnp.zeros((112, 3 * WIDTH), BF)
    wnat[...] = waug[0:WIDTH, :]
    wt[...] = waug[...].T

    def canvases(batch, carry):
        steps = [batch * BATCH + i for i in range(BATCH)]
        units = [(i, w, g) for i in range(BATCH) for w, g in UNITS]
        all_t = [dot_nt(wt[...], nas[s]).astype(BF) for s in steps]
        kv = [dot_nt(nas[s], wt[WIDTH:, :]).astype(BF) for s in steps]
        masks = {}
        for i, s in enumerate(steps):
            for win in range(4):
                row = jnp.concatenate([codes_row[s, 0:1, window(win)]] * PACK, axis=1)
                masks[i, win] = jnp.where(codes_col[s, window(win), 0:1] == row, 0.0, MASKED)
        scores = {
            (i, w, g): dot_nn(kv[i][window(w), feats(g)], spread(all_t[i][feats(g), window(w)]))
            for i, w, g in units
        }
        probs = {}
        for i, w, g in units:
            sc = scores[i, w, g] * (SCALE * LOG2E) + (tb[g] + masks[i, w])
            grown = jnp.exp2(sc - jnp.max(sc, axis=0, keepdims=True))
            probs[i, w, g] = (grown * (1.0 / jnp.sum(grown, axis=0, keepdims=True))).astype(BF)
        mixed = {
            (i, w, g): dot_nn(all_t[i][2 * WIDTH :][feats(g), window(w)], probs[i, w, g])
            for i, w, g in units
        }
        for i, s in enumerate(steps):
            turn, start = s % 4, canvas_start(s)
            merged_t = own_blocks({(w, g): mixed[i, w, g] for w, g in UNITS}).astype(BF)
            back = dot_nt(u[turn], merged_t).astype(BF)
            for w, g in UNITS:
                pt[s, w * GROUPS + g] = probs[i, w, g]
            mt[s] = merged_t
            qt[s] = all_t[i][0:WIDTH]
            kt[s] = all_t[i][WIDTH : 2 * WIDTH]
            vv[s] = kv[i][:, WIDTH:]
            begin = pl.ds(start, 16)
            mrg[begin, :] = back[0:16] + jnp.where(
                turn == 0, jnp.zeros((16, WIDTH), BF), mrg[begin, :]
            )
            mrg[pl.ds(pl.multiple_of(start + 16, 16), SPAN - 16), :] = back[16:]
        return carry

    lax.fori_loop(0, nas.shape[0] // BATCH, canvases, 0)


TILE = 784


def mlp_begin(mrg, tok, outt, par, mid, n2, n2t):
    lane = lax.broadcasted_iota(jnp.int32, (TILE, 128), 1)
    ones = jnp.where(lane == 0, 1.0, 0.0).astype(BF)

    def head_rows(t, carry):
        rows = pl.ds(pl.multiple_of(t * TILE, 16), TILE)
        middle = tok[rows, :].astype(F32) + dot_nt(mrg[rows, :], outt[...]) + par[4:5, :]
        mid[rows, :] = middle
        hat, _ = stats(middle)
        n2[rows, 0:WIDTH] = (hat * par[2:3, :] + par[3:4, :]).astype(BF)
        n2[rows, WIDTH:512] = ones
        return carry

    lax.fori_loop(0, tok.shape[0] // TILE, head_rows, 0)
    n2t[...] = n2[...].T[0:400, :]


def mlp(
    idx, mine, other, n2, n2t, got, gout, eb,
    acc_m, acc_g, keep, send, ebg,
    eaug, ct, hid, gpr, cg, eg,
):

    def put(row, head, value):
        lanes = pl.ds(pl.multiple_of(head * WIDTH, 128), WIDTH)
        eaug[pl.ds(row, 48), lanes] = value[:, 0:WIDTH]
        ct[pl.ds(row, 48), lanes] = value[:, WIDTH:]

    assemble(idx, (mine, other), put, order=(0, 2, 1, 3))
    eaug[WIDTH : WIDTH + 16, :] = eb[...]
    eaug[WIDTH + 16 : 512, :] = jnp.zeros((112, HIDDEN), BF)
    acc_m[...] = jnp.zeros(acc_m.shape, F32)
    acc_g[...] = jnp.zeros(acc_g.shape, F32)

    def chunk(step, carry):
        cols = pl.ds(pl.multiple_of(step * CHUNK, 128), CHUNK)

        pre = dot_nn(n2[...], eaug[:, cols])
        grad_hidden = dot_nn(gout[...], ct[:, cols])
        phi = 0.5 + 0.5 * lax.erf(pre * ROOT_HALF)
        bell = jnp.exp2(pre * pre * (-0.5 * LOG2E)) * INV_ROOT_TWO_PI
        hidden = (pre * phi).astype(BF)
        grad_pre = (grad_hidden * (phi + pre * bell)).astype(BF)
        hid[...] = hidden
        gpr[...] = grad_pre
        acc_m[...] += dot_nt(hidden, ct[:, cols])
        acc_g[...] += dot_nt(grad_pre, eaug[0:WIDTH, cols])
        cg[:, cols] = dot_nn(got[...], hid[...]).astype(BF)
        grads = dot_nn(n2t[...], gpr[...])
        eg[:, cols] = grads[0:WIDTH].astype(BF)
        ebg[:, cols] = grads[WIDTH : WIDTH + 8]
        return carry

    lax.fori_loop(0, HIDDEN // CHUNK, chunk, 0)
    for e, k, s, row, head in owners(idx):
        dst = (keep, send)[e]
        lanes = pl.ds(pl.multiple_of(head * WIDTH, 128), WIDTH)
        base = (k * 4 + s) * 48
        dst[base : base + 48, 0:WIDTH] = eg[pl.ds(row, 48), lanes]
        dst[base : base + 48, WIDTH:] = cg[pl.ds(row, 48), lanes]


def mlp_end(mid, acc_m, acc_g, gout, par, blk, gmid, sums):
    def tail_rows(t, carry):
        rows = pl.ds(pl.multiple_of(t * TILE, 16), TILE)
        middle = mid[rows, :]
        blk[rows, :] = (middle + acc_m[rows, :] + par[5:6, :]).astype(BF)
        hat, inv = stats(middle)
        g = acc_g[rows, :]
        top = gout[rows, :].astype(F32)
        grad_mid = top + norm_back(g, hat, inv, par[2:3, :])
        gmid[rows, :] = grad_mid
        parts = (g * hat, g, grad_mid, top)
        return tuple(c + jnp.sum(p, axis=0, keepdims=True) for c, p in zip(carry, parts))

    zero = jnp.zeros((1, WIDTH), F32)
    totals = lax.fori_loop(0, mid.shape[0] // TILE, tail_rows, (zero,) * 4)
    sums[...] = jnp.concatenate([zero, zero, *totals, zero, zero], axis=0)


def attention_backward(
    idx, gmid, qt, kt, vv, pt, mt, xt, wout, ut, wnat, par, sums, ebg, down, across,
    keep, send, gta,
    ntall, wacc, oacc, table,
):
    table[...] = jnp.zeros(table.shape, F32)
    oacc[...] = jnp.zeros(oacc.shape, F32)
    wacc[...] = jnp.zeros(wacc.shape, F32)

    def rows_of(parts):
        return jnp.concatenate(
            [jnp.concatenate([parts[w, g] for w in range(4)], axis=1) for g in range(GROUPS)],
            axis=0,
        )

    def canvases(batch, carry):
        steps = [batch * BATCH + i for i in range(BATCH)]
        units = [(i, w, g) for i in range(BATCH) for w, g in UNITS]
        gmw = [
            dot_nn(ut[s % 4], gmid[pl.ds(canvas_start(s), SPAN), :].astype(BF)).astype(BF)
            for s in steps
        ]
        gmt = [dot_nt(wout[...], v).astype(BF) for v in gmw]
        gm_s = {(i, w, g): spread(gmt[i][feats(g), window(w)]) for i, w, g in units}
        gp = {
            (i, w, g): dot_nn(vv[steps[i], window(w), feats(g)], gm_s[i, w, g])
            for i, w, g in units
        }
        gs = {}
        for i, w, g in units:
            probs = pt[steps[i], w * GROUPS + g].astype(F32)
            delta = jnp.sum(probs * gp[i, w, g], axis=0, keepdims=True)
            gs[i, w, g] = (probs * (gp[i, w, g] - delta)).astype(BF)
        q_s = {(i, w, g): spread(qt[steps[i], feats(g), window(w)]) for i, w, g in units}
        gq = {
            (i, w, g): dot_nn(kt[steps[i], feats(g), window(w)], gs[i, w, g])
            for i, w, g in units
        }
        gk = {(i, w, g): dot_nt(q_s[i, w, g], gs[i, w, g]) for i, w, g in units}
        gv = {
            (i, w, g): dot_nt(gm_s[i, w, g], pt[steps[i], w * GROUPS + g]) for i, w, g in units
        }
        g_all = []
        for i in range(BATCH):
            parts = [{(w, g): v[i, w, g] for w, g in UNITS} for v in (gq, gk, gv)]
            g_all.append(
                jnp.concatenate(
                    [
                        (own_blocks(parts[0]) * SCALE).astype(BF),
                        (rows_of(parts[1]) * SCALE).astype(BF),
                        rows_of(parts[2]).astype(BF),
                    ],
                    axis=0,
                )
            )
            gta[steps[i]] = g_all[i]
        wacc[...] += dot_nt(
            jnp.concatenate([xt[s] for s in steps], axis=1), jnp.concatenate(g_all, axis=1)
        )
        oacc[...] += dot_nn(
            jnp.concatenate([mt[s] for s in steps], axis=1), jnp.concatenate(gmw, axis=0)
        )
        for g in range(GROUPS):
            table[g] += sum(gs[i, w, g].astype(F32) for i in range(BATCH) for w in range(4))
        return carry

    lax.fori_loop(0, qt.shape[0] // BATCH, canvases, 0)
    columns = par[...].T
    gain, offset = columns[:, 0:1], columns[:, 1:2]
    totals = wacc[WIDTH : WIDTH + 1, :]
    weights = wnat[...].astype(F32)
    gain_sum = jnp.sum(weights * wacc[0:WIDTH, :], axis=1, keepdims=True)
    offset_sum = jnp.sum(weights * totals, axis=1, keepdims=True)
    norm_rows = jnp.concatenate([gain_sum, offset_sum, jnp.zeros((WIDTH, 6), F32)], axis=1).T
    grads = wacc[0:WIDTH, :] * gain + offset * totals
    out_t = oacc[...].T
    for h in range(4):
        pieces = [grads[:, j * WIDTH + 96 * h : j * WIDTH + 96 * (h + 1)] for j in range(3)]
        pieces.append(out_t[:, 96 * h : 96 * (h + 1)])
        ntall[h] = jnp.concatenate(pieces, axis=1).astype(BF)
    for e, k, s, row, head in owners(idx):
        base = (k * 4 + s) * 48
        (keep, send)[e][base : base + 48, :] = ntall[head, pl.ds(row, 48), :]
    rows = [norm_rows[0:2, :], sums[2:6, :], totals[:, 0:WIDTH], totals[:, 2 * WIDTH :]]
    rows += [ebg[0:1, j * WIDTH : (j + 1) * WIDTH] for j in range(4)]
    for g in range(GROUPS):
        high = table[g].astype(BF)
        low = (table[g] - high.astype(F32)).astype(BF)
        both = jnp.concatenate([high, low], axis=0)
        for h in range(PACK):
            spaced = dot_nt(both[:, h * SLOT : (h + 1) * SLOT], across[...]).astype(BF)
            lines = dot_nn(down[...], spaced)
            lines = pltpu.roll(lines, 0, axis=1, stride=1, stride_axis=0)
            row = jnp.sum(lines, axis=0, keepdims=True)
            rows.append(jnp.concatenate([row, jnp.zeros((1, 128), F32)], axis=1))
    rows.append(jnp.zeros((8, WIDTH), F32))
    small = jnp.concatenate(rows, axis=0).astype(BF)
    keep[768:800, :] = small
    send[768:800, :] = small


def tokens_end(tok, gmid, gta, wnat, u, par, *refs):
    state, (gtok, *near) = refs[: len(refs) // 2], refs[len(refs) // 2 :]
    for source, target in zip(state, near):
        target[...] = source[...]

    def block_rows(block, carry):
        ends = [
            dot_nt(u[turn], gta[4 * block + turn]).astype(BF) for turn in range(4)
        ]
        pieces = [ends[0][0:192]]
        for turn in range(1, 4):
            pieces += [ends[turn - 1][192:] + ends[turn][0:16], ends[turn][16:192]]
        g1 = dot_nt(jnp.concatenate([*pieces, ends[3][192:]], axis=0), wnat[...])
        rows = pl.ds(pl.multiple_of(block * QUAD_ROWS, 16), QUAD_ROWS)
        hat, inv = stats(tok[rows, :].astype(F32))
        gtok[rows, :] = gmid[rows, :] + norm_back(g1, hat, inv, par[0:1, :])
        return carry

    lax.fori_loop(0, gta.shape[0] // 4, block_rows, 0)


def plane_sum(keep, got, *refs):
    small = None
    if len(refs) > 4:
        small = keep[768:, :].astype(F32) + got[768:, :].astype(F32)
        refs[4][...] = small
    for k in range(4):
        block = slice(k * 192, (k + 1) * 192)
        value = keep[block, :].astype(F32) + got[block, :].astype(F32)
        if k == 0:
            refs[0][...] = value
        else:
            refs[k][0:192, :] = value.astype(BF)
            if small is not None:
                refs[k][192:, :] = small.astype(BF)


def line_sum(own, r1, r2, r3, mine, *refs):
    parts = (r1, r2, r3)
    small = mine[...] + sum(r[192:, :].astype(F32) for r in parts)
    refs[4][...] = small
    for s in range(4):
        block = slice(s * 48, (s + 1) * 48)
        value = own[block, :] + sum(r[block, :].astype(F32) for r in parts)
        if s == 0:
            refs[0][...] = value
        else:
            refs[s][0:48, :] = value.astype(BF)
            refs[s][48:, :] = small.astype(BF)


def half_sum(own, *refs):
    parts, (keep, send) = refs[:-2], refs[-2:]
    half = own.shape[0] // 2
    total = own[...] + sum(r[...].astype(F32) for r in parts)
    keep[...] = total[0:half]
    send[...] = total[half:].astype(BF)


def adamw(master, grad, moment, square, step_rate, decay_rate):
    moment_new = BETA_ONE * moment + (1.0 - BETA_ONE) * grad
    square_new = BETA_TWO * square + (1.0 - BETA_TWO) * grad * grad
    moment_hat = moment_new * (1.0 / (1.0 - BETA_ONE**STEP))
    square_hat = square_new * (1.0 / (1.0 - BETA_TWO**STEP))
    step = moment_hat / (jnp.sqrt(square_hat) + ADAM_EPS)
    if decay_rate:
        step = step + decay_rate * master
    return master - step_rate * step, moment_new, square_new


def update(refs, grad, outs, step_rate, decay_rate, at=...):
    master, moment, square = (r[at] for r in refs)
    news = adamw(master, grad, moment, square, step_rate, decay_rate)
    for out, new in zip(outs, news):
        out[at] = new


def step_all(n_mlp, n_parts, rows, idx, *refs):
    parts, refs = refs[:n_mlp], refs[n_mlp:]
    total = sum(r[...].astype(F32) for r in parts)
    parts, refs = refs[:n_parts], refs[n_parts:]
    half = (len(refs) - 1) // 2
    small, ins, outs = refs[0], refs[1 : half + 1], refs[half + 1 :]
    update(ins[0:3], total[:, 0:WIDTH], outs[0:3], RATE_MATRIX, DECAY_MATRIX)
    update(ins[3:6], total[:, WIDTH:], outs[3:6], RATE_MATRIX, DECAY_MATRIX)
    ins, outs = ins[6:], outs[6:]
    total = sum(r[0:rows, :].astype(F32) for r in parts)
    small = small[...] + sum(r[rows:, :].astype(F32) for r in parts[1:])
    head = idx[2] * 2 + idx[3]

    def pick(blocks):
        return sum(jnp.where(head == h, block, 0.0) for h, block in enumerate(blocks))

    for j in range(3):
        update(
            ins[0:3], total[:, 96 * j : 96 * (j + 1)], outs[0:3], RATE_MATRIX, DECAY_MATRIX, at=j
        )
    update(ins[3:6], total[:, 288:384], outs[3:6], RATE_MATRIX, DECAY_MATRIX)
    qv = pick([small[6:8, 96 * h : 96 * (h + 1)] for h in range(4)])
    update(ins[6:9], qv, outs[6:9], RATE_SMALL, 0.0)
    eb = pick([small[8 + h : 9 + h, :] for h in range(4)])
    update(ins[9:12], eb.reshape(ins[9].shape), outs[9:12], RATE_SMALL, 0.0)
    table_rows = ins[12].shape[1]
    table = pick([small[12 + 3 * h : 15 + 3 * h, 0:table_rows] for h in range(4)])
    update(ins[12:15], table, outs[12:15], RATE_SMALL, 0.0)
    update(ins[15:18], small[0:6, :], outs[15:18], RATE_SMALL, 0.0)


class Links:
    def __init__(self, sizes):
        self.sizes = sizes
        self.outer = sizes["dp"] // 8

    def perm(self, z=0, y=0, x=0, c=0):
        pairs = []
        for flat in range(self.sizes["dp"] * self.sizes["head"]):
            head, dp = flat % 4, flat // 4
            inner, place = dp // self.outer, dp % self.outer
            inner ^= z * 2 + y
            pairs.append((flat, (inner * self.outer + place) * 4 + (head ^ (x * 2 + c))))
        return pairs

    def send(self, value, **flips):
        return lax.ppermute(value, ("dp", "head"), self.perm(**flips))

    def groups(self):
        return [[i * self.outer + j for j in range(self.outer)] for i in range(8)]

    def outer_gather(self, shard):
        if self.outer > 1:
            shard = lax.all_gather(
                shard, "dp", axis=0, tiled=True, axis_index_groups=self.groups()
            )
        return shard

    def gather_line(self, shard):
        return jnp.concatenate([shard] + [self.send(shard, z=s) for s in range(1, 4)], axis=0)

    def gather_plane(self, line):
        return [line] + [self.send(line, x=k & 1, y=k >> 1) for k in range(1, 4)]

    def gather_core(self, plane):
        plane = jnp.concatenate(plane, axis=0)
        return plane, self.send(plane, c=1)

    def to_plane(self, blocks):
        return [self.send(b, x=k & 1, y=k >> 1) for k, b in enumerate(blocks, 1)]

    def to_line(self, blocks):
        return [self.send(b, z=s) for s, b in enumerate(blocks, 1)]

    def outer_sum(self, value):
        if self.outer > 1:
            value = lax.psum_scatter(
                value, "dp", scatter_dimension=0, tiled=True, axis_index_groups=self.groups()
            )
        return value


SMEM = pl.BlockSpec(memory_space=pltpu.SMEM)
VMEM = pl.BlockSpec(memory_space=pltpu.VMEM)


class Far:
    def __init__(self, value):
        self.value = value


def placed(arg):
    if isinstance(arg, Far):
        return pltpu.with_memory_space_constraint(arg.value, pltpu.HBM)
    return pltpu.with_memory_space_constraint(arg, pltpu.VMEM)


def call(kernel, outs, *args, scratch=(), limit=16, scalars=None, far=(), time=1):
    lead = [] if scalars is None else [scalars]
    name = getattr(kernel, "__name__", None) or kernel.func.__name__
    return pl.pallas_call(
        kernel,
        in_specs=[SMEM] * len(lead) + [VMEM] * len(args),
        out_specs=[VMEM] * len(outs),
        out_shape=[(pltpu.HBM if i in far else pltpu.VMEM)(s, d) for i, (s, d) in enumerate(outs)],
        scratch_shapes=[pltpu.VMEM(s, d) for s, d in scratch],
        compiler_params=pltpu.CompilerParams(vmem_limit_bytes=limit * 2**20),
        cost_estimate=pl.CostEstimate(
            flops=int(time * 1.15e9), bytes_accessed=0, transcendentals=0
        ),
        name=name,
    )(*lead, *(placed(a) for a in args))


def per_device(links, *args):
    (
        tokens, crop_ids, grad_out, qkv_w, out_w, exp_w, con_w, qv_b, exp_b, table_w, norm_p,
        qkv_m, qkv_s, out_m, out_s, exp_m, exp_s, con_m, con_s,
        qv_m, qv_s, eb_m, eb_s, tab_m, tab_s, norm_m, norm_s,
    ) = args
    rows_all = tokens.shape[0]
    canvases = rows_all // CANVAS
    head = lax.axis_index("head")
    dp = lax.axis_index("dp") // links.outer
    idx = jnp.stack([dp // 2, dp % 2, head // 2, head % 2]).astype(jnp.int32)
    slots = 4 * SLOT
    wide = (rows_all, WIDTH)
    square = (WIDTH, WIDTH)
    fm = (canvases, WIDTH, slots)
    tm = (canvases, slots, WIDTH)

    rows_own = exp_w.shape[0]
    (first,) = call(
        pack_attention, [((rows_own, WIDTH), BF)], Far(qkv_w), Far(out_w.T),
    )
    second, own = call(
        pack_mlp, [((rows_own, 2 * WIDTH), BF), ((16, WIDTH), BF)],
        first[0:1, 0:128], Far(exp_w), Far(con_w.T), Far(qv_b), Far(exp_b), Far(table_w.T),
    )
    first = links.outer_gather(first)
    line = links.gather_line(first)
    second = links.outer_gather(second)
    pair_s = jnp.concatenate([second, links.send(second, z=2)], axis=0)
    own = jnp.concatenate([own, links.send(own, x=1)], axis=0)
    line, pair_s, own = lax.optimization_barrier((line, pair_s, own))
    plane = links.gather_plane(line)
    by_c = links.send(own, c=1)
    by_c, pair_s = lax.optimization_barrier((by_c, pair_s))
    line_s = jnp.concatenate([pair_s, links.send(pair_s, z=1)], axis=0)
    crop_rows = crop_ids.reshape(-1, QUAD_ROWS)
    rows_c, cols_c = (jnp.asarray(t) for t in tables())
    to_slots = (4, slots, SPAN)
    nas, xt, ut, u, tok, gout, got, code_row, code_col, par, down, across = call(
        prepare,
        [
            ((canvases, slots, 512), BF), ((canvases, 400, slots), BF), (to_slots, BF),
            ((4, SPAN, slots), BF), (wide, BF), (wide, BF), ((WIDTH, rows_all), BF),
            ((canvases, 8, slots), F32), ((canvases, slots, 8), F32), ((8, WIDTH), F32),
            ((128, 2 * SLOT), BF), ((256, SLOT), BF),
        ],
        by_c, Far(tokens), Far(grad_out), Far(crop_rows), Far(rows_c), Far(cols_c),
        Far(norm_p), limit=16, scalars=idx, time=4,
    )
    bias_t, bias16, eb16 = call(
        spread_small, [((GROUPS, SLOT, slots), F32), ((16, 3 * WIDTH), BF), ((16, HIDDEN), BF)],
        own, by_c, Far(cols_c), across, scratch=[((4, 16, WIDTH), F32)], scalars=idx,
    )
    *plane, line_s, bias_t = lax.optimization_barrier((*plane, line_s, bias_t))
    plane_s = links.gather_plane(line_s)
    firsts = list(links.gather_core(plane))
    merged, qt, kt, vv, pt, mt, wnat, outt, wout = call(
        attention_forward,
        [
            (wide, BF), (fm, BF), (fm, BF), (tm, BF), ((canvases, 12, SLOT, slots), BF), (fm, BF),
            ((WIDTH, 3 * WIDTH), BF), (square, BF), (square, BF),
        ],
        *firsts, nas, code_row, code_col, u, bias16, bias_t,
        scratch=[
            ((4, WIDTH, WIDTH), BF), ((512, 3 * WIDTH), BF), ((3 * WIDTH, 512), BF),
        ],
        limit=20, scalars=idx, time=11,
    )
    merged, *plane_s = lax.optimization_barrier((merged, *plane_s))
    seconds = links.gather_core(plane_s)
    middle, n2, n2t = call(
        mlp_begin, [(wide, F32), ((rows_all, 512), BF), ((400, rows_all), BF)],
        merged, tok, outt, par, time=3,
    )
    acc_m, acc_g, keep_r, send_r, eb_grad = call(
        mlp,
        [
            (wide, F32), (wide, F32), ((768, 2 * WIDTH), BF), ((768, 2 * WIDTH), BF),
            ((8, HIDDEN), F32),
        ],
        *seconds, n2, n2t, got, gout, eb16,
        scratch=[
            ((512, HIDDEN), BF), ((WIDTH, HIDDEN), BF), ((rows_all, CHUNK), BF),
            ((rows_all, CHUNK), BF), ((WIDTH, HIDDEN), BF), ((WIDTH, HIDDEN), BF),
        ],
        limit=34, scalars=idx, time=17,
    )
    got_r = links.send(send_r, c=1)
    block_out, grad_mid, sums = call(
        mlp_end, [(wide, BF), (wide, F32), ((8, WIDTH), F32)], middle, acc_m, acc_g, gout, par,
        limit=16, far=(0,), time=3,
    )
    block_r = [((192, 2 * WIDTH), F32)] + [((192, 2 * WIDTH), BF)] * 3
    got_r, grad_mid = lax.optimization_barrier((got_r, grad_mid))
    own_r, *blocks_r = call(plane_sum, block_r, keep_r, got_r)
    grad_mid, *blocks_r = lax.optimization_barrier((grad_mid, *blocks_r))
    plane_r = links.to_plane(blocks_r)
    keep_q, send_q, g_all = call(
        attention_backward,
        [((800, WIDTH), BF), ((800, WIDTH), BF), ((canvases, 3 * WIDTH, slots), BF)],
        grad_mid, qt, kt, vv, pt, mt, xt, wout, ut, wnat, par, sums, eb_grad, down, across,
        scratch=[
            ((4, WIDTH, WIDTH), BF), ((400, 3 * WIDTH), F32), (square, F32),
            ((GROUPS, SLOT, slots), F32),
        ],
        limit=24, scalars=idx, time=15,
    )
    *plane_r, send_q = lax.optimization_barrier((*plane_r, send_q))
    got_q = links.send(send_q, c=1)
    own_r, block_r = call(
        half_sum, [((96, 2 * WIDTH), F32), ((96, 2 * WIDTH), BF)], own_r, *plane_r,
    )
    got_q, block_r = lax.optimization_barrier((got_q, block_r))
    block_q = [((192, WIDTH), F32)] + [((224, WIDTH), BF)] * 3 + [((32, WIDTH), F32)]
    own_q, *blocks_q, small = call(plane_sum, block_q, keep_q, got_q)
    plane_q = links.to_plane(blocks_q)
    got_r = links.send(block_r, z=2)
    g_all = lax.optimization_barrier((g_all, *blocks_q))[0]
    state = [
        exp_w, exp_m, exp_s, con_w.T, con_m.T, con_s.T, qkv_w, qkv_m, qkv_s, out_w.T, out_m.T,
        out_s.T, qv_b, qv_m, qv_s, exp_b, eb_m, eb_s, table_w.T, tab_m.T, tab_s.T, norm_p, norm_m,
        norm_s,
    ]
    grad_tokens, *near = call(
        tokens_end, [(wide, F32)] + [(a.shape, F32) for a in state],
        tok, grad_mid, g_all, wnat, u, par, *(Far(a) for a in state), far=(0,), time=5,
    )
    *plane_q, got_r, grad_tokens = lax.optimization_barrier((*plane_q, got_r, grad_tokens))
    line_q = [((48, WIDTH), F32)] + [((80, WIDTH), BF)] * 3 + [((32, WIDTH), F32)]
    own_q, *blocks_q, small = call(line_sum, line_q, own_q, *plane_q, small)
    parts_q = [own_q, *links.to_line(blocks_q)]
    own_r, block_r = call(
        half_sum, [((48, 2 * WIDTH), F32), ((48, 2 * WIDTH), BF)], own_r, got_r,
    )
    parts_r = [own_r, links.send(block_r, z=1)]
    rows = 48
    if links.outer > 1:
        small = small + sum(p[48:].astype(F32) for p in parts_q[1:])
        small = lax.psum(small, "dp", axis_index_groups=links.groups())
        parts_q = [links.outer_sum(sum(p[:48].astype(F32) for p in parts_q))]
        parts_r = [links.outer_sum(sum(p.astype(F32) for p in parts_r))]
        rows = parts_q[0].shape[0]
    news = call(
        functools.partial(step_all, len(parts_r), len(parts_q), rows),
        [(a.shape, F32) for a in state], *parts_r, *parts_q, small, *near, scalars=idx,
        far=range(len(state)), time=2,
    )
    third, fourth = news[0:6], news[6:]
    return (
        block_out, grad_tokens, *fourth[0:3], *(a.T for a in fourth[3:6]), *third[0:3],
        *(a.T for a in third[3:6]), *fourth[6:12], *(a.T for a in fourth[12:15]), *fourth[15:],
    )


def solution(mesh):
    tokens = P(("dp", "head"), None)
    qkv, rows_head, rows_dp = P(None, "dp", "head"), P("head", "dp"), P("dp", "head")
    pair, unit, none = P(None, "head"), P("head"), P()
    matrices = (qkv, rows_head, rows_dp, rows_head)
    small = (pair, unit, pair, none)
    in_specs = (tokens, P("dp"), tokens, *matrices, *small)
    in_specs += tuple(s for spec in (*matrices, *small) for s in (spec, spec))
    out_specs = (tokens, tokens) + tuple(
        s for spec in (*matrices, *small) for s in (spec, spec, spec)
    )
    return jax.shard_map(
        functools.partial(per_device, Links(dict(mesh.shape))),
        mesh=mesh, in_specs=in_specs, out_specs=out_specs, check_vma=False,
    )
```

```python
import functools
import math

import jax
import jax.numpy as jnp
import numpy as np
from jax import lax
from jax.experimental import pallas as pl
from jax.experimental.pallas import tpu as pltpu
from jax.sharding import PartitionSpec as P

HEAD_DIM = 32
WINDOW = 7
SIDE = 14
SHIFT = 3
STEP = 10
CANVAS = SIDE * SIDE
PLACES = WINDOW * WINDOW
SLOT = 64
QUAD_ROWS = 4 * CANVAS
SPAN = 208
WIDTH = 384
GROUPS = 3
PACK = 4
HIDDEN = 1536
CHUNK = 512

NORM_EPS = 1e-05
BETA_ONE = 0.9
BETA_TWO = 0.999
ADAM_EPS = 1e-08
RATE_MATRIX = 0.1
RATE_SMALL = 0.5
DECAY_MATRIX = 0.05
MASKED = -1e30
LOG2E = math.log2(math.e)
SCALE = HEAD_DIM**-0.5
ROOT_HALF = 0.7071067811865476
INV_ROOT_TWO_PI = 1.0 / 2.5066282746310002
BF = jnp.bfloat16
F32 = jnp.float32


def slot_rows():
    rows = -np.ones((4, SLOT), np.int64)
    for win in range(4):
        for place in range(PLACES):
            row = (win // 2) * WINDOW + place // WINDOW
            col = (win % 2) * WINDOW + place % WINDOW
            rows[win, place] = ((row + SHIFT) % SIDE) * SIDE + (col + SHIFT) % SIDE
    return rows.reshape(-1)


def region_codes():
    def band(v):
        return 0 if v < SIDE - WINDOW else (1 if v < SIDE - SHIFT else 2)

    codes = np.full((4, SLOT), 999.0, np.float32)
    for win in range(4):
        for place in range(PLACES):
            row = (win // 2) * WINDOW + place // WINDOW
            col = (win % 2) * WINDOW + place % WINDOW
            codes[win, place] = 4 * (3 * band(row) + band(col))
    return codes.reshape(-1)


def tables():
    line = np.array([13 * (p // WINDOW) + p % WINDOW for p in range(PLACES)], np.float32)
    out = np.full((8, 4 * SLOT), -1000.0, np.float32)
    out[0] = slot_rows()
    out[0][out[0] < 0] = -1000.0
    out[1] = region_codes()
    out[2, :PLACES] = 43 + line
    out[3, :PLACES] = out[3, SLOT : SLOT + PLACES] = 84 - line
    out[4, :PLACES] = line
    return out, out.T.copy()


def onehot(shape, axis, places):
    index = lax.broadcasted_iota(jnp.int32, shape, axis).astype(F32)
    return jnp.where(index == places, 1.0, 0.0).astype(BF)


def dot_nn(a, b):
    return jnp.dot(a, b, preferred_element_type=F32)


def dot_nt(a, b):
    return lax.dot_general(a, b, (((1,), (1,)), ((), ())), preferred_element_type=F32)


def stats(values):
    centred = values - jnp.mean(values, axis=-1, keepdims=True)
    inv_std = lax.rsqrt(jnp.mean(centred * centred, axis=-1, keepdims=True) + NORM_EPS)
    return centred * inv_std, inv_std


def norm_back(grad_norm, hat, inv_std, gain_row):
    grad_hat = grad_norm * gain_row
    inner = grad_hat - jnp.mean(grad_hat, axis=-1, keepdims=True)
    return inv_std * (inner - hat * jnp.mean(grad_hat * hat, axis=-1, keepdims=True))


def owners(idx):
    z, y, x, c = idx[0], idx[1], idx[2], idx[3]
    for e in range(2):
        for k in range(4):
            for s in range(4):
                row = ((z ^ s) * 2 + (y ^ (k >> 1))) * 48
                yield e, k, s, pl.multiple_of(row, 16), (x ^ (k & 1)) * 2 + (c ^ e)


def spread(block):
    four = jnp.concatenate([block] * PACK, axis=1)
    rows = lax.broadcasted_iota(jnp.int32, four.shape, 0) // HEAD_DIM
    lanes = lax.broadcasted_iota(jnp.int32, four.shape, 1) // SLOT
    return jnp.where(rows == lanes, four, jnp.zeros_like(four))


def assemble(idx, refs, put, order=(0, 1, 2, 3)):
    for e, k, s, row, head in owners(idx):
        start = (k * 4 + order.index(s)) * 48
        put(row, head, refs[e][start : start + 48, :])


UNITS = [(win, g) for win in range(4) for g in range(GROUPS)]


def window(win):
    return slice(win * SLOT, (win + 1) * SLOT)


def feats(g):
    return slice(g * 128, (g + 1) * 128)


def own_blocks(parts):
    rows = []
    for g in range(GROUPS):
        for h in range(PACK):
            rows.append(
                jnp.concatenate(
                    [
                        parts[win, g][
                            h * HEAD_DIM : (h + 1) * HEAD_DIM, h * SLOT : (h + 1) * SLOT
                        ]
                        for win in range(4)
                    ],
                    axis=1,
                )
            )
    return jnp.concatenate(rows, axis=0)


def pack(qkv, out_t, expand, contract_t, qv, eb, table_t, first, second, own):
    first[...] = jnp.concatenate([qkv[0], qkv[1], qkv[2], out_t[...]], axis=1).astype(BF)
    second[:, 0:WIDTH] = expand[...].astype(BF)
    second[:, WIDTH:] = contract_t[...].astype(BF)
    own[...] = jnp.zeros(own.shape, BF)
    own[0:2, 0:96] = qv[...].astype(BF)
    own[2:3, :] = eb[...].reshape(1, -1).astype(BF)
    own[3:6, 0 : table_t.shape[1]] = table_t[...].astype(BF)


def prepare(
    idx, after, tok, gout, crop, rows_c, cols_c, par_h,
    na, xt, ut, u, tokv, goutv, got, code_row, code_col, par, down, across,
):
    down[...] = onehot((128, 2 * SLOT), 0, rows_c[3:4, 0 : 2 * SLOT])
    across[...] = onehot((256, SLOT), 0, rows_c[4:5, 0:SLOT])
    tokv[...] = tok[...]
    goutv[...] = gout[...]
    par[...] = jnp.concatenate([par_h[...], jnp.zeros((2, WIDTH), F32)], axis=0)
    lane = lax.broadcasted_iota(jnp.int32, (4 * SLOT, 128), 1)
    ones = jnp.where(lane == 0, 1.0, 0.0).astype(BF)
    to_slots = []
    for turn in range(4):
        ut[turn] = onehot((4 * SLOT, SPAN), 1, cols_c[:, 0:1] + 4.0 * turn)
        u[turn] = onehot((SPAN, 4 * SLOT), 0, rows_c[0:1, :] + 4.0 * turn)
        to_slots.append(ut[turn])
    head = idx[2] * 2 + idx[3]
    for block in range(na.shape[0] // 4):
        hat, _ = stats(tok[block * QUAD_ROWS : (block + 1) * QUAD_ROWS, :].astype(F32))
        n1 = (hat * par_h[0:1, :] + par_h[1:2, :]).astype(BF)
        sides = jnp.concatenate([n1, hat.astype(BF)], axis=1)
        crops = crop[pl.ds(head * (na.shape[0] // 4) + block, 1), :] & 3
        for turn in range(4):
            step, start = 4 * block + turn, 192 * turn
            both = dot_nn(to_slots[turn], sides[start : start + SPAN]).astype(BF)
            na[step] = jnp.concatenate([both[:, 0:WIDTH], ones], axis=1)
            xt[step] = jnp.concatenate([both[:, WIDTH:], ones], axis=1).T[0:400, :]
            quad = crops[:, start : start + SPAN]
            quad = jnp.broadcast_to(quad.astype(F32), (8, SPAN)).astype(BF)
            code_row[step] = dot_nt(quad, to_slots[turn]) + rows_c[1:2, :]
            code_col[step] = dot_nt(to_slots[turn], quad) + cols_c[:, 1:2]
    got[...] = gout[...].T


def spread_small(idx, own, by_c, cols_c, across, tb, bias, eb, sbuf):
    x, c = idx[2], idx[3]
    for ref, dc in ((own, 0), (by_c, 1)):
        for dx in range(2):
            sbuf[(x ^ dx) * 2 + (c ^ dc)] = ref[16 * dx : 16 * (dx + 1), :].astype(F32)
    pad = jnp.zeros((1, WIDTH), F32)
    qv = [jnp.concatenate([sbuf[h, r : r + 1, 0:96] for h in range(4)], axis=1) for r in (0, 1)]
    bias[0:16, :] = jnp.concatenate(
        [jnp.concatenate([qv[0], pad, qv[1]], axis=1), jnp.zeros((15, 3 * WIDTH), F32)], axis=0
    ).astype(BF)
    eb[...] = jnp.concatenate(
        [
            jnp.concatenate([sbuf[h, 2:3, :] for h in range(4)], axis=1),
            jnp.zeros((15, HIDDEN), F32),
        ],
        axis=0,
    ).astype(BF)
    up = onehot((SLOT, 128), 1, cols_c[0:SLOT, 2:3])
    for g in range(GROUPS):
        blocks = []
        for h in range(g * PACK, (g + 1) * PACK):
            row = sbuf[h // 3, 3 + h % 3 : 4 + h % 3, 0:256]
            lines = pltpu.roll(
                jnp.broadcast_to(row, (128, 256)), 129, axis=1, stride=1, stride_axis=0
            )
            keyed = dot_nn(up, lines.astype(BF)).astype(BF)
            blocks.append(dot_nn(keyed, across[...]))
        tb[g] = jnp.concatenate(blocks, axis=1) * LOG2E


BATCH = 4


def canvas_start(step):
    return pl.multiple_of((step // 4) * QUAD_ROWS + (step % 4) * 192, 16)


def attention_forward(
    idx, mine, other, nas, codes_row, codes_col, u, bias, tb,
    mrg, qt, kt, vv, pt, mt, wnat, outt, wout,
    wbuf, waug, wt,
):
    def put(row, head, value):
        wbuf[head, pl.ds(row, 48), :] = value

    assemble(idx, (mine, other), put)
    for j in range(3):
        waug[0:WIDTH, j * WIDTH : (j + 1) * WIDTH] = jnp.concatenate(
            [wbuf[h, :, 96 * j : 96 * (j + 1)] for h in range(4)], axis=1
        )
    out_t = jnp.concatenate([wbuf[h, :, 288:384] for h in range(4)], axis=1)
    outt[...] = out_t
    wout[...] = out_t.T
    waug[WIDTH : WIDTH + 16, :] = bias[...]
    waug[WIDTH + 16 : 512, :] = jnp.zeros((112, 3 * WIDTH), BF)
    wnat[...] = waug[0:WIDTH, :]
    wt[...] = waug[...].T

    def canvases(batch, carry):
        steps = [batch * BATCH + i for i in range(BATCH)]
        units = [(i, w, g) for i in range(BATCH) for w, g in UNITS]
        all_t = [dot_nt(wt[...], nas[s]).astype(BF) for s in steps]
        kv = [dot_nt(nas[s], wt[WIDTH:, :]).astype(BF) for s in steps]
        masks = {}
        for i, s in enumerate(steps):
            for win in range(4):
                row = jnp.concatenate([codes_row[s, 0:1, window(win)]] * PACK, axis=1)
                masks[i, win] = jnp.where(codes_col[s, window(win), 0:1] == row, 0.0, MASKED)
        scores = {
            (i, w, g): dot_nn(kv[i][window(w), feats(g)], spread(all_t[i][feats(g), window(w)]))
            for i, w, g in units
        }
        probs = {}
        for i, w, g in units:
            sc = scores[i, w, g] * (SCALE * LOG2E) + (tb[g] + masks[i, w])
            grown = jnp.exp2(sc - jnp.max(sc, axis=0, keepdims=True))
            probs[i, w, g] = (grown * (1.0 / jnp.sum(grown, axis=0, keepdims=True))).astype(BF)
        mixed = {
            (i, w, g): dot_nn(all_t[i][2 * WIDTH :][feats(g), window(w)], probs[i, w, g])
            for i, w, g in units
        }
        for i, s in enumerate(steps):
            turn, start = s % 4, canvas_start(s)
            merged_t = own_blocks({(w, g): mixed[i, w, g] for w, g in UNITS}).astype(BF)
            back = dot_nt(u[turn], merged_t).astype(BF)
            for w, g in UNITS:
                pt[s, w * GROUPS + g] = probs[i, w, g]
            mt[s] = merged_t
            qt[s] = all_t[i][0:WIDTH]
            kt[s] = all_t[i][WIDTH : 2 * WIDTH]
            vv[s] = kv[i][:, WIDTH:]
            begin = pl.ds(start, 16)
            mrg[begin, :] = back[0:16] + jnp.where(
                turn == 0, jnp.zeros((16, WIDTH), BF), mrg[begin, :]
            )
            mrg[pl.ds(pl.multiple_of(start + 16, 16), SPAN - 16), :] = back[16:]
        return carry

    lax.fori_loop(0, nas.shape[0] // BATCH, canvases, 0)


TILE = 784


def mlp_begin(mrg, tok, outt, par, mid, n2, n2t):
    lane = lax.broadcasted_iota(jnp.int32, (TILE, 128), 1)
    ones = jnp.where(lane == 0, 1.0, 0.0).astype(BF)

    def head_rows(t, carry):
        rows = pl.ds(pl.multiple_of(t * TILE, 16), TILE)
        middle = tok[rows, :].astype(F32) + dot_nt(mrg[rows, :], outt[...]) + par[4:5, :]
        mid[rows, :] = middle
        hat, _ = stats(middle)
        n2[rows, 0:WIDTH] = (hat * par[2:3, :] + par[3:4, :]).astype(BF)
        n2[rows, WIDTH:512] = ones
        return carry

    lax.fori_loop(0, tok.shape[0] // TILE, head_rows, 0)
    n2t[...] = n2[...].T[0:400, :]


HALF = 2 * WIDTH


def mlp_half(other, idx, weights, n2, n2t, got, gout, eb, *refs):
    if other:
        before_m, before_g, before_eb, *refs = refs
        acc_m, acc_g, grads_out, rows_out, *refs = refs
    else:
        acc_m, acc_g, grads_out, ebg, *refs = refs
    eaug, ct, hid, gpr, cg, eg, *refs = refs
    core = idx[3] ^ 1 if other else idx[3]
    for e, k, s, row, head in owners(idx):
        if e == 0:
            start = (k * 4 + (0, 2, 1, 3).index(s)) * 48
            lanes = pl.ds(pl.multiple_of((idx[2] ^ (k & 1)) * WIDTH, 128), WIDTH)
            eaug[pl.ds(row, 48), lanes] = weights[start : start + 48, 0:WIDTH]
            ct[pl.ds(row, 48), lanes] = weights[start : start + 48, WIDTH:]
    for x in range(2):
        lanes = pl.ds(pl.multiple_of((2 * x + core) * WIDTH, 128), WIDTH)
        eaug[WIDTH : WIDTH + 16, x * WIDTH : (x + 1) * WIDTH] = eb[:, lanes]
    eaug[WIDTH + 16 : 512, :] = jnp.zeros((112, HALF), BF)
    pre = dot_nn(n2[...], eaug[...])
    grad_hidden = dot_nn(gout[...], ct[...])
    phi = 0.5 + 0.5 * lax.erf(pre * ROOT_HALF)
    bell = jnp.exp2(pre * pre * (-0.5 * LOG2E)) * INV_ROOT_TWO_PI
    hidden = (pre * phi).astype(BF)
    grad_pre = (grad_hidden * (phi + pre * bell)).astype(BF)
    hid[...] = hidden
    gpr[...] = grad_pre
    if other:
        acc_m[...] = before_m[...] + dot_nt(hidden, ct[...])
        acc_g[...] = before_g[...] + dot_nt(grad_pre, eaug[0:WIDTH, :])
    else:
        acc_m[...] = dot_nt(hidden, ct[...])
        acc_g[...] = dot_nt(grad_pre, eaug[0:WIDTH, :])
    cg[...] = dot_nn(got[...], hid[...]).astype(BF)
    grads = dot_nn(n2t[...], gpr[...])
    eg[...] = grads[0:WIDTH].astype(BF)
    if not other:
        ebg[...] = grads[WIDTH : WIDTH + 8]
    for e, k, s, row, head in owners(idx):
        if e == 0:
            lanes = pl.ds(pl.multiple_of((idx[2] ^ (k & 1)) * WIDTH, 128), WIDTH)
            base = (k * 4 + s) * 48
            grads_out[base : base + 48, 0:WIDTH] = eg[pl.ds(row, 48), lanes]
            grads_out[base : base + 48, WIDTH:] = cg[pl.ds(row, 48), lanes]
    if other:
        (small,) = refs
        small[...] = jnp.zeros(small.shape, F32)
        for x in range(2):
            block = slice(x * WIDTH, (x + 1) * WIDTH)
            for place, part in ((core, grads[WIDTH : WIDTH + 1]), (idx[3], before_eb[0:1, :])):
                lanes = pl.ds(pl.multiple_of(place * WIDTH, 128), WIDTH)
                small[x : x + 1, lanes] = part[:, block]
        rows_out[...] = small[...].astype(BF)
        grads_out[768:784, :] = small[...].astype(BF)


def mlp_end(mid, acc_m, acc_g, gout, par, blk, gmid, sums):
    def tail_rows(t, carry):
        rows = pl.ds(pl.multiple_of(t * TILE, 16), TILE)
        middle = mid[rows, :]
        blk[rows, :] = (middle + acc_m[rows, :] + par[5:6, :]).astype(BF)
        hat, inv = stats(middle)
        g = acc_g[rows, :]
        top = gout[rows, :].astype(F32)
        grad_mid = top + norm_back(g, hat, inv, par[2:3, :])
        gmid[rows, :] = grad_mid
        parts = (g * hat, g, grad_mid, top)
        return tuple(c + jnp.sum(p, axis=0, keepdims=True) for c, p in zip(carry, parts))

    zero = jnp.zeros((1, WIDTH), F32)
    totals = lax.fori_loop(0, mid.shape[0] // TILE, tail_rows, (zero,) * 4)
    sums[...] = jnp.concatenate([zero, zero, *totals, zero, zero], axis=0)


def small_rows(wacc, table, wnat, sums, down, across, small):
    totals = wacc[WIDTH : WIDTH + 1, :]
    weights = wnat[...].astype(F32)
    gain_sum = jnp.sum(weights * wacc[0:WIDTH, :], axis=1, keepdims=True)
    offset_sum = jnp.sum(weights * totals, axis=1, keepdims=True)
    norm_rows = jnp.concatenate([gain_sum, offset_sum, jnp.zeros((WIDTH, 6), F32)], axis=1).T
    rows = [norm_rows[0:2, :], sums[2:6, :], totals[:, 0:WIDTH], totals[:, 2 * WIDTH :]]
    lines = []
    for g in range(GROUPS):
        high = table[g].astype(BF)
        low = (table[g] - high.astype(F32)).astype(BF)
        both = jnp.concatenate([high, low], axis=0)
        for h in range(PACK):
            spaced = dot_nt(both[:, h * SLOT : (h + 1) * SLOT], across[...]).astype(BF)
            shifted = pltpu.roll(dot_nn(down[...], spaced), 0, axis=1, stride=1, stride_axis=0)
            lines.append(jnp.sum(shifted, axis=0, keepdims=True)[:, 0:192])
    rows += [jnp.concatenate(lines[2 * i : 2 * i + 2], axis=1) for i in range(6)]
    rows.append(jnp.zeros((2, WIDTH), F32))
    small[...] = jnp.concatenate(rows, axis=0).astype(BF)


def attention_backward(
    n_state, idx, gmid, qt, kt, vv, pt, mt, xt, wout, ut, par, wnat, sums, down, across, *refs
):
    state, (keep, send, gta, small, *refs) = refs[:n_state], refs[n_state:]
    near, (ntall, oacc, wacc, table, arrived) = refs[:n_state], refs[n_state:]
    copies = [
        pltpu.make_async_copy(source, target, arrived.at[i])
        for i, (source, target) in enumerate(zip(state, near))
    ]
    for copy in copies:
        copy.start()
    table[...] = jnp.zeros(table.shape, F32)
    oacc[...] = jnp.zeros(oacc.shape, F32)
    wacc[...] = jnp.zeros(wacc.shape, F32)

    def rows_of(parts):
        return jnp.concatenate(
            [jnp.concatenate([parts[w, g] for w in range(4)], axis=1) for g in range(GROUPS)],
            axis=0,
        )

    def canvases(batch, carry):
        steps = [batch * BATCH + i for i in range(BATCH)]
        units = [(i, w, g) for i in range(BATCH) for w, g in UNITS]
        gmw = [
            dot_nn(ut[s % 4], gmid[pl.ds(canvas_start(s), SPAN), :].astype(BF)).astype(BF)
            for s in steps
        ]
        gmt = [dot_nt(wout[...], v).astype(BF) for v in gmw]
        gm_s = {(i, w, g): spread(gmt[i][feats(g), window(w)]) for i, w, g in units}
        gp = {
            (i, w, g): dot_nn(vv[steps[i], window(w), feats(g)], gm_s[i, w, g])
            for i, w, g in units
        }
        gs = {}
        for i, w, g in units:
            probs = pt[steps[i], w * GROUPS + g].astype(F32)
            delta = jnp.sum(probs * gp[i, w, g], axis=0, keepdims=True)
            gs[i, w, g] = (probs * (gp[i, w, g] - delta)).astype(BF)
        q_s = {(i, w, g): spread(qt[steps[i], feats(g), window(w)]) for i, w, g in units}
        gq = {
            (i, w, g): dot_nn(kt[steps[i], feats(g), window(w)], gs[i, w, g])
            for i, w, g in units
        }
        gk = {(i, w, g): dot_nt(q_s[i, w, g], gs[i, w, g]) for i, w, g in units}
        gv = {
            (i, w, g): dot_nt(gm_s[i, w, g], pt[steps[i], w * GROUPS + g]) for i, w, g in units
        }
        g_all = []
        for i in range(BATCH):
            parts = [{(w, g): v[i, w, g] for w, g in UNITS} for v in (gq, gk, gv)]
            g_all.append(
                jnp.concatenate(
                    [
                        (own_blocks(parts[0]) * SCALE).astype(BF),
                        (rows_of(parts[1]) * SCALE).astype(BF),
                        rows_of(parts[2]).astype(BF),
                    ],
                    axis=0,
                )
            )
            gta[steps[i]] = g_all[i]
        wacc[...] += dot_nt(
            jnp.concatenate([xt[s] for s in steps], axis=1), jnp.concatenate(g_all, axis=1)
        )
        oacc[...] += dot_nn(
            jnp.concatenate([mt[s] for s in steps], axis=1), jnp.concatenate(gmw, axis=0)
        )
        for g in range(GROUPS):
            table[g] += sum(gs[i, w, g].astype(F32) for i in range(BATCH) for w in range(4))
        return carry

    lax.fori_loop(0, qt.shape[0] // BATCH, canvases, 0)
    columns = par[...].T
    grads = wacc[0:WIDTH, :] * columns[:, 0:1] + columns[:, 1:2] * wacc[WIDTH : WIDTH + 1, :]
    out_t = oacc[...].T
    for h in range(4):
        pieces = [grads[:, j * WIDTH + 96 * h : j * WIDTH + 96 * (h + 1)] for j in range(3)]
        pieces.append(out_t[:, 96 * h : 96 * (h + 1)])
        ntall[h] = jnp.concatenate(pieces, axis=1).astype(BF)
    for e, k, s, row, head in owners(idx):
        base = (k * 4 + s) * 48
        (keep, send)[e][base : base + 48, :] = ntall[head, pl.ds(row, 48), :]
    small_rows(wacc, table, wnat, sums, down, across, small)
    send[768:784, :] = small[...]
    for copy in copies:
        copy.wait()


def tokens_end(tok, gmid, gta, wnat, u, par, gtok):

    def block_rows(block, carry):
        ends = [
            dot_nt(u[turn], gta[4 * block + turn]).astype(BF) for turn in range(4)
        ]
        pieces = [ends[0][0:192]]
        for turn in range(1, 4):
            pieces += [ends[turn - 1][192:] + ends[turn][0:16], ends[turn][16:192]]
        g1 = dot_nt(jnp.concatenate([*pieces, ends[3][192:]], axis=0), wnat[...])
        rows = pl.ds(pl.multiple_of(block * QUAD_ROWS, 16), QUAD_ROWS)
        hat, inv = stats(tok[rows, :].astype(F32))
        gtok[rows, :] = gmid[rows, :] + norm_back(g1, hat, inv, par[0:1, :])
        return carry

    lax.fori_loop(0, gta.shape[0] // 4, block_rows, 0)


def join(*refs):
    parts, out = refs[:-1], refs[-1]
    start = 0
    for part in parts:
        out[start : start + part.shape[0], :] = part[...]
        start += part.shape[0]


def plane_sum(keep, got, mine, theirs, own, send1, send2, send3, rest):
    small = mine[...].astype(F32) + theirs[...].astype(F32)
    rest[...] = small
    for k, ref in enumerate((own, send1, send2, send3)):
        block = slice(k * 192, (k + 1) * 192)
        value = keep[block, :].astype(F32) + got[block, :].astype(F32)
        ref[0:192, :] = value.astype(ref.dtype)
        if k:
            ref[192:, :] = small.astype(BF)


def line_sum(own, r1, r2, r3, mine, *refs):
    parts = (r1, r2, r3)
    small = mine[...] + sum(r[192:, :].astype(F32) for r in parts)
    refs[4][...] = small
    for s in range(4):
        block = slice(s * 48, (s + 1) * 48)
        value = own[block, :] + sum(r[block, :].astype(F32) for r in parts)
        if s == 0:
            refs[0][...] = value
        else:
            refs[s][0:48, :] = value.astype(BF)
            refs[s][48:, :] = small.astype(BF)


def half_sum(own, mine, *refs):
    parts, (keep, send, rest) = refs[:-3], refs[-3:]
    rows = own.shape[0]
    half = rows // 2
    total = own[...] + sum(r[0:rows, :].astype(F32) for r in parts)
    small = mine[...] + sum(r[rows:, :].astype(F32) for r in parts)
    keep[...] = total[0:half]
    send[0:half, :] = total[half:].astype(BF)
    send[half:, :] = small.astype(BF)
    rest[...] = small


def adamw(master, grad, moment, square, step_rate, decay_rate):
    moment_new = BETA_ONE * moment + (1.0 - BETA_ONE) * grad
    square_new = BETA_TWO * square + (1.0 - BETA_TWO) * grad * grad
    moment_hat = moment_new * (1.0 / (1.0 - BETA_ONE**STEP))
    square_hat = square_new * (1.0 / (1.0 - BETA_TWO**STEP))
    step = moment_hat / (jnp.sqrt(square_hat) + ADAM_EPS)
    if decay_rate:
        step = step + decay_rate * master
    return master - step_rate * step, moment_new, square_new


def update(refs, grad, outs, step_rate, decay_rate, at=...):
    master, moment, square = (r[at] for r in refs)
    news = adamw(master, grad, moment, square, step_rate, decay_rate)
    for out, new in zip(outs, news):
        out[at] = new


def step_all(n_mlp, n_parts, rows, idx, *refs):
    parts, refs = refs[:n_mlp], refs[n_mlp:]
    total = sum(r[0:rows, :].astype(F32) for r in parts)
    rest = parts[1:]
    parts, refs = refs[:n_parts], refs[n_parts:]
    half = (len(refs) - 2) // 2
    rest = refs[0][...] + sum(r[rows:, :].astype(F32) for r in rest)
    small, ins, outs = refs[1], refs[2 : half + 2], refs[half + 2 :]
    update(ins[0:3], total[:, 0:WIDTH], outs[0:3], RATE_MATRIX, DECAY_MATRIX)
    update(ins[3:6], total[:, WIDTH:], outs[3:6], RATE_MATRIX, DECAY_MATRIX)
    ins, outs = ins[6:], outs[6:]
    total = sum(r[0:rows, :].astype(F32) for r in parts)
    small = small[...] + sum(r[rows:, :].astype(F32) for r in parts[1:])
    head = idx[2] * 2 + idx[3]

    def pick(blocks):
        return sum(jnp.where(head == h, block, 0.0) for h, block in enumerate(blocks))

    for j in range(3):
        update(
            ins[0:3], total[:, 96 * j : 96 * (j + 1)], outs[0:3], RATE_MATRIX, DECAY_MATRIX, at=j
        )
    update(ins[3:6], total[:, 288:384], outs[3:6], RATE_MATRIX, DECAY_MATRIX)
    qv = pick([small[6:8, 96 * h : 96 * (h + 1)] for h in range(4)])
    update(ins[6:9], qv, outs[6:9], RATE_SMALL, 0.0)
    eb = pick([rest[h // 2 : h // 2 + 1, WIDTH * (h % 2) : WIDTH * (h % 2 + 1)] for h in range(4)])
    update(ins[9:12], eb.reshape(ins[9].shape), outs[9:12], RATE_SMALL, 0.0)
    table_rows = ins[12].shape[1]
    lines = [
        small[8 + n // 2 : 9 + n // 2, 192 * (n % 2) : 192 * (n % 2) + table_rows]
        for n in range(12)
    ]
    table = pick([jnp.concatenate(lines[3 * h : 3 * h + 3], axis=0) for h in range(4)])
    update(ins[12:15], table, outs[12:15], RATE_SMALL, 0.0)
    update(ins[15:18], small[0:6, :], outs[15:18], RATE_SMALL, 0.0)


class Links:
    def __init__(self, sizes):
        self.sizes = sizes
        self.outer = sizes["dp"] // 8

    def perm(self, z=0, y=0, x=0, c=0):
        pairs = []
        for flat in range(self.sizes["dp"] * self.sizes["head"]):
            head, dp = flat % 4, flat // 4
            inner, place = dp // self.outer, dp % self.outer
            inner ^= z * 2 + y
            pairs.append((flat, (inner * self.outer + place) * 4 + (head ^ (x * 2 + c))))
        return pairs

    def send(self, value, **flips):
        return lax.ppermute(value, ("dp", "head"), self.perm(**flips))

    def groups(self):
        return [[i * self.outer + j for j in range(self.outer)] for i in range(8)]

    def outer_gather(self, shard):
        if self.outer > 1:
            shard = lax.all_gather(
                shard, "dp", axis=0, tiled=True, axis_index_groups=self.groups()
            )
        return shard

    def gather_line(self, shard):
        return jnp.concatenate([shard] + [self.send(shard, z=s) for s in range(1, 4)], axis=0)

    def gather_plane(self, line):
        return [line] + [self.send(line, x=k & 1, y=k >> 1) for k in range(1, 4)]

    def gather_core(self, plane):
        rows = sum(p.shape[0] for p in plane)
        (plane,) = call(join, [((rows, plane[0].shape[1]), BF)], *plane)
        return plane, self.send(plane, c=1)

    def to_plane(self, blocks):
        return [self.send(b, x=k & 1, y=k >> 1) for k, b in enumerate(blocks, 1)]

    def to_line(self, blocks):
        return [self.send(b, z=s) for s, b in enumerate(blocks, 1)]

    def outer_sum(self, value):
        if self.outer > 1:
            value = lax.psum_scatter(
                value, "dp", scatter_dimension=0, tiled=True, axis_index_groups=self.groups()
            )
        return value


SMEM = pl.BlockSpec(memory_space=pltpu.SMEM)
VMEM = pl.BlockSpec(memory_space=pltpu.VMEM)
HBM = pl.BlockSpec(memory_space=pltpu.HBM)


class Far:
    def __init__(self, value, pinned=False):
        self.value, self.pinned = value, pinned


def placed(arg):
    if isinstance(arg, Far):
        return pltpu.with_memory_space_constraint(arg.value, pltpu.HBM)
    return pltpu.with_memory_space_constraint(arg, pltpu.VMEM)


def call(kernel, outs, *args, scratch=(), limit=10, scalars=None, far=(), time=1, same=()):
    lead = [] if scalars is None else [scalars]
    name = getattr(kernel, "__name__", None) or kernel.func.__name__
    return pl.pallas_call(
        kernel,
        in_specs=[SMEM] * len(lead)
        + [HBM if isinstance(a, Far) and a.pinned else VMEM for a in args],
        out_specs=[VMEM] * len(outs),
        out_shape=[(pltpu.HBM if i in far else pltpu.VMEM)(s, d) for i, (s, d) in enumerate(outs)],
        scratch_shapes=[
            pltpu.SemaphoreType.DMA((s,)) if isinstance(s, int) else pltpu.VMEM(*s)
            for s in scratch
        ],
        compiler_params=pltpu.CompilerParams(vmem_limit_bytes=limit * 2**20),
        cost_estimate=pl.CostEstimate(
            flops=int(time * 1.15e9), bytes_accessed=0, transcendentals=0
        ),
        input_output_aliases={i + len(lead): o for i, o in same},
        name=name,
    )(*lead, *(placed(a) for a in args))


def per_device(links, *args):
    (
        tokens, crop_ids, grad_out, qkv_w, out_w, exp_w, con_w, qv_b, exp_b, table_w, norm_p,
        qkv_m, qkv_s, out_m, out_s, exp_m, exp_s, con_m, con_s,
        qv_m, qv_s, eb_m, eb_s, tab_m, tab_s, norm_m, norm_s,
    ) = args
    rows_all = tokens.shape[0]
    canvases = rows_all // CANVAS
    head = lax.axis_index("head")
    dp = lax.axis_index("dp") // links.outer
    idx = jnp.stack([dp // 2, dp % 2, head // 2, head % 2]).astype(jnp.int32)
    slots = 4 * SLOT
    wide = (rows_all, WIDTH)
    square = (WIDTH, WIDTH)
    fm = (canvases, WIDTH, slots)
    tm = (canvases, slots, WIDTH)

    rows_own = exp_w.shape[0]
    first, second, own = call(
        pack,
        [((rows_own, WIDTH), BF), ((rows_own, 2 * WIDTH), BF), ((16, WIDTH), BF)],
        Far(qkv_w), Far(out_w.T), Far(exp_w), Far(con_w.T), Far(qv_b), Far(exp_b), Far(table_w.T),
    )
    first = links.outer_gather(first)
    line = links.gather_line(first)
    second = links.outer_gather(second)
    pair_s = jnp.concatenate([second, links.send(second, z=2)], axis=0)
    own = jnp.concatenate([own, links.send(own, x=1)], axis=0)
    line, own = lax.optimization_barrier((line, own))
    plane = links.gather_plane(line)
    by_c = links.send(own, c=1)
    crop_rows, _ = lax.optimization_barrier((crop_ids, line))
    crop_rows = crop_rows.reshape(-1, QUAD_ROWS)
    pair_s, crop_rows = lax.optimization_barrier((pair_s, crop_rows))
    line_s = jnp.concatenate([pair_s, links.send(pair_s, z=1)], axis=0)
    rows_c, cols_c = (jnp.asarray(t) for t in tables())
    to_slots = (4, slots, SPAN)
    nas, xt, ut, u, tok, gout, got, code_row, code_col, par, down, across = call(
        prepare,
        [
            ((canvases, slots, 512), BF), ((canvases, 400, slots), BF), (to_slots, BF),
            ((4, SPAN, slots), BF), (wide, BF), (wide, BF), ((WIDTH, rows_all), BF),
            ((canvases, 8, slots), F32), ((canvases, slots, 8), F32), ((8, WIDTH), F32),
            ((128, 2 * SLOT), BF), ((256, SLOT), BF),
        ],
        own, Far(tokens), Far(grad_out), Far(crop_rows), Far(rows_c), Far(cols_c),
        Far(norm_p), limit=12, scalars=idx, time=4,
    )
    by_c, nas = lax.optimization_barrier((by_c, nas))
    bias_t, bias16, eb16 = call(
        spread_small, [((GROUPS, SLOT, slots), F32), ((16, 3 * WIDTH), BF), ((16, HIDDEN), BF)],
        own, by_c, Far(cols_c), across, scratch=[((4, 16, WIDTH), F32)], scalars=idx, time=2,
    )
    *plane, line_s, bias_t = lax.optimization_barrier((*plane, line_s, bias_t))
    plane_s = links.gather_plane(line_s)
    firsts = links.gather_core(plane)
    merged, qt, kt, vv, pt, mt, wnat, outt, wout = call(
        attention_forward,
        [
            (wide, BF), (fm, BF), (fm, BF), (tm, BF), ((canvases, 12, SLOT, slots), BF), (fm, BF),
            ((WIDTH, 3 * WIDTH), BF), (square, BF), (square, BF),
        ],
        *firsts, nas, code_row, code_col, u, bias16, bias_t,
        scratch=[
            ((4, WIDTH, WIDTH), BF), ((512, 3 * WIDTH), BF), ((3 * WIDTH, 512), BF),
        ],
        limit=14, scalars=idx, time=11,
    )
    middle, n2, n2t = call(
        mlp_begin, [(wide, F32), ((rows_all, 512), BF), ((400, rows_all), BF)],
        merged, tok, outt, par, time=3,
    )
    n2, *plane_s = lax.optimization_barrier((n2, *plane_s))
    seconds = links.gather_core(plane_s)
    scratch = [
        ((512, HALF), BF), ((WIDTH, HALF), BF), ((rows_all, HALF), BF), ((rows_all, HALF), BF),
        ((WIDTH, HALF), BF), ((WIDTH, HALF), BF),
    ]
    acc_m, acc_g, keep_r, eb_grad = call(
        functools.partial(mlp_half, False),
        [(wide, F32), (wide, F32), ((768, HALF), BF), ((8, HALF), F32)],
        seconds[0], n2, n2t, got, gout, eb16, scratch=scratch, limit=17, scalars=idx, time=9,
    )
    acc_m, other_s = lax.optimization_barrier((acc_m, seconds[1]))
    acc_m, acc_g, send_r, rest = call(
        functools.partial(mlp_half, True),
        [(wide, F32), (wide, F32), ((784, HALF), BF), ((16, HALF), BF)],
        other_s, n2, n2t, got, gout, eb16, acc_m, acc_g, eb_grad,
        scratch=scratch + [((16, HALF), F32)], limit=17, scalars=idx, time=9, same=((6, 0), (7, 1)),
    )
    got_r = links.send(send_r, c=1)
    block_out, grad_mid, sums = call(
        mlp_end, [(wide, BF), (wide, F32), ((8, WIDTH), F32)], middle, acc_m, acc_g, gout, par,
        limit=10, far=(0,), time=3,
    )
    wide_r = 2 * WIDTH
    block_r = [((192, wide_r), F32)] + [((208, wide_r), BF)] * 3 + [((16, wide_r), F32)]
    got_r, grad_mid = lax.optimization_barrier((got_r, grad_mid))
    own_r, *blocks_r, rest = call(
        plane_sum, block_r, keep_r, got_r, rest, got_r[768:]
    )
    grad_mid, *blocks_r = lax.optimization_barrier((grad_mid, *blocks_r))
    plane_r = links.to_plane(blocks_r)
    state = [
        exp_w, exp_m, exp_s, con_w.T, con_m.T, con_s.T, qkv_w, qkv_m, qkv_s, out_w.T, out_m.T,
        out_s.T, qv_b, qv_m, qv_s, exp_b, eb_m, eb_s, table_w.T, tab_m.T, tab_s.T, norm_p, norm_m,
        norm_s,
    ]
    keep_q, send_q, g_all, small, *near = call(
        functools.partial(attention_backward, len(state)),
        [
            ((768, WIDTH), BF), ((784, WIDTH), BF), ((canvases, 3 * WIDTH, slots), BF),
            ((16, WIDTH), BF),
        ]
        + [(a.shape, F32) for a in state],
        grad_mid, qt, kt, vv, pt, mt, xt, wout, ut, par, wnat, sums, down, across,
        *(Far(a, pinned=True) for a in state),
        scratch=[
            ((4, WIDTH, WIDTH), BF), (square, F32), ((400, 3 * WIDTH), F32),
            ((GROUPS, SLOT, slots), F32), len(state),
        ],
        limit=20, scalars=idx, time=15,
    )
    *plane_r, send_q = lax.optimization_barrier((*plane_r, send_q))
    got_q = links.send(send_q, c=1)
    own_r, block_r, rest = call(
        half_sum, [((96, wide_r), F32), ((112, wide_r), BF), ((16, wide_r), F32)],
        own_r, rest, *plane_r,
    )
    block_q = [((192, WIDTH), F32)] + [((208, WIDTH), BF)] * 3 + [((16, WIDTH), F32)]
    own_q, *blocks_q, small = call(plane_sum, block_q, keep_q, got_q, small, got_q[768:])
    plane_q = links.to_plane(blocks_q)
    got_r = links.send(block_r, z=2)
    g_all = lax.optimization_barrier((g_all, *blocks_q))[0]
    (grad_tokens,) = call(
        tokens_end, [(wide, F32)], tok, grad_mid, g_all, wnat, u, par, far=(0,), time=6,
    )
    got_r, grad_tokens = lax.optimization_barrier((got_r, grad_tokens))
    own_r, block_r, rest = call(
        half_sum, [((48, wide_r), F32), ((64, wide_r), BF), ((16, wide_r), F32)],
        own_r, rest, got_r,
    )
    line_q = [((48, WIDTH), F32)] + [((64, WIDTH), BF)] * 3 + [((16, WIDTH), F32)]
    own_q, *blocks_q, small = call(line_sum, line_q, own_q, *plane_q, small)
    parts_q = [own_q, *links.to_line(blocks_q)]
    parts_r = [own_r, links.send(block_r, z=1)]
    rows = 48
    if links.outer > 1:
        small = small + sum(p[48:].astype(F32) for p in parts_q[1:])
        rest = rest + parts_r[1][48:].astype(F32)
        small, rest = lax.psum((small, rest), "dp", axis_index_groups=links.groups())
        parts_q = [links.outer_sum(sum(p[:48].astype(F32) for p in parts_q))]
        parts_r = [links.outer_sum(sum(p[:48].astype(F32) for p in parts_r))]
        rows = parts_q[0].shape[0]
    news = call(
        functools.partial(step_all, len(parts_r), len(parts_q), rows),
        [(a.shape, F32) for a in state], *parts_r, *parts_q, rest, small, *near, scalars=idx,
        far=range(len(state)), time=2,
    )
    third, fourth = news[0:6], news[6:]
    return (
        block_out, grad_tokens, *fourth[0:3], *(a.T for a in fourth[3:6]), *third[0:3],
        *(a.T for a in third[3:6]), *fourth[6:12], *(a.T for a in fourth[12:15]), *fourth[15:],
    )


def solution(mesh):
    tokens = P(("dp", "head"), None)
    qkv, rows_head, rows_dp = P(None, "dp", "head"), P("head", "dp"), P("dp", "head")
    pair, unit, none = P(None, "head"), P("head"), P()
    matrices = (qkv, rows_head, rows_dp, rows_head)
    small = (pair, unit, pair, none)
    in_specs = (tokens, P("dp"), tokens, *matrices, *small)
    in_specs += tuple(s for spec in (*matrices, *small) for s in (spec, spec))
    out_specs = (tokens, tokens) + tuple(
        s for spec in (*matrices, *small) for s in (spec, spec, spec)
    )
    return jax.shard_map(
        functools.partial(per_device, Links(dict(mesh.shape))),
        mesh=mesh, in_specs=in_specs, out_specs=out_specs, check_vma=False,
    )
```

```python
import functools
import math

import jax
import jax.numpy as jnp
import numpy as np
from jax import lax
from jax.experimental import pallas as pl
from jax.experimental.pallas import tpu as pltpu
from jax.sharding import PartitionSpec as P

HEAD_DIM = 32
WINDOW = 7
SIDE = 14
SHIFT = 3
STEP = 10
CANVAS = SIDE * SIDE
PLACES = WINDOW * WINDOW
SLOT = 64
QUAD_ROWS = 4 * CANVAS
SPAN = 208
WIDTH = 384
GROUPS = 3
PACK = 4
HIDDEN = 1536
CHUNK = 512

NORM_EPS = 1e-05
BETA_ONE = 0.9
BETA_TWO = 0.999
ADAM_EPS = 1e-08
RATE_MATRIX = 0.1
RATE_SMALL = 0.5
DECAY_MATRIX = 0.05
MASKED = -1e30
LOG2E = math.log2(math.e)
SCALE = HEAD_DIM**-0.5
ROOT_HALF = 0.7071067811865476
INV_ROOT_TWO_PI = 1.0 / 2.5066282746310002
BF = jnp.bfloat16
F32 = jnp.float32


def slot_rows():
    rows = -np.ones((4, SLOT), np.int64)
    for win in range(4):
        for place in range(PLACES):
            row = (win // 2) * WINDOW + place // WINDOW
            col = (win % 2) * WINDOW + place % WINDOW
            rows[win, place] = ((row + SHIFT) % SIDE) * SIDE + (col + SHIFT) % SIDE
    return rows.reshape(-1)


def region_codes():
    def band(v):
        return 0 if v < SIDE - WINDOW else (1 if v < SIDE - SHIFT else 2)

    codes = np.full((4, SLOT), 999.0, np.float32)
    for win in range(4):
        for place in range(PLACES):
            row = (win // 2) * WINDOW + place // WINDOW
            col = (win % 2) * WINDOW + place % WINDOW
            codes[win, place] = 4 * (3 * band(row) + band(col))
    return codes.reshape(-1)


def tables():
    line = np.array([13 * (p // WINDOW) + p % WINDOW for p in range(PLACES)], np.float32)
    out = np.full((8, 4 * SLOT), -1000.0, np.float32)
    out[0] = slot_rows()
    out[0][out[0] < 0] = -1000.0
    out[1] = region_codes()
    out[2, :PLACES] = 43 + line
    out[3, :PLACES] = out[3, SLOT : SLOT + PLACES] = 84 - line
    out[4, :PLACES] = line
    return out, out.T.copy()


def onehot(shape, axis, places):
    index = lax.broadcasted_iota(jnp.int32, shape, axis).astype(F32)
    return jnp.where(index == places, 1.0, 0.0).astype(BF)


def dot_nn(a, b):
    return jnp.dot(a, b, preferred_element_type=F32)


def dot_nt(a, b):
    return lax.dot_general(a, b, (((1,), (1,)), ((), ())), preferred_element_type=F32)


def stats(values):
    centred = values - jnp.mean(values, axis=-1, keepdims=True)
    inv_std = lax.rsqrt(jnp.mean(centred * centred, axis=-1, keepdims=True) + NORM_EPS)
    return centred * inv_std, inv_std


def norm_back(grad_norm, hat, inv_std, gain_row):
    grad_hat = grad_norm * gain_row
    inner = grad_hat - jnp.mean(grad_hat, axis=-1, keepdims=True)
    return inv_std * (inner - hat * jnp.mean(grad_hat * hat, axis=-1, keepdims=True))


def owners(idx):
    z, y, x, c = idx[0], idx[1], idx[2], idx[3]
    for e in range(2):
        for k in range(4):
            for s in range(4):
                row = ((z ^ s) * 2 + (y ^ (k >> 1))) * 48
                yield e, k, s, pl.multiple_of(row, 16), (x ^ (k & 1)) * 2 + (c ^ e)


def spread(block):
    four = jnp.concatenate([block] * PACK, axis=1)
    rows = lax.broadcasted_iota(jnp.int32, four.shape, 0) // HEAD_DIM
    lanes = lax.broadcasted_iota(jnp.int32, four.shape, 1) // SLOT
    return jnp.where(rows == lanes, four, jnp.zeros_like(four))


def assemble(idx, refs, put, order=(0, 1, 2, 3)):
    for e, k, s, row, head in owners(idx):
        start = (k * 4 + order.index(s)) * 48
        put(row, head, refs[e][start : start + 48, :])


UNITS = [(win, g) for win in range(4) for g in range(GROUPS)]


def window(win):
    return slice(win * SLOT, (win + 1) * SLOT)


def feats(g):
    return slice(g * 128, (g + 1) * 128)


def own_blocks(parts):
    rows = []
    for g in range(GROUPS):
        for h in range(PACK):
            rows.append(
                jnp.concatenate(
                    [
                        parts[win, g][
                            h * HEAD_DIM : (h + 1) * HEAD_DIM, h * SLOT : (h + 1) * SLOT
                        ]
                        for win in range(4)
                    ],
                    axis=1,
                )
            )
    return jnp.concatenate(rows, axis=0)


def pack(qkv, out_t, expand, contract_t, qv, eb, table_t, first, second, own):
    first[...] = jnp.concatenate([qkv[0], qkv[1], qkv[2], out_t[...]], axis=1).astype(BF)
    second[:, 0:WIDTH] = expand[...].astype(BF)
    second[:, WIDTH:] = contract_t[...].astype(BF)
    own[...] = jnp.zeros(own.shape, BF)
    own[0:2, 0:96] = qv[...].astype(BF)
    own[2:3, :] = eb[...].reshape(1, -1).astype(BF)
    own[3:6, 0 : table_t.shape[1]] = table_t[...].astype(BF)


def prepare(
    idx, after, tok, gout, crop, rows_c, cols_c, par_h,
    na, xt, ut, u, tokv, goutv, got, code_row, code_col, par, down, across,
):
    down[...] = onehot((128, 2 * SLOT), 0, rows_c[3:4, 0 : 2 * SLOT])
    across[...] = onehot((256, SLOT), 0, rows_c[4:5, 0:SLOT])
    tokv[...] = tok[...]
    goutv[...] = gout[...]
    par[...] = jnp.concatenate([par_h[...], jnp.zeros((2, WIDTH), F32)], axis=0)
    lane = lax.broadcasted_iota(jnp.int32, (4 * SLOT, 128), 1)
    ones = jnp.where(lane == 0, 1.0, 0.0).astype(BF)
    to_slots = []
    for turn in range(4):
        ut[turn] = onehot((4 * SLOT, SPAN), 1, cols_c[:, 0:1] + 4.0 * turn)
        u[turn] = onehot((SPAN, 4 * SLOT), 0, rows_c[0:1, :] + 4.0 * turn)
        to_slots.append(ut[turn])
    head = idx[2] * 2 + idx[3]
    for block in range(na.shape[0] // 4):
        hat, _ = stats(tok[block * QUAD_ROWS : (block + 1) * QUAD_ROWS, :].astype(F32))
        n1 = (hat * par_h[0:1, :] + par_h[1:2, :]).astype(BF)
        sides = jnp.concatenate([n1, hat.astype(BF)], axis=1)
        crops = crop[pl.ds(head * (na.shape[0] // 4) + block, 1), :] & 3
        for turn in range(4):
            step, start = 4 * block + turn, 192 * turn
            both = dot_nn(to_slots[turn], sides[start : start + SPAN]).astype(BF)
            na[step] = jnp.concatenate([both[:, 0:WIDTH], ones], axis=1)
            xt[step] = jnp.concatenate([both[:, WIDTH:], ones], axis=1).T[0:400, :]
            quad = crops[:, start : start + SPAN]
            quad = jnp.broadcast_to(quad.astype(F32), (8, SPAN)).astype(BF)
            code_row[step] = dot_nt(quad, to_slots[turn]) + rows_c[1:2, :]
            code_col[step] = dot_nt(to_slots[turn], quad) + cols_c[:, 1:2]
    got[...] = gout[...].T


def spread_small(idx, own, by_c, cols_c, across, tb, bias, eb, sbuf):
    x, c = idx[2], idx[3]
    for ref, dc in ((own, 0), (by_c, 1)):
        for dx in range(2):
            sbuf[(x ^ dx) * 2 + (c ^ dc)] = ref[16 * dx : 16 * (dx + 1), :].astype(F32)
    pad = jnp.zeros((1, WIDTH), F32)
    qv = [jnp.concatenate([sbuf[h, r : r + 1, 0:96] for h in range(4)], axis=1) for r in (0, 1)]
    bias[0:16, :] = jnp.concatenate(
        [jnp.concatenate([qv[0], pad, qv[1]], axis=1), jnp.zeros((15, 3 * WIDTH), F32)], axis=0
    ).astype(BF)
    eb[...] = jnp.concatenate(
        [
            jnp.concatenate([sbuf[h, 2:3, :] for h in range(4)], axis=1),
            jnp.zeros((15, HIDDEN), F32),
        ],
        axis=0,
    ).astype(BF)
    up = onehot((SLOT, 128), 1, cols_c[0:SLOT, 2:3])
    for g in range(GROUPS):
        blocks = []
        for h in range(g * PACK, (g + 1) * PACK):
            row = sbuf[h // 3, 3 + h % 3 : 4 + h % 3, 0:256]
            lines = pltpu.roll(
                jnp.broadcast_to(row, (128, 256)), 129, axis=1, stride=1, stride_axis=0
            )
            keyed = dot_nn(up, lines.astype(BF)).astype(BF)
            blocks.append(dot_nn(keyed, across[...]))
        tb[g] = jnp.concatenate(blocks, axis=1) * LOG2E


BATCH = 4


def canvas_start(step):
    return pl.multiple_of((step // 4) * QUAD_ROWS + (step % 4) * 192, 16)


def attention_forward(
    idx, mine, other, nas, codes_row, codes_col, u, bias, tb,
    mrg, qt, kt, vv, pt, mt, wnat, outt, wout,
    wbuf, waug, wt,
):
    def put(row, head, value):
        wbuf[head, pl.ds(row, 48), :] = value

    assemble(idx, (mine, other), put)
    for j in range(3):
        waug[0:WIDTH, j * WIDTH : (j + 1) * WIDTH] = jnp.concatenate(
            [wbuf[h, :, 96 * j : 96 * (j + 1)] for h in range(4)], axis=1
        )
    out_t = jnp.concatenate([wbuf[h, :, 288:384] for h in range(4)], axis=1)
    outt[...] = out_t
    wout[...] = out_t.T
    waug[WIDTH : WIDTH + 16, :] = bias[...]
    waug[WIDTH + 16 : 512, :] = jnp.zeros((112, 3 * WIDTH), BF)
    wnat[...] = waug[0:WIDTH, :]
    wt[...] = waug[...].T

    def canvases(batch, carry):
        steps = [batch * BATCH + i for i in range(BATCH)]
        units = [(i, w, g) for i in range(BATCH) for w, g in UNITS]
        all_t = [dot_nt(wt[...], nas[s]).astype(BF) for s in steps]
        kv = [dot_nt(nas[s], wt[WIDTH:, :]).astype(BF) for s in steps]
        masks = {}
        for i, s in enumerate(steps):
            for win in range(4):
                row = jnp.concatenate([codes_row[s, 0:1, window(win)]] * PACK, axis=1)
                masks[i, win] = jnp.where(codes_col[s, window(win), 0:1] == row, 0.0, MASKED)
        scores = {
            (i, w, g): dot_nn(kv[i][window(w), feats(g)], spread(all_t[i][feats(g), window(w)]))
            for i, w, g in units
        }
        probs = {}
        for i, w, g in units:
            sc = scores[i, w, g] * (SCALE * LOG2E) + (tb[g] + masks[i, w])
            grown = jnp.exp2(sc - jnp.max(sc, axis=0, keepdims=True))
            probs[i, w, g] = (grown * (1.0 / jnp.sum(grown, axis=0, keepdims=True))).astype(BF)
        mixed = {
            (i, w, g): dot_nn(all_t[i][2 * WIDTH :][feats(g), window(w)], probs[i, w, g])
            for i, w, g in units
        }
        for i, s in enumerate(steps):
            turn, start = s % 4, canvas_start(s)
            merged_t = own_blocks({(w, g): mixed[i, w, g] for w, g in UNITS}).astype(BF)
            back = dot_nt(u[turn], merged_t).astype(BF)
            for w, g in UNITS:
                pt[s, w * GROUPS + g] = probs[i, w, g]
            mt[s] = merged_t
            qt[s] = all_t[i][0:WIDTH]
            kt[s] = all_t[i][WIDTH : 2 * WIDTH]
            vv[s] = kv[i][:, WIDTH:]
            begin = pl.ds(start, 16)
            mrg[begin, :] = back[0:16] + jnp.where(
                turn == 0, jnp.zeros((16, WIDTH), BF), mrg[begin, :]
            )
            mrg[pl.ds(pl.multiple_of(start + 16, 16), SPAN - 16), :] = back[16:]
        return carry

    lax.fori_loop(0, nas.shape[0] // BATCH, canvases, 0)


TILE = 784


def mlp_begin(mrg, tok, outt, par, mid, n2, n2t):
    lane = lax.broadcasted_iota(jnp.int32, (TILE, 128), 1)
    ones = jnp.where(lane == 0, 1.0, 0.0).astype(BF)

    def head_rows(t, carry):
        rows = pl.ds(pl.multiple_of(t * TILE, 16), TILE)
        middle = tok[rows, :].astype(F32) + dot_nt(mrg[rows, :], outt[...]) + par[4:5, :]
        mid[rows, :] = middle
        hat, _ = stats(middle)
        n2[rows, 0:WIDTH] = (hat * par[2:3, :] + par[3:4, :]).astype(BF)
        n2[rows, WIDTH:512] = ones
        return carry

    lax.fori_loop(0, tok.shape[0] // TILE, head_rows, 0)
    n2t[...] = n2[...].T[0:400, :]


HALF = 2 * WIDTH


def mlp_half(other, idx, weights, n2, n2t, got, gout, eb, *refs):
    if other:
        before_m, before_g, before_eb, *refs = refs
        acc_m, acc_g, grads_out, rows_out, *refs = refs
    else:
        acc_m, acc_g, grads_out, ebg, *refs = refs
    eaug, ct, hid, gpr, cg, eg, *refs = refs
    core = idx[3] ^ 1 if other else idx[3]
    for e, k, s, row, head in owners(idx):
        if e == 0:
            start = (k * 4 + (0, 2, 1, 3).index(s)) * 48
            lanes = pl.ds(pl.multiple_of((idx[2] ^ (k & 1)) * WIDTH, 128), WIDTH)
            eaug[pl.ds(row, 48), lanes] = weights[start : start + 48, 0:WIDTH]
            ct[pl.ds(row, 48), lanes] = weights[start : start + 48, WIDTH:]
    for x in range(2):
        lanes = pl.ds(pl.multiple_of((2 * x + core) * WIDTH, 128), WIDTH)
        eaug[WIDTH : WIDTH + 16, x * WIDTH : (x + 1) * WIDTH] = eb[:, lanes]
    eaug[WIDTH + 16 : 512, :] = jnp.zeros((112, HALF), BF)
    pre = dot_nn(n2[...], eaug[...])
    grad_hidden = dot_nn(gout[...], ct[...])
    phi = 0.5 + 0.5 * lax.erf(pre * ROOT_HALF)
    bell = jnp.exp2(pre * pre * (-0.5 * LOG2E)) * INV_ROOT_TWO_PI
    hidden = (pre * phi).astype(BF)
    grad_pre = (grad_hidden * (phi + pre * bell)).astype(BF)
    hid[...] = hidden
    gpr[...] = grad_pre
    if other:
        acc_m[...] = before_m[...] + dot_nt(hidden, ct[...])
        acc_g[...] = before_g[...] + dot_nt(grad_pre, eaug[0:WIDTH, :])
    else:
        acc_m[...] = dot_nt(hidden, ct[...])
        acc_g[...] = dot_nt(grad_pre, eaug[0:WIDTH, :])
    cg[...] = dot_nn(got[...], hid[...]).astype(BF)
    grads = dot_nn(n2t[...], gpr[...])
    eg[...] = grads[0:WIDTH].astype(BF)
    if not other:
        ebg[...] = grads[WIDTH : WIDTH + 8]
    for e, k, s, row, head in owners(idx):
        if e == 0:
            lanes = pl.ds(pl.multiple_of((idx[2] ^ (k & 1)) * WIDTH, 128), WIDTH)
            base = (k * 4 + s) * 48
            grads_out[base : base + 48, 0:WIDTH] = eg[pl.ds(row, 48), lanes]
            grads_out[base : base + 48, WIDTH:] = cg[pl.ds(row, 48), lanes]
    if other:
        (small,) = refs
        small[...] = jnp.zeros(small.shape, F32)
        for x in range(2):
            block = slice(x * WIDTH, (x + 1) * WIDTH)
            for place, part in ((core, grads[WIDTH : WIDTH + 1]), (idx[3], before_eb[0:1, :])):
                lanes = pl.ds(pl.multiple_of(place * WIDTH, 128), WIDTH)
                small[x : x + 1, lanes] = part[:, block]
        rows_out[...] = small[...].astype(BF)
        grads_out[768:784, :] = small[...].astype(BF)


def mlp_end(mid, acc_m, acc_g, gout, par, blk, gmid, sums):
    def tail_rows(t, carry):
        rows = pl.ds(pl.multiple_of(t * TILE, 16), TILE)
        middle = mid[rows, :]
        blk[rows, :] = (middle + acc_m[rows, :] + par[5:6, :]).astype(BF)
        hat, inv = stats(middle)
        g = acc_g[rows, :]
        top = gout[rows, :].astype(F32)
        grad_mid = top + norm_back(g, hat, inv, par[2:3, :])
        gmid[rows, :] = grad_mid
        parts = (g * hat, g, grad_mid, top)
        return tuple(c + jnp.sum(p, axis=0, keepdims=True) for c, p in zip(carry, parts))

    zero = jnp.zeros((1, WIDTH), F32)
    totals = lax.fori_loop(0, mid.shape[0] // TILE, tail_rows, (zero,) * 4)
    sums[...] = jnp.concatenate([zero, zero, *totals, zero, zero], axis=0)


def small_rows(wacc, table, wnat, sums, down, across, small):
    totals = wacc[WIDTH : WIDTH + 1, :]
    high = totals.astype(BF)
    split = [high, (totals - high.astype(F32)).astype(BF), jnp.zeros((6, 3 * WIDTH), BF)]
    offset_sum = jnp.sum(
        dot_nt(jnp.concatenate(split, axis=0), wnat[...]), axis=0, keepdims=True
    )
    products = (wnat[...].astype(F32) * wacc[0:WIDTH, :]).astype(BF)
    gain_sum = dot_nt(jnp.full((8, 3 * WIDTH), 1.0, BF), products)[0:1, :]
    rows = [gain_sum, offset_sum, sums[2:6, :], totals[:, 0:WIDTH], totals[:, 2 * WIDTH :]]
    lines = []
    for g in range(GROUPS):
        high = table[g].astype(BF)
        low = (table[g] - high.astype(F32)).astype(BF)
        both = jnp.concatenate([high, low], axis=0)
        heads = [both[:, h * SLOT : (h + 1) * SLOT] for h in range(PACK)]
        spaced = dot_nt(jnp.concatenate(heads, axis=0), across[...]).astype(BF)
        spaced = [spaced[h * 128 : (h + 1) * 128] for h in range(PACK)]
        spread_out = dot_nn(down[...], jnp.concatenate(spaced, axis=1))
        for h in range(PACK):
            shifted = pltpu.roll(
                spread_out[:, h * 256 : (h + 1) * 256], 0, axis=1, stride=1, stride_axis=0
            )
            lines.append(jnp.sum(shifted, axis=0, keepdims=True)[:, 0:192])
    rows += [jnp.concatenate(lines[2 * i : 2 * i + 2], axis=1) for i in range(6)]
    rows.append(jnp.zeros((2, WIDTH), F32))
    small[...] = jnp.concatenate(rows, axis=0).astype(BF)


def attention_backward(
    idx, gmid, qt, kt, vv, pt, mt, xt, wout, ut, par, wnat, sums, down, across,
    keep, send, gta, small,
    ntall, oacc, wacc, table,
):
    table[...] = jnp.zeros(table.shape, F32)
    oacc[...] = jnp.zeros(oacc.shape, F32)
    wacc[...] = jnp.zeros(wacc.shape, F32)

    def rows_of(parts):
        return jnp.concatenate(
            [jnp.concatenate([parts[w, g] for w in range(4)], axis=1) for g in range(GROUPS)],
            axis=0,
        )

    def canvases(batch, carry):
        steps = [batch * BATCH + i for i in range(BATCH)]
        units = [(i, w, g) for i in range(BATCH) for w, g in UNITS]
        gmw = [
            dot_nn(ut[s % 4], gmid[pl.ds(canvas_start(s), SPAN), :].astype(BF)).astype(BF)
            for s in steps
        ]
        gmt = [dot_nt(wout[...], v).astype(BF) for v in gmw]
        gm_s = {(i, w, g): spread(gmt[i][feats(g), window(w)]) for i, w, g in units}
        gp = {
            (i, w, g): dot_nn(vv[steps[i], window(w), feats(g)], gm_s[i, w, g])
            for i, w, g in units
        }
        gs = {}
        for i, w, g in units:
            probs = pt[steps[i], w * GROUPS + g].astype(F32)
            delta = jnp.sum(probs * gp[i, w, g], axis=0, keepdims=True)
            gs[i, w, g] = (probs * (gp[i, w, g] - delta)).astype(BF)
        q_s = {(i, w, g): spread(qt[steps[i], feats(g), window(w)]) for i, w, g in units}
        gq = {
            (i, w, g): dot_nn(kt[steps[i], feats(g), window(w)], gs[i, w, g])
            for i, w, g in units
        }
        gk = {(i, w, g): dot_nt(q_s[i, w, g], gs[i, w, g]) for i, w, g in units}
        gv = {
            (i, w, g): dot_nt(gm_s[i, w, g], pt[steps[i], w * GROUPS + g]) for i, w, g in units
        }
        g_all = []
        for i in range(BATCH):
            parts = [{(w, g): v[i, w, g] for w, g in UNITS} for v in (gq, gk, gv)]
            g_all.append(
                jnp.concatenate(
                    [
                        (own_blocks(parts[0]) * SCALE).astype(BF),
                        (rows_of(parts[1]) * SCALE).astype(BF),
                        rows_of(parts[2]).astype(BF),
                    ],
                    axis=0,
                )
            )
            gta[steps[i]] = g_all[i]
        wacc[...] += dot_nt(
            jnp.concatenate([xt[s] for s in steps], axis=1), jnp.concatenate(g_all, axis=1)
        )
        oacc[...] += dot_nn(
            jnp.concatenate([mt[s] for s in steps], axis=1), jnp.concatenate(gmw, axis=0)
        )
        for g in range(GROUPS):
            table[g] += sum(gs[i, w, g].astype(F32) for i in range(BATCH) for w in range(4))
        return carry

    lax.fori_loop(0, qt.shape[0] // BATCH, canvases, 0)
    columns = par[...].T
    grads = wacc[0:WIDTH, :] * columns[:, 0:1] + columns[:, 1:2] * wacc[WIDTH : WIDTH + 1, :]
    grads = grads.astype(BF)
    out_t = oacc[...].astype(BF).T
    for h in range(4):
        pieces = [grads[:, j * WIDTH + 96 * h : j * WIDTH + 96 * (h + 1)] for j in range(3)]
        pieces.append(out_t[:, 96 * h : 96 * (h + 1)])
        ntall[h] = jnp.concatenate(pieces, axis=1)
    for e, k, s, row, head in owners(idx):
        base = (k * 4 + s) * 48
        (keep, send)[e][base : base + 48, :] = ntall[head, pl.ds(row, 48), :]
    small_rows(wacc, table, wnat, sums, down, across, small)
    send[768:784, :] = small[...]


def tokens_end(n_state, tok, gmid, gta, wnat, u, par, *refs):
    state, (gtok, *near), arrived = refs[:n_state], refs[n_state:-1], refs[-1]
    copies = [
        pltpu.make_async_copy(source, target, arrived.at[i])
        for i, (source, target) in enumerate(zip(state, near))
    ]
    for copy in copies:
        copy.start()

    def block_rows(block, carry):
        ends = [
            dot_nt(u[turn], gta[4 * block + turn]).astype(BF) for turn in range(4)
        ]
        pieces = [ends[0][0:192]]
        for turn in range(1, 4):
            pieces += [ends[turn - 1][192:] + ends[turn][0:16], ends[turn][16:192]]
        g1 = dot_nt(jnp.concatenate([*pieces, ends[3][192:]], axis=0), wnat[...])
        rows = pl.ds(pl.multiple_of(block * QUAD_ROWS, 16), QUAD_ROWS)
        hat, inv = stats(tok[rows, :].astype(F32))
        gtok[rows, :] = gmid[rows, :] + norm_back(g1, hat, inv, par[0:1, :])
        return carry

    lax.fori_loop(0, gta.shape[0] // 4, block_rows, 0)
    for copy in copies:
        copy.wait()


def join(*refs):
    parts, out = refs[:-1], refs[-1]
    start = 0
    for part in parts:
        out[start : start + part.shape[0], :] = part[...]
        start += part.shape[0]


def plane_sum(keep, got, mine, theirs, own, send1, send2, send3, rest):
    small = mine[...].astype(F32) + theirs[...].astype(F32)
    rest[...] = small
    for k, ref in enumerate((own, send1, send2, send3)):
        block = slice(k * 192, (k + 1) * 192)
        value = keep[block, :].astype(F32) + got[block, :].astype(F32)
        ref[0:192, :] = value.astype(ref.dtype)
        if k:
            ref[192:, :] = small.astype(BF)


def line_sum(own, r1, r2, r3, mine, *refs):
    parts = (r1, r2, r3)
    small = mine[...] + sum(r[192:, :].astype(F32) for r in parts)
    refs[4][...] = small
    for s in range(4):
        block = slice(s * 48, (s + 1) * 48)
        value = own[block, :] + sum(r[block, :].astype(F32) for r in parts)
        if s == 0:
            refs[0][...] = value
        else:
            refs[s][0:48, :] = value.astype(BF)
            refs[s][48:, :] = small.astype(BF)


def half_sum(own, mine, *refs):
    parts, (keep, send, rest) = refs[:-3], refs[-3:]
    rows = own.shape[0]
    half = rows // 2
    total = own[...] + sum(r[0:rows, :].astype(F32) for r in parts)
    small = mine[...] + sum(r[rows:, :].astype(F32) for r in parts)
    keep[...] = total[0:half]
    send[0:half, :] = total[half:].astype(BF)
    send[half:, :] = small.astype(BF)
    rest[...] = small


def adamw(master, grad, moment, square, step_rate, decay_rate):
    moment_new = BETA_ONE * moment + (1.0 - BETA_ONE) * grad
    square_new = BETA_TWO * square + (1.0 - BETA_TWO) * grad * grad
    moment_hat = moment_new * (1.0 / (1.0 - BETA_ONE**STEP))
    square_hat = square_new * (1.0 / (1.0 - BETA_TWO**STEP))
    step = moment_hat / (jnp.sqrt(square_hat) + ADAM_EPS)
    if decay_rate:
        step = step + decay_rate * master
    return master - step_rate * step, moment_new, square_new


def update(refs, grad, outs, step_rate, decay_rate, at=...):
    master, moment, square = (r[at] for r in refs)
    news = adamw(master, grad, moment, square, step_rate, decay_rate)
    for out, new in zip(outs, news):
        out[at] = new


def step_mlp(n_parts, rows, *refs):
    parts, rest, refs = refs[:n_parts], refs[n_parts], refs[n_parts + 1 :]
    ins, outs, total_rest = refs[:6], refs[6:12], refs[12]
    total = sum(r[0:rows, :].astype(F32) for r in parts)
    total_rest[...] = rest[...] + sum(r[rows:, :].astype(F32) for r in parts[1:])
    update(ins[0:3], total[:, 0:WIDTH], outs[0:3], RATE_MATRIX, DECAY_MATRIX)
    update(ins[3:6], total[:, WIDTH:], outs[3:6], RATE_MATRIX, DECAY_MATRIX)


def step_attention(n_parts, rows, idx, *refs):
    parts, refs = refs[:n_parts], refs[n_parts:]
    half = (len(refs) - 2) // 2
    rest, small, ins, outs = refs[0], refs[1], refs[2 : half + 2], refs[half + 2 :]
    total = sum(r[0:rows, :].astype(F32) for r in parts)
    small = small[...] + sum(r[rows:, :].astype(F32) for r in parts[1:])
    head = idx[2] * 2 + idx[3]

    def pick(blocks):
        return sum(jnp.where(head == h, block, 0.0) for h, block in enumerate(blocks))

    for j in range(3):
        update(
            ins[0:3], total[:, 96 * j : 96 * (j + 1)], outs[0:3], RATE_MATRIX, DECAY_MATRIX, at=j
        )
    update(ins[3:6], total[:, 288:384], outs[3:6], RATE_MATRIX, DECAY_MATRIX)
    qv = pick([small[6:8, 96 * h : 96 * (h + 1)] for h in range(4)])
    update(ins[6:9], qv, outs[6:9], RATE_SMALL, 0.0)
    eb = pick([rest[h // 2 : h // 2 + 1, WIDTH * (h % 2) : WIDTH * (h % 2 + 1)] for h in range(4)])
    update(ins[9:12], eb.reshape(ins[9].shape), outs[9:12], RATE_SMALL, 0.0)
    table_rows = ins[12].shape[1]
    lines = [
        small[8 + n // 2 : 9 + n // 2, 192 * (n % 2) : 192 * (n % 2) + table_rows]
        for n in range(12)
    ]
    table = pick([jnp.concatenate(lines[3 * h : 3 * h + 3], axis=0) for h in range(4)])
    update(ins[12:15], table, outs[12:15], RATE_SMALL, 0.0)
    update(ins[15:18], small[0:6, :], outs[15:18], RATE_SMALL, 0.0)


class Links:
    def __init__(self, sizes):
        self.sizes = sizes
        self.outer = sizes["dp"] // 8

    def perm(self, z=0, y=0, x=0, c=0):
        pairs = []
        for flat in range(self.sizes["dp"] * self.sizes["head"]):
            head, dp = flat % 4, flat // 4
            inner, place = dp // self.outer, dp % self.outer
            inner ^= z * 2 + y
            pairs.append((flat, (inner * self.outer + place) * 4 + (head ^ (x * 2 + c))))
        return pairs

    def send(self, value, **flips):
        return lax.ppermute(value, ("dp", "head"), self.perm(**flips))

    def groups(self):
        return [[i * self.outer + j for j in range(self.outer)] for i in range(8)]

    def outer_gather(self, shard):
        if self.outer > 1:
            shard = lax.all_gather(
                shard, "dp", axis=0, tiled=True, axis_index_groups=self.groups()
            )
        return shard

    def gather_line(self, shard):
        return jnp.concatenate([shard] + [self.send(shard, z=s) for s in range(1, 4)], axis=0)

    def gather_plane(self, line):
        return [line] + [self.send(line, x=k & 1, y=k >> 1) for k in range(1, 4)]

    def gather_core(self, plane):
        rows = sum(p.shape[0] for p in plane)
        (plane,) = call(join, [((rows, plane[0].shape[1]), BF)], *plane)
        return plane, self.send(plane, c=1)

    def to_plane(self, blocks):
        return [self.send(b, x=k & 1, y=k >> 1) for k, b in enumerate(blocks, 1)]

    def to_line(self, blocks):
        return [self.send(b, z=s) for s, b in enumerate(blocks, 1)]

    def outer_sum(self, value):
        if self.outer > 1:
            value = lax.psum_scatter(
                value, "dp", scatter_dimension=0, tiled=True, axis_index_groups=self.groups()
            )
        return value


SMEM = pl.BlockSpec(memory_space=pltpu.SMEM)
VMEM = pl.BlockSpec(memory_space=pltpu.VMEM)
HBM = pl.BlockSpec(memory_space=pltpu.HBM)


class Far:
    def __init__(self, value, pinned=False):
        self.value, self.pinned = value, pinned


def placed(arg):
    if isinstance(arg, Far):
        return pltpu.with_memory_space_constraint(arg.value, pltpu.HBM)
    return pltpu.with_memory_space_constraint(arg, pltpu.VMEM)


def call(kernel, outs, *args, scratch=(), limit=10, scalars=None, far=(), time=1, same=()):
    lead = [] if scalars is None else [scalars]
    name = getattr(kernel, "__name__", None) or kernel.func.__name__
    return pl.pallas_call(
        kernel,
        in_specs=[SMEM] * len(lead)
        + [HBM if isinstance(a, Far) and a.pinned else VMEM for a in args],
        out_specs=[VMEM] * len(outs),
        out_shape=[(pltpu.HBM if i in far else pltpu.VMEM)(s, d) for i, (s, d) in enumerate(outs)],
        scratch_shapes=[
            pltpu.SemaphoreType.DMA((s,)) if isinstance(s, int) else pltpu.VMEM(*s)
            for s in scratch
        ],
        compiler_params=pltpu.CompilerParams(vmem_limit_bytes=limit * 2**20),
        cost_estimate=pl.CostEstimate(
            flops=int(time * 1.15e9), bytes_accessed=0, transcendentals=0
        ),
        input_output_aliases={i + len(lead): o for i, o in same},
        name=name,
    )(*lead, *(placed(a) for a in args))


def per_device(links, *args):
    (
        tokens, crop_ids, grad_out, qkv_w, out_w, exp_w, con_w, qv_b, exp_b, table_w, norm_p,
        qkv_m, qkv_s, out_m, out_s, exp_m, exp_s, con_m, con_s,
        qv_m, qv_s, eb_m, eb_s, tab_m, tab_s, norm_m, norm_s,
    ) = args
    rows_all = tokens.shape[0]
    canvases = rows_all // CANVAS
    head = lax.axis_index("head")
    dp = lax.axis_index("dp") // links.outer
    idx = jnp.stack([dp // 2, dp % 2, head // 2, head % 2]).astype(jnp.int32)
    slots = 4 * SLOT
    wide = (rows_all, WIDTH)
    square = (WIDTH, WIDTH)
    fm = (canvases, WIDTH, slots)
    tm = (canvases, slots, WIDTH)

    rows_own = exp_w.shape[0]
    first, second, own = call(
        pack,
        [((rows_own, WIDTH), BF), ((rows_own, 2 * WIDTH), BF), ((16, WIDTH), BF)],
        Far(qkv_w), Far(out_w.T), Far(exp_w), Far(con_w.T), Far(qv_b), Far(exp_b), Far(table_w.T),
    )
    first = links.outer_gather(first)
    line = links.gather_line(first)
    second = links.outer_gather(second)
    pair_s = jnp.concatenate([second, links.send(second, z=2)], axis=0)
    own = jnp.concatenate([own, links.send(own, x=1)], axis=0)
    line, own = lax.optimization_barrier((line, own))
    plane = links.gather_plane(line)
    by_c = links.send(own, c=1)
    crop_rows, _ = lax.optimization_barrier((crop_ids, line))
    crop_rows = crop_rows.reshape(-1, QUAD_ROWS)
    pair_s, crop_rows = lax.optimization_barrier((pair_s, crop_rows))
    line_s = jnp.concatenate([pair_s, links.send(pair_s, z=1)], axis=0)
    rows_c, cols_c = (jnp.asarray(t) for t in tables())
    to_slots = (4, slots, SPAN)
    nas, xt, ut, u, tok, gout, got, code_row, code_col, par, down, across = call(
        prepare,
        [
            ((canvases, slots, 512), BF), ((canvases, 400, slots), BF), (to_slots, BF),
            ((4, SPAN, slots), BF), (wide, BF), (wide, BF), ((WIDTH, rows_all), BF),
            ((canvases, 8, slots), F32), ((canvases, slots, 8), F32), ((8, WIDTH), F32),
            ((128, 2 * SLOT), BF), ((256, SLOT), BF),
        ],
        own, Far(tokens), Far(grad_out), Far(crop_rows), Far(rows_c), Far(cols_c),
        Far(norm_p), limit=12, scalars=idx, time=4,
    )
    by_c, nas = lax.optimization_barrier((by_c, nas))
    bias_t, bias16, eb16 = call(
        spread_small, [((GROUPS, SLOT, slots), F32), ((16, 3 * WIDTH), BF), ((16, HIDDEN), BF)],
        own, by_c, Far(cols_c), across, scratch=[((4, 16, WIDTH), F32)], scalars=idx, time=2,
    )
    *plane, line_s, bias_t = lax.optimization_barrier((*plane, line_s, bias_t))
    plane_s = links.gather_plane(line_s)
    firsts = links.gather_core(plane)
    merged, qt, kt, vv, pt, mt, wnat, outt, wout = call(
        attention_forward,
        [
            (wide, BF), (fm, BF), (fm, BF), (tm, BF), ((canvases, 12, SLOT, slots), BF), (fm, BF),
            ((WIDTH, 3 * WIDTH), BF), (square, BF), (square, BF),
        ],
        *firsts, nas, code_row, code_col, u, bias16, bias_t,
        scratch=[
            ((4, WIDTH, WIDTH), BF), ((512, 3 * WIDTH), BF), ((3 * WIDTH, 512), BF),
        ],
        limit=14, scalars=idx, time=11,
    )
    middle, n2, n2t = call(
        mlp_begin, [(wide, F32), ((rows_all, 512), BF), ((400, rows_all), BF)],
        merged, tok, outt, par, time=3,
    )
    n2, *plane_s = lax.optimization_barrier((n2, *plane_s))
    seconds = links.gather_core(plane_s)
    scratch = [
        ((512, HALF), BF), ((WIDTH, HALF), BF), ((rows_all, HALF), BF), ((rows_all, HALF), BF),
        ((WIDTH, HALF), BF), ((WIDTH, HALF), BF),
    ]
    acc_m, acc_g, keep_r, eb_grad = call(
        functools.partial(mlp_half, False),
        [(wide, F32), (wide, F32), ((768, HALF), BF), ((8, HALF), F32)],
        seconds[0], n2, n2t, got, gout, eb16, scratch=scratch, limit=17, scalars=idx, time=9,
    )
    acc_m, other_s = lax.optimization_barrier((acc_m, seconds[1]))
    acc_m, acc_g, send_r, rest = call(
        functools.partial(mlp_half, True),
        [(wide, F32), (wide, F32), ((784, HALF), BF), ((16, HALF), BF)],
        other_s, n2, n2t, got, gout, eb16, acc_m, acc_g, eb_grad,
        scratch=scratch + [((16, HALF), F32)], limit=17, scalars=idx, time=9, same=((6, 0), (7, 1)),
    )
    got_r = links.send(send_r, c=1)
    block_out, grad_mid, sums = call(
        mlp_end, [(wide, BF), (wide, F32), ((8, WIDTH), F32)], middle, acc_m, acc_g, gout, par,
        limit=10, far=(0,), time=3,
    )
    wide_r = 2 * WIDTH
    block_r = [((192, wide_r), F32)] + [((208, wide_r), BF)] * 3 + [((16, wide_r), F32)]
    got_r, grad_mid = lax.optimization_barrier((got_r, grad_mid))
    own_r, *blocks_r, rest = call(
        plane_sum, block_r, keep_r, got_r, rest, got_r[768:]
    )
    grad_mid, *blocks_r = lax.optimization_barrier((grad_mid, *blocks_r))
    plane_r = links.to_plane(blocks_r)
    state = [
        exp_w, exp_m, exp_s, con_w.T, con_m.T, con_s.T, qkv_w, qkv_m, qkv_s, out_w.T, out_m.T,
        out_s.T, qv_b, qv_m, qv_s, exp_b, eb_m, eb_s, table_w.T, tab_m.T, tab_s.T, norm_p, norm_m,
        norm_s,
    ]
    keep_q, send_q, g_all, small = call(
        attention_backward,
        [
            ((768, WIDTH), BF), ((784, WIDTH), BF), ((canvases, 3 * WIDTH, slots), BF),
            ((16, WIDTH), BF),
        ],
        grad_mid, qt, kt, vv, pt, mt, xt, wout, ut, par, wnat, sums, down, across,
        scratch=[
            ((4, WIDTH, WIDTH), BF), (square, F32), ((400, 3 * WIDTH), F32),
            ((GROUPS, SLOT, slots), F32),
        ],
        limit=20, scalars=idx, time=15,
    )
    *plane_r, send_q = lax.optimization_barrier((*plane_r, send_q))
    got_q = links.send(send_q, c=1)
    own_r, block_r, rest = call(
        half_sum, [((96, wide_r), F32), ((112, wide_r), BF), ((16, wide_r), F32)],
        own_r, rest, *plane_r,
    )
    block_q = [((192, WIDTH), F32)] + [((208, WIDTH), BF)] * 3 + [((16, WIDTH), F32)]
    own_q, *blocks_q, small = call(plane_sum, block_q, keep_q, got_q, small, got_q[768:])
    plane_q = links.to_plane(blocks_q)
    got_r = links.send(block_r, z=2)
    g_all = lax.optimization_barrier((g_all, *blocks_q))[0]
    grad_tokens, *near = call(
        functools.partial(tokens_end, len(state)),
        [(wide, F32)] + [(a.shape, F32) for a in state],
        tok, grad_mid, g_all, wnat, u, par, *(Far(a, pinned=True) for a in state),
        scratch=[len(state)], far=(0,), time=6,
    )
    got_r, grad_tokens = lax.optimization_barrier((got_r, grad_tokens))
    own_r, block_r, rest = call(
        half_sum, [((48, wide_r), F32), ((64, wide_r), BF), ((16, wide_r), F32)],
        own_r, rest, got_r,
    )
    line_q = [((48, WIDTH), F32)] + [((64, WIDTH), BF)] * 3 + [((16, WIDTH), F32)]
    own_q, *blocks_q, small = call(line_sum, line_q, own_q, *plane_q, small)
    parts_q = [own_q, *links.to_line(blocks_q)]
    parts_r = [own_r, links.send(block_r, z=1)]
    rows = 48
    if links.outer > 1:
        small = small + sum(p[48:].astype(F32) for p in parts_q[1:])
        rest = rest + parts_r[1][48:].astype(F32)
        small, rest = lax.psum((small, rest), "dp", axis_index_groups=links.groups())
        parts_q = [links.outer_sum(sum(p[:48].astype(F32) for p in parts_q))]
        parts_r = [links.outer_sum(sum(p[:48].astype(F32) for p in parts_r))]
        rows = parts_q[0].shape[0]
    *third, rest = call(
        functools.partial(step_mlp, len(parts_r), rows),
        [(a.shape, F32) for a in state[:6]] + [((16, wide_r), F32)],
        *parts_r, rest, *near[:6], far=range(6),
    )
    *parts_q, rest = lax.optimization_barrier((*parts_q, rest))
    fourth = call(
        functools.partial(step_attention, len(parts_q), rows),
        [(a.shape, F32) for a in state[6:]], *parts_q, rest, small, *near[6:], scalars=idx,
        far=range(len(state) - 6), time=2,
    )
    return (
        block_out, grad_tokens, *fourth[0:3], *(a.T for a in fourth[3:6]), *third[0:3],
        *(a.T for a in third[3:6]), *fourth[6:12], *(a.T for a in fourth[12:15]), *fourth[15:],
    )


def solution(mesh):
    tokens = P(("dp", "head"), None)
    qkv, rows_head, rows_dp = P(None, "dp", "head"), P("head", "dp"), P("dp", "head")
    pair, unit, none = P(None, "head"), P("head"), P()
    matrices = (qkv, rows_head, rows_dp, rows_head)
    small = (pair, unit, pair, none)
    in_specs = (tokens, P("dp"), tokens, *matrices, *small)
    in_specs += tuple(s for spec in (*matrices, *small) for s in (spec, spec))
    out_specs = (tokens, tokens) + tuple(
        s for spec in (*matrices, *small) for s in (spec, spec, spec)
    )
    return jax.shard_map(
        functools.partial(per_device, Links(dict(mesh.shape))),
        mesh=mesh, in_specs=in_specs, out_specs=out_specs, check_vma=False,
    )
```

```python
import functools
import math

import jax
import jax.numpy as jnp
import numpy as np
from jax import lax
from jax.experimental import pallas as pl
from jax.experimental.pallas import tpu as pltpu
from jax.sharding import PartitionSpec as P

HEAD_DIM = 32
WINDOW = 7
SIDE = 14
SHIFT = 3
STEP = 10
CANVAS = SIDE * SIDE
PLACES = WINDOW * WINDOW
SLOT = 64
QUAD_ROWS = 4 * CANVAS
SPAN = 208
WIDTH = 384
GROUPS = 3
PACK = 4
HIDDEN = 1536
CHUNK = 512

NORM_EPS = 1e-05
BETA_ONE = 0.9
BETA_TWO = 0.999
ADAM_EPS = 1e-08
RATE_MATRIX = 0.1
RATE_SMALL = 0.5
DECAY_MATRIX = 0.05
MASKED = -1e30
LOG2E = math.log2(math.e)
SCALE = HEAD_DIM**-0.5
ROOT_HALF = 0.7071067811865476
INV_ROOT_TWO_PI = 1.0 / 2.5066282746310002
BF = jnp.bfloat16
F32 = jnp.float32


def slot_rows():
    rows = -np.ones((4, SLOT), np.int64)
    for win in range(4):
        for place in range(PLACES):
            row = (win // 2) * WINDOW + place // WINDOW
            col = (win % 2) * WINDOW + place % WINDOW
            rows[win, place] = ((row + SHIFT) % SIDE) * SIDE + (col + SHIFT) % SIDE
    return rows.reshape(-1)


def region_codes():
    def band(v):
        return 0 if v < SIDE - WINDOW else (1 if v < SIDE - SHIFT else 2)

    codes = np.full((4, SLOT), 999.0, np.float32)
    for win in range(4):
        for place in range(PLACES):
            row = (win // 2) * WINDOW + place // WINDOW
            col = (win % 2) * WINDOW + place % WINDOW
            codes[win, place] = 4 * (3 * band(row) + band(col))
    return codes.reshape(-1)


def tables():
    line = np.array([13 * (p // WINDOW) + p % WINDOW for p in range(PLACES)], np.float32)
    out = np.full((8, 4 * SLOT), -1000.0, np.float32)
    out[0] = slot_rows()
    out[0][out[0] < 0] = -1000.0
    out[1] = region_codes()
    out[2, :PLACES] = 43 + line
    out[3, :PLACES] = out[3, SLOT : SLOT + PLACES] = 84 - line
    out[4, :PLACES] = line
    return out, out.T.copy()


def onehot(shape, axis, places):
    index = lax.broadcasted_iota(jnp.int32, shape, axis).astype(F32)
    return jnp.where(index == places, 1.0, 0.0).astype(BF)


def dot_nn(a, b):
    return jnp.dot(a, b, preferred_element_type=F32)


def dot_nt(a, b):
    return lax.dot_general(a, b, (((1,), (1,)), ((), ())), preferred_element_type=F32)


def stats(values):
    centred = values - jnp.mean(values, axis=-1, keepdims=True)
    inv_std = lax.rsqrt(jnp.mean(centred * centred, axis=-1, keepdims=True) + NORM_EPS)
    return centred * inv_std, inv_std


def norm_back(grad_norm, hat, inv_std, gain_row):
    grad_hat = grad_norm * gain_row
    inner = grad_hat - jnp.mean(grad_hat, axis=-1, keepdims=True)
    return inv_std * (inner - hat * jnp.mean(grad_hat * hat, axis=-1, keepdims=True))


def owners(idx):
    z, y, x, c = idx[0], idx[1], idx[2], idx[3]
    for e in range(2):
        for k in range(4):
            for s in range(4):
                row = ((z ^ s) * 2 + (y ^ (k >> 1))) * 48
                yield e, k, s, pl.multiple_of(row, 16), (x ^ (k & 1)) * 2 + (c ^ e)


def spread(block):
    four = jnp.concatenate([block] * PACK, axis=1)
    rows = lax.broadcasted_iota(jnp.int32, four.shape, 0) // HEAD_DIM
    lanes = lax.broadcasted_iota(jnp.int32, four.shape, 1) // SLOT
    return jnp.where(rows == lanes, four, jnp.zeros_like(four))


def assemble(idx, refs, put, order=(0, 1, 2, 3)):
    for e, k, s, row, head in owners(idx):
        start = (k * 4 + order.index(s)) * 48
        put(row, head, refs[e][start : start + 48, :])


UNITS = [(win, g) for win in range(4) for g in range(GROUPS)]


def window(win):
    return slice(win * SLOT, (win + 1) * SLOT)


def feats(g):
    return slice(g * 128, (g + 1) * 128)


def own_blocks(parts):
    rows = []
    for g in range(GROUPS):
        for h in range(PACK):
            rows.append(
                jnp.concatenate(
                    [
                        parts[win, g][
                            h * HEAD_DIM : (h + 1) * HEAD_DIM, h * SLOT : (h + 1) * SLOT
                        ]
                        for win in range(4)
                    ],
                    axis=1,
                )
            )
    return jnp.concatenate(rows, axis=0)


def pack(qkv, out_t, expand, contract_t, qv, eb, table_t, first, second, own):
    first[...] = jnp.concatenate([qkv[0], qkv[1], qkv[2], out_t[...]], axis=1).astype(BF)
    second[:, 0:WIDTH] = expand[...].astype(BF)
    second[:, WIDTH:] = contract_t[...].astype(BF)
    own[...] = jnp.zeros(own.shape, BF)
    own[0:2, 0:96] = qv[...].astype(BF)
    own[2:3, :] = eb[...].reshape(1, -1).astype(BF)
    own[3:6, 0 : table_t.shape[1]] = table_t[...].astype(BF)


def prepare(
    idx, after, tok, gout, crop, rows_c, cols_c, par_h,
    na, xt, ut, u, tokv, goutv, got, code_row, code_col, par, down, across,
):
    down[...] = onehot((128, 2 * SLOT), 0, rows_c[3:4, 0 : 2 * SLOT])
    across[...] = onehot((256, SLOT), 0, rows_c[4:5, 0:SLOT])
    tokv[...] = tok[...]
    goutv[...] = gout[...]
    par[...] = jnp.concatenate([par_h[...], jnp.zeros((2, WIDTH), F32)], axis=0)
    lane = lax.broadcasted_iota(jnp.int32, (4 * SLOT, 128), 1)
    ones = jnp.where(lane == 0, 1.0, 0.0).astype(BF)
    to_slots = []
    for turn in range(4):
        ut[turn] = onehot((4 * SLOT, SPAN), 1, cols_c[:, 0:1] + 4.0 * turn)
        u[turn] = onehot((SPAN, 4 * SLOT), 0, rows_c[0:1, :] + 4.0 * turn)
        to_slots.append(ut[turn])
    head = idx[2] * 2 + idx[3]
    for block in range(na.shape[0] // 4):
        hat, _ = stats(tok[block * QUAD_ROWS : (block + 1) * QUAD_ROWS, :].astype(F32))
        n1 = (hat * par_h[0:1, :] + par_h[1:2, :]).astype(BF)
        sides = jnp.concatenate([n1, hat.astype(BF)], axis=1)
        crops = crop[pl.ds(head * (na.shape[0] // 4) + block, 1), :] & 3
        for turn in range(4):
            step, start = 4 * block + turn, 192 * turn
            both = dot_nn(to_slots[turn], sides[start : start + SPAN]).astype(BF)
            na[step] = jnp.concatenate([both[:, 0:WIDTH], ones], axis=1)
            xt[step] = jnp.concatenate([both[:, WIDTH:], ones], axis=1).T[0:400, :]
            quad = crops[:, start : start + SPAN]
            quad = jnp.broadcast_to(quad.astype(F32), (8, SPAN)).astype(BF)
            code_row[step] = dot_nt(quad, to_slots[turn]) + rows_c[1:2, :]
            code_col[step] = dot_nt(to_slots[turn], quad) + cols_c[:, 1:2]
    got[...] = gout[...].T


def spread_small(idx, own, by_c, cols_c, across, tb, bias, eb, sbuf):
    x, c = idx[2], idx[3]
    for ref, dc in ((own, 0), (by_c, 1)):
        for dx in range(2):
            sbuf[(x ^ dx) * 2 + (c ^ dc)] = ref[16 * dx : 16 * (dx + 1), :].astype(F32)
    pad = jnp.zeros((1, WIDTH), F32)
    qv = [jnp.concatenate([sbuf[h, r : r + 1, 0:96] for h in range(4)], axis=1) for r in (0, 1)]
    bias[0:16, :] = jnp.concatenate(
        [jnp.concatenate([qv[0], pad, qv[1]], axis=1), jnp.zeros((15, 3 * WIDTH), F32)], axis=0
    ).astype(BF)
    eb[...] = jnp.concatenate(
        [
            jnp.concatenate([sbuf[h, 2:3, :] for h in range(4)], axis=1),
            jnp.zeros((15, HIDDEN), F32),
        ],
        axis=0,
    ).astype(BF)
    up = onehot((SLOT, 128), 1, cols_c[0:SLOT, 2:3])
    for g in range(GROUPS):
        blocks = []
        for h in range(g * PACK, (g + 1) * PACK):
            row = sbuf[h // 3, 3 + h % 3 : 4 + h % 3, 0:256]
            lines = pltpu.roll(
                jnp.broadcast_to(row, (128, 256)), 129, axis=1, stride=1, stride_axis=0
            )
            keyed = dot_nn(up, lines.astype(BF)).astype(BF)
            blocks.append(dot_nn(keyed, across[...]))
        tb[g] = jnp.concatenate(blocks, axis=1) * LOG2E


BATCH = 4


def canvas_start(step):
    return pl.multiple_of((step // 4) * QUAD_ROWS + (step % 4) * 192, 16)


def attention_forward(
    idx, mine, other, nas, codes_row, codes_col, u, bias, tb,
    mrg, qt, kt, vv, pt, mt, wnat, outt, wout,
    wbuf, waug, wt,
):
    def put(row, head, value):
        wbuf[head, pl.ds(row, 48), :] = value

    assemble(idx, (mine, other), put)
    for j in range(3):
        waug[0:WIDTH, j * WIDTH : (j + 1) * WIDTH] = jnp.concatenate(
            [wbuf[h, :, 96 * j : 96 * (j + 1)] for h in range(4)], axis=1
        )
    out_t = jnp.concatenate([wbuf[h, :, 288:384] for h in range(4)], axis=1)
    outt[...] = out_t
    wout[...] = out_t.T
    waug[WIDTH : WIDTH + 16, :] = bias[...]
    waug[WIDTH + 16 : 512, :] = jnp.zeros((112, 3 * WIDTH), BF)
    wnat[...] = waug[0:WIDTH, :]
    wt[...] = waug[...].T

    def canvases(batch, carry):
        steps = [batch * BATCH + i for i in range(BATCH)]
        units = [(i, w, g) for i in range(BATCH) for w, g in UNITS]
        all_t = [dot_nt(wt[...], nas[s]).astype(BF) for s in steps]
        kv = [dot_nt(nas[s], wt[WIDTH:, :]).astype(BF) for s in steps]
        masks = {}
        for i, s in enumerate(steps):
            for win in range(4):
                row = jnp.concatenate([codes_row[s, 0:1, window(win)]] * PACK, axis=1)
                masks[i, win] = jnp.where(codes_col[s, window(win), 0:1] == row, 0.0, MASKED)
        scores = {
            (i, w, g): dot_nn(kv[i][window(w), feats(g)], spread(all_t[i][feats(g), window(w)]))
            for i, w, g in units
        }
        probs = {}
        for i, w, g in units:
            sc = scores[i, w, g] * (SCALE * LOG2E) + (tb[g] + masks[i, w])
            grown = jnp.exp2(sc - jnp.max(sc, axis=0, keepdims=True))
            probs[i, w, g] = (grown * (1.0 / jnp.sum(grown, axis=0, keepdims=True))).astype(BF)
        mixed = {
            (i, w, g): dot_nn(all_t[i][2 * WIDTH :][feats(g), window(w)], probs[i, w, g])
            for i, w, g in units
        }
        for i, s in enumerate(steps):
            turn, start = s % 4, canvas_start(s)
            merged_t = own_blocks({(w, g): mixed[i, w, g] for w, g in UNITS}).astype(BF)
            back = dot_nt(u[turn], merged_t).astype(BF)
            for w, g in UNITS:
                pt[s, w * GROUPS + g] = probs[i, w, g]
            mt[s] = merged_t
            qt[s] = all_t[i][0:WIDTH]
            kt[s] = all_t[i][WIDTH : 2 * WIDTH]
            vv[s] = kv[i][:, WIDTH:]
            begin = pl.ds(start, 16)
            mrg[begin, :] = back[0:16] + jnp.where(
                turn == 0, jnp.zeros((16, WIDTH), BF), mrg[begin, :]
            )
            mrg[pl.ds(pl.multiple_of(start + 16, 16), SPAN - 16), :] = back[16:]
        return carry

    lax.fori_loop(0, nas.shape[0] // BATCH, canvases, 0)


TILE = 784


def mlp_begin(mrg, tok, outt, par, mid, n2, n2t):
    lane = lax.broadcasted_iota(jnp.int32, (TILE, 128), 1)
    ones = jnp.where(lane == 0, 1.0, 0.0).astype(BF)

    def head_rows(t, carry):
        rows = pl.ds(pl.multiple_of(t * TILE, 16), TILE)
        middle = tok[rows, :].astype(F32) + dot_nt(mrg[rows, :], outt[...]) + par[4:5, :]
        mid[rows, :] = middle
        hat, _ = stats(middle)
        n2[rows, 0:WIDTH] = (hat * par[2:3, :] + par[3:4, :]).astype(BF)
        n2[rows, WIDTH:512] = ones
        return carry

    lax.fori_loop(0, tok.shape[0] // TILE, head_rows, 0)
    n2t[...] = n2[...].T[0:400, :]


HALF = 2 * WIDTH


def mlp_half(other, idx, weights, n2, n2t, got, gout, eb, *refs):
    if other:
        before_m, before_g, before_eb, *refs = refs
        acc_m, acc_g, grads_out, rows_out, *refs = refs
    else:
        acc_m, acc_g, grads_out, ebg, *refs = refs
    eaug, ct, hid, gpr, cg, eg, *refs = refs
    core = idx[3] ^ 1 if other else idx[3]
    for e, k, s, row, head in owners(idx):
        if e == 0:
            start = (k * 4 + (0, 2, 1, 3).index(s)) * 48
            lanes = pl.ds(pl.multiple_of((idx[2] ^ (k & 1)) * WIDTH, 128), WIDTH)
            eaug[pl.ds(row, 48), lanes] = weights[start : start + 48, 0:WIDTH]
            ct[pl.ds(row, 48), lanes] = weights[start : start + 48, WIDTH:]
    for x in range(2):
        lanes = pl.ds(pl.multiple_of((2 * x + core) * WIDTH, 128), WIDTH)
        eaug[WIDTH : WIDTH + 16, x * WIDTH : (x + 1) * WIDTH] = eb[:, lanes]
    eaug[WIDTH + 16 : 512, :] = jnp.zeros((112, HALF), BF)
    pre = dot_nn(n2[...], eaug[...])
    grad_hidden = dot_nn(gout[...], ct[...])
    phi = 0.5 + 0.5 * lax.erf(pre * ROOT_HALF)
    bell = jnp.exp2(pre * pre * (-0.5 * LOG2E)) * INV_ROOT_TWO_PI
    hidden = (pre * phi).astype(BF)
    grad_pre = (grad_hidden * (phi + pre * bell)).astype(BF)
    hid[...] = hidden
    gpr[...] = grad_pre
    if other:
        acc_m[...] = before_m[...] + dot_nt(hidden, ct[...])
        acc_g[...] = before_g[...] + dot_nt(grad_pre, eaug[0:WIDTH, :])
    else:
        acc_m[...] = dot_nt(hidden, ct[...])
        acc_g[...] = dot_nt(grad_pre, eaug[0:WIDTH, :])
    cg[...] = dot_nn(got[...], hid[...]).astype(BF)
    grads = dot_nn(n2t[...], gpr[...])
    eg[...] = grads[0:WIDTH].astype(BF)
    if not other:
        ebg[...] = grads[WIDTH : WIDTH + 8]
    for e, k, s, row, head in owners(idx):
        if e == 0:
            lanes = pl.ds(pl.multiple_of((idx[2] ^ (k & 1)) * WIDTH, 128), WIDTH)
            base = (k * 4 + s) * 48
            grads_out[base : base + 48, 0:WIDTH] = eg[pl.ds(row, 48), lanes]
            grads_out[base : base + 48, WIDTH:] = cg[pl.ds(row, 48), lanes]
    if other:
        (small,) = refs
        small[...] = jnp.zeros(small.shape, F32)
        for x in range(2):
            block = slice(x * WIDTH, (x + 1) * WIDTH)
            for place, part in ((core, grads[WIDTH : WIDTH + 1]), (idx[3], before_eb[0:1, :])):
                lanes = pl.ds(pl.multiple_of(place * WIDTH, 128), WIDTH)
                small[x : x + 1, lanes] = part[:, block]
        rows_out[...] = small[...].astype(BF)
        grads_out[768:784, :] = small[...].astype(BF)


def mlp_end(mid, acc_m, acc_g, gout, par, blk, gmid, sums):
    def tail_rows(t, carry):
        rows = pl.ds(pl.multiple_of(t * TILE, 16), TILE)
        middle = mid[rows, :]
        blk[rows, :] = (middle + acc_m[rows, :] + par[5:6, :]).astype(BF)
        hat, inv = stats(middle)
        g = acc_g[rows, :]
        top = gout[rows, :].astype(F32)
        grad_mid = top + norm_back(g, hat, inv, par[2:3, :])
        gmid[rows, :] = grad_mid
        parts = (g * hat, g, grad_mid, top)
        return tuple(c + jnp.sum(p, axis=0, keepdims=True) for c, p in zip(carry, parts))

    zero = jnp.zeros((1, WIDTH), F32)
    totals = lax.fori_loop(0, mid.shape[0] // TILE, tail_rows, (zero,) * 4)
    sums[...] = jnp.concatenate([zero, zero, *totals, zero, zero], axis=0)


def small_rows(wacc, table, wnat, sums, down, across, small):
    totals = wacc[WIDTH : WIDTH + 1, :]
    high = totals.astype(BF)
    split = [high, (totals - high.astype(F32)).astype(BF), jnp.zeros((6, 3 * WIDTH), BF)]
    offset_sum = jnp.sum(
        dot_nt(jnp.concatenate(split, axis=0), wnat[...]), axis=0, keepdims=True
    )
    products = (wnat[...].astype(F32) * wacc[0:WIDTH, :]).astype(BF)
    gain_sum = dot_nt(jnp.full((8, 3 * WIDTH), 1.0, BF), products)[0:1, :]
    rows = [gain_sum, offset_sum, sums[2:6, :], totals[:, 0:WIDTH], totals[:, 2 * WIDTH :]]
    lines = []
    for g in range(GROUPS):
        high = table[g].astype(BF)
        low = (table[g] - high.astype(F32)).astype(BF)
        both = jnp.concatenate([high, low], axis=0)
        heads = [both[:, h * SLOT : (h + 1) * SLOT] for h in range(PACK)]
        spaced = dot_nt(jnp.concatenate(heads, axis=0), across[...]).astype(BF)
        spaced = [spaced[h * 128 : (h + 1) * 128] for h in range(PACK)]
        spread_out = dot_nn(down[...], jnp.concatenate(spaced, axis=1))
        for h in range(PACK):
            shifted = pltpu.roll(
                spread_out[:, h * 256 : (h + 1) * 256], 0, axis=1, stride=1, stride_axis=0
            )
            lines.append(jnp.sum(shifted, axis=0, keepdims=True)[:, 0:192])
    rows += [jnp.concatenate(lines[2 * i : 2 * i + 2], axis=1) for i in range(6)]
    rows.append(jnp.zeros((2, WIDTH), F32))
    small[...] = jnp.concatenate(rows, axis=0).astype(BF)


def attention_backward(
    idx, gmid, qt, kt, vv, pt, mt, xt, wout, ut, par, wnat, sums, down, across,
    keep, send, gta, small,
    ntall, oacc, wacc, table,
):
    table[...] = jnp.zeros(table.shape, F32)
    oacc[...] = jnp.zeros(oacc.shape, F32)
    wacc[...] = jnp.zeros(wacc.shape, F32)

    def rows_of(parts):
        return jnp.concatenate(
            [jnp.concatenate([parts[w, g] for w in range(4)], axis=1) for g in range(GROUPS)],
            axis=0,
        )

    def canvases(batch, carry):
        steps = [batch * BATCH + i for i in range(BATCH)]
        units = [(i, w, g) for i in range(BATCH) for w, g in UNITS]
        gmw = [
            dot_nn(ut[s % 4], gmid[pl.ds(canvas_start(s), SPAN), :].astype(BF)).astype(BF)
            for s in steps
        ]
        gmt = [dot_nt(wout[...], v).astype(BF) for v in gmw]
        gm_s = {(i, w, g): spread(gmt[i][feats(g), window(w)]) for i, w, g in units}
        gp = {
            (i, w, g): dot_nn(vv[steps[i], window(w), feats(g)], gm_s[i, w, g])
            for i, w, g in units
        }
        gs = {}
        for i, w, g in units:
            probs = pt[steps[i], w * GROUPS + g].astype(F32)
            delta = jnp.sum(probs * gp[i, w, g], axis=0, keepdims=True)
            gs[i, w, g] = (probs * (gp[i, w, g] - delta)).astype(BF)
        q_s = {(i, w, g): spread(qt[steps[i], feats(g), window(w)]) for i, w, g in units}
        gq = {
            (i, w, g): dot_nn(kt[steps[i], feats(g), window(w)], gs[i, w, g])
            for i, w, g in units
        }
        gk = {(i, w, g): dot_nt(q_s[i, w, g], gs[i, w, g]) for i, w, g in units}
        gv = {
            (i, w, g): dot_nt(gm_s[i, w, g], pt[steps[i], w * GROUPS + g]) for i, w, g in units
        }
        g_all = []
        for i in range(BATCH):
            parts = [{(w, g): v[i, w, g] for w, g in UNITS} for v in (gq, gk, gv)]
            g_all.append(
                jnp.concatenate(
                    [
                        (own_blocks(parts[0]) * SCALE).astype(BF),
                        (rows_of(parts[1]) * SCALE).astype(BF),
                        rows_of(parts[2]).astype(BF),
                    ],
                    axis=0,
                )
            )
            gta[steps[i]] = g_all[i]
        wacc[...] += dot_nt(
            jnp.concatenate([xt[s] for s in steps], axis=1), jnp.concatenate(g_all, axis=1)
        )
        oacc[...] += dot_nn(
            jnp.concatenate([mt[s] for s in steps], axis=1), jnp.concatenate(gmw, axis=0)
        )
        for g in range(GROUPS):
            table[g] += sum(gs[i, w, g].astype(F32) for i in range(BATCH) for w in range(4))
        return carry

    lax.fori_loop(0, qt.shape[0] // BATCH, canvases, 0)
    columns = par[...].T
    grads = wacc[0:WIDTH, :] * columns[:, 0:1] + columns[:, 1:2] * wacc[WIDTH : WIDTH + 1, :]
    grads = grads.astype(BF)
    out_t = oacc[...].astype(BF).T
    for h in range(4):
        pieces = [grads[:, j * WIDTH + 96 * h : j * WIDTH + 96 * (h + 1)] for j in range(3)]
        pieces.append(out_t[:, 96 * h : 96 * (h + 1)])
        ntall[h] = jnp.concatenate(pieces, axis=1)
    for e, k, s, row, head in owners(idx):
        base = (k * 4 + s) * 48
        (keep, send)[e][base : base + 48, :] = ntall[head, pl.ds(row, 48), :]
    small_rows(wacc, table, wnat, sums, down, across, small)
    send[768:784, :] = small[...]


def tokens_end(tok, gmid, gta, wnat, u, par, gtok):
    def block_rows(block, carry):
        ends = [
            dot_nt(u[turn], gta[4 * block + turn]).astype(BF) for turn in range(4)
        ]
        pieces = [ends[0][0:192]]
        for turn in range(1, 4):
            pieces += [ends[turn - 1][192:] + ends[turn][0:16], ends[turn][16:192]]
        g1 = dot_nt(jnp.concatenate([*pieces, ends[3][192:]], axis=0), wnat[...])
        rows = pl.ds(pl.multiple_of(block * QUAD_ROWS, 16), QUAD_ROWS)
        hat, inv = stats(tok[rows, :].astype(F32))
        gtok[rows, :] = gmid[rows, :] + norm_back(g1, hat, inv, par[0:1, :])
        return carry

    lax.fori_loop(0, gta.shape[0] // 4, block_rows, 0)


def join(*refs):
    parts, out = refs[:-1], refs[-1]
    start = 0
    for part in parts:
        out[start : start + part.shape[0], :] = part[...]
        start += part.shape[0]


def plane_sum(keep, got, mine, theirs, own, send1, send2, send3, rest):
    small = mine[...].astype(F32) + theirs[...].astype(F32)
    rest[...] = small
    for k, ref in enumerate((own, send1, send2, send3)):
        block = slice(k * 192, (k + 1) * 192)
        value = keep[block, :].astype(F32) + got[block, :].astype(F32)
        ref[0:192, :] = value.astype(ref.dtype)
        if k:
            ref[192:, :] = small.astype(BF)


def line_sum(own, r1, r2, r3, mine, *refs):
    parts = (r1, r2, r3)
    small = mine[...] + sum(r[192:, :].astype(F32) for r in parts)
    refs[4][...] = small
    for s in range(4):
        block = slice(s * 48, (s + 1) * 48)
        value = own[block, :] + sum(r[block, :].astype(F32) for r in parts)
        if s == 0:
            refs[0][...] = value
        else:
            refs[s][0:48, :] = value.astype(BF)
            refs[s][48:, :] = small.astype(BF)


def half_sum(own, mine, *refs):
    parts, (keep, send, rest) = refs[:-3], refs[-3:]
    rows = own.shape[0]
    half = rows // 2
    total = own[...] + sum(r[0:rows, :].astype(F32) for r in parts)
    small = mine[...] + sum(r[rows:, :].astype(F32) for r in parts)
    keep[...] = total[0:half]
    send[0:half, :] = total[half:].astype(BF)
    send[half:, :] = small.astype(BF)
    rest[...] = small


def adamw(master, grad, moment, square, step_rate, decay_rate):
    moment_new = BETA_ONE * moment + (1.0 - BETA_ONE) * grad
    square_new = BETA_TWO * square + (1.0 - BETA_TWO) * grad * grad
    moment_hat = moment_new * (1.0 / (1.0 - BETA_ONE**STEP))
    square_hat = square_new * (1.0 / (1.0 - BETA_TWO**STEP))
    step = moment_hat / (jnp.sqrt(square_hat) + ADAM_EPS)
    if decay_rate:
        step = step + decay_rate * master
    return master - step_rate * step, moment_new, square_new


def update(refs, grad, outs, step_rate, decay_rate, at=...):
    master, moment, square = (r[at] for r in refs)
    news = adamw(master, grad, moment, square, step_rate, decay_rate)
    for out, new in zip(outs, news):
        out[at] = new


def step_mlp(n_parts, rows, *refs):
    parts, rest, refs = refs[:n_parts], refs[n_parts], refs[n_parts + 1 :]
    half = (len(refs) - 1) // 2
    ins, outs, total_rest = refs[:half], refs[half : 2 * half], refs[2 * half]
    for source, target in zip(ins[6:], outs[6:]):
        target[...] = source[...]
    total = sum(r[0:rows, :].astype(F32) for r in parts)
    total_rest[...] = rest[...] + sum(r[rows:, :].astype(F32) for r in parts[1:])
    update(ins[0:3], total[:, 0:WIDTH], outs[0:3], RATE_MATRIX, DECAY_MATRIX)
    update(ins[3:6], total[:, WIDTH:], outs[3:6], RATE_MATRIX, DECAY_MATRIX)


def step_attention(n_parts, rows, idx, *refs):
    parts, refs = refs[:n_parts], refs[n_parts:]
    half = (len(refs) - 2) // 2
    rest, small, ins, outs = refs[0], refs[1], refs[2 : half + 2], refs[half + 2 :]
    total = sum(r[0:rows, :].astype(F32) for r in parts)
    small = small[...] + sum(r[rows:, :].astype(F32) for r in parts[1:])
    head = idx[2] * 2 + idx[3]

    def pick(blocks):
        return sum(jnp.where(head == h, block, 0.0) for h, block in enumerate(blocks))

    for j in range(3):
        update(
            ins[0:3], total[:, 96 * j : 96 * (j + 1)], outs[0:3], RATE_MATRIX, DECAY_MATRIX, at=j
        )
    update(ins[3:6], total[:, 288:384], outs[3:6], RATE_MATRIX, DECAY_MATRIX)
    qv = pick([small[6:8, 96 * h : 96 * (h + 1)] for h in range(4)])
    update(ins[6:9], qv, outs[6:9], RATE_SMALL, 0.0)
    eb = pick([rest[h // 2 : h // 2 + 1, WIDTH * (h % 2) : WIDTH * (h % 2 + 1)] for h in range(4)])
    update(ins[9:12], eb.reshape(ins[9].shape), outs[9:12], RATE_SMALL, 0.0)
    table_rows = ins[12].shape[1]
    lines = [
        small[8 + n // 2 : 9 + n // 2, 192 * (n % 2) : 192 * (n % 2) + table_rows]
        for n in range(12)
    ]
    table = pick([jnp.concatenate(lines[3 * h : 3 * h + 3], axis=0) for h in range(4)])
    update(ins[12:15], table, outs[12:15], RATE_SMALL, 0.0)
    update(ins[15:18], small[0:6, :], outs[15:18], RATE_SMALL, 0.0)


class Links:
    def __init__(self, sizes):
        self.sizes = sizes
        self.outer = sizes["dp"] // 8

    def perm(self, z=0, y=0, x=0, c=0):
        pairs = []
        for flat in range(self.sizes["dp"] * self.sizes["head"]):
            head, dp = flat % 4, flat // 4
            inner, place = dp // self.outer, dp % self.outer
            inner ^= z * 2 + y
            pairs.append((flat, (inner * self.outer + place) * 4 + (head ^ (x * 2 + c))))
        return pairs

    def send(self, value, **flips):
        return lax.ppermute(value, ("dp", "head"), self.perm(**flips))

    def groups(self):
        return [[i * self.outer + j for j in range(self.outer)] for i in range(8)]

    def outer_gather(self, shard):
        if self.outer > 1:
            shard = lax.all_gather(
                shard, "dp", axis=0, tiled=True, axis_index_groups=self.groups()
            )
        return shard

    def gather_line(self, shard):
        return jnp.concatenate([shard] + [self.send(shard, z=s) for s in range(1, 4)], axis=0)

    def gather_plane(self, line):
        return [line] + [self.send(line, x=k & 1, y=k >> 1) for k in range(1, 4)]

    def gather_core(self, plane):
        rows = sum(p.shape[0] for p in plane)
        (plane,) = call(join, [((rows, plane[0].shape[1]), BF)], *plane)
        return plane, self.send(plane, c=1)

    def to_plane(self, blocks):
        return [self.send(b, x=k & 1, y=k >> 1) for k, b in enumerate(blocks, 1)]

    def to_line(self, blocks):
        return [self.send(b, z=s) for s, b in enumerate(blocks, 1)]

    def outer_sum(self, value):
        if self.outer > 1:
            value = lax.psum_scatter(
                value, "dp", scatter_dimension=0, tiled=True, axis_index_groups=self.groups()
            )
        return value


SMEM = pl.BlockSpec(memory_space=pltpu.SMEM)
VMEM = pl.BlockSpec(memory_space=pltpu.VMEM)


class Far:
    def __init__(self, value):
        self.value = value


def placed(arg):
    if isinstance(arg, Far):
        return pltpu.with_memory_space_constraint(arg.value, pltpu.HBM)
    return pltpu.with_memory_space_constraint(arg, pltpu.VMEM)


def call(kernel, outs, *args, scratch=(), limit=10, scalars=None, far=(), time=1):
    lead = [] if scalars is None else [scalars]
    name = getattr(kernel, "__name__", None) or kernel.func.__name__
    return pl.pallas_call(
        kernel,
        in_specs=[SMEM] * len(lead) + [VMEM] * len(args),
        out_specs=[VMEM] * len(outs),
        out_shape=[(pltpu.HBM if i in far else pltpu.VMEM)(s, d) for i, (s, d) in enumerate(outs)],
        scratch_shapes=[pltpu.VMEM(s, d) for s, d in scratch],
        compiler_params=pltpu.CompilerParams(vmem_limit_bytes=limit * 2**20),
        cost_estimate=pl.CostEstimate(
            flops=int(time * 1.15e9), bytes_accessed=0, transcendentals=0
        ),
        name=name,
    )(*lead, *(placed(a) for a in args))


def per_device(links, *args):
    (
        tokens, crop_ids, grad_out, qkv_w, out_w, exp_w, con_w, qv_b, exp_b, table_w, norm_p,
        qkv_m, qkv_s, out_m, out_s, exp_m, exp_s, con_m, con_s,
        qv_m, qv_s, eb_m, eb_s, tab_m, tab_s, norm_m, norm_s,
    ) = args
    rows_all = tokens.shape[0]
    canvases = rows_all // CANVAS
    head = lax.axis_index("head")
    dp = lax.axis_index("dp") // links.outer
    idx = jnp.stack([dp // 2, dp % 2, head // 2, head % 2]).astype(jnp.int32)
    slots = 4 * SLOT
    wide = (rows_all, WIDTH)
    square = (WIDTH, WIDTH)
    fm = (canvases, WIDTH, slots)
    tm = (canvases, slots, WIDTH)

    rows_own = exp_w.shape[0]
    first, second, own = call(
        pack,
        [((rows_own, WIDTH), BF), ((rows_own, 2 * WIDTH), BF), ((16, WIDTH), BF)],
        Far(qkv_w), Far(out_w.T), Far(exp_w), Far(con_w.T), Far(qv_b), Far(exp_b), Far(table_w.T),
    )
    first = links.outer_gather(first)
    line = links.gather_line(first)
    second = links.outer_gather(second)
    pair_s = jnp.concatenate([second, links.send(second, z=2)], axis=0)
    own = jnp.concatenate([own, links.send(own, x=1)], axis=0)
    line, own = lax.optimization_barrier((line, own))
    plane = links.gather_plane(line)
    by_c = links.send(own, c=1)
    crop_rows, _ = lax.optimization_barrier((crop_ids, line))
    crop_rows = crop_rows.reshape(-1, QUAD_ROWS)
    pair_s, crop_rows = lax.optimization_barrier((pair_s, crop_rows))
    line_s = jnp.concatenate([pair_s, links.send(pair_s, z=1)], axis=0)
    rows_c, cols_c = (jnp.asarray(t) for t in tables())
    to_slots = (4, slots, SPAN)
    nas, xt, ut, u, tok, gout, got, code_row, code_col, par, down, across = call(
        prepare,
        [
            ((canvases, slots, 512), BF), ((canvases, 400, slots), BF), (to_slots, BF),
            ((4, SPAN, slots), BF), (wide, BF), (wide, BF), ((WIDTH, rows_all), BF),
            ((canvases, 8, slots), F32), ((canvases, slots, 8), F32), ((8, WIDTH), F32),
            ((128, 2 * SLOT), BF), ((256, SLOT), BF),
        ],
        own, Far(tokens), Far(grad_out), Far(crop_rows), Far(rows_c), Far(cols_c),
        Far(norm_p), limit=12, scalars=idx, time=4,
    )
    by_c, nas = lax.optimization_barrier((by_c, nas))
    bias_t, bias16, eb16 = call(
        spread_small, [((GROUPS, SLOT, slots), F32), ((16, 3 * WIDTH), BF), ((16, HIDDEN), BF)],
        own, by_c, Far(cols_c), across, scratch=[((4, 16, WIDTH), F32)], scalars=idx, time=2,
    )
    *plane, line_s, bias_t = lax.optimization_barrier((*plane, line_s, bias_t))
    plane_s = links.gather_plane(line_s)
    firsts = links.gather_core(plane)
    merged, qt, kt, vv, pt, mt, wnat, outt, wout = call(
        attention_forward,
        [
            (wide, BF), (fm, BF), (fm, BF), (tm, BF), ((canvases, 12, SLOT, slots), BF), (fm, BF),
            ((WIDTH, 3 * WIDTH), BF), (square, BF), (square, BF),
        ],
        *firsts, nas, code_row, code_col, u, bias16, bias_t,
        scratch=[
            ((4, WIDTH, WIDTH), BF), ((512, 3 * WIDTH), BF), ((3 * WIDTH, 512), BF),
        ],
        limit=14, scalars=idx, time=11,
    )
    middle, n2, n2t = call(
        mlp_begin, [(wide, F32), ((rows_all, 512), BF), ((400, rows_all), BF)],
        merged, tok, outt, par, time=3,
    )
    n2, *plane_s = lax.optimization_barrier((n2, *plane_s))
    seconds = links.gather_core(plane_s)
    scratch = [
        ((512, HALF), BF), ((WIDTH, HALF), BF), ((rows_all, HALF), BF), ((rows_all, HALF), BF),
        ((WIDTH, HALF), BF), ((WIDTH, HALF), BF),
    ]
    acc_m, acc_g, keep_r, eb_grad = call(
        functools.partial(mlp_half, False),
        [(wide, F32), (wide, F32), ((768, HALF), BF), ((8, HALF), F32)],
        seconds[0], n2, n2t, got, gout, eb16, scratch=scratch, limit=17, scalars=idx, time=9,
    )
    acc_m, other_s = lax.optimization_barrier((acc_m, seconds[1]))
    acc_m, acc_g, send_r, rest = call(
        functools.partial(mlp_half, True),
        [(wide, F32), (wide, F32), ((784, HALF), BF), ((16, HALF), BF)],
        other_s, n2, n2t, got, gout, eb16, acc_m, acc_g, eb_grad,
        scratch=scratch + [((16, HALF), F32)], limit=17, scalars=idx, time=9,
    )
    got_r = links.send(send_r, c=1)
    block_out, grad_mid, sums = call(
        mlp_end, [(wide, BF), (wide, F32), ((8, WIDTH), F32)], middle, acc_m, acc_g, gout, par,
        limit=10, far=(0,), time=3,
    )
    wide_r = 2 * WIDTH
    block_r = [((192, wide_r), F32)] + [((208, wide_r), BF)] * 3 + [((16, wide_r), F32)]
    got_r, grad_mid = lax.optimization_barrier((got_r, grad_mid))
    own_r, *blocks_r, rest = call(
        plane_sum, block_r, keep_r, got_r, rest, got_r[768:]
    )
    grad_mid, *blocks_r = lax.optimization_barrier((grad_mid, *blocks_r))
    plane_r = links.to_plane(blocks_r)
    state = [
        exp_w, exp_m, exp_s, con_w.T, con_m.T, con_s.T, qkv_w, qkv_m, qkv_s, out_w.T, out_m.T,
        out_s.T, qv_b, qv_m, qv_s, exp_b, eb_m, eb_s, table_w.T, tab_m.T, tab_s.T, norm_p, norm_m,
        norm_s,
    ]
    keep_q, send_q, g_all, small = call(
        attention_backward,
        [
            ((768, WIDTH), BF), ((784, WIDTH), BF), ((canvases, 3 * WIDTH, slots), BF),
            ((16, WIDTH), BF),
        ],
        grad_mid, qt, kt, vv, pt, mt, xt, wout, ut, par, wnat, sums, down, across,
        scratch=[
            ((4, WIDTH, WIDTH), BF), (square, F32), ((400, 3 * WIDTH), F32),
            ((GROUPS, SLOT, slots), F32),
        ],
        limit=20, scalars=idx, time=15,
    )
    *plane_r, send_q = lax.optimization_barrier((*plane_r, send_q))
    got_q = links.send(send_q, c=1)
    own_r, block_r, rest = call(
        half_sum, [((96, wide_r), F32), ((112, wide_r), BF), ((16, wide_r), F32)],
        own_r, rest, *plane_r,
    )
    block_q = [((192, WIDTH), F32)] + [((208, WIDTH), BF)] * 3 + [((16, WIDTH), F32)]
    own_q, *blocks_q, small = call(plane_sum, block_q, keep_q, got_q, small, got_q[768:])
    plane_q = links.to_plane(blocks_q)
    got_r = links.send(block_r, z=2)
    g_all = lax.optimization_barrier((g_all, *blocks_q))[0]
    (grad_tokens,) = call(
        tokens_end, [(wide, F32)], tok, grad_mid, g_all, wnat, u, par, far=(0,), time=6,
    )
    got_r, grad_tokens = lax.optimization_barrier((got_r, grad_tokens))
    own_r, block_r, rest = call(
        half_sum, [((48, wide_r), F32), ((64, wide_r), BF), ((16, wide_r), F32)],
        own_r, rest, got_r,
    )
    line_q = [((48, WIDTH), F32)] + [((64, WIDTH), BF)] * 3 + [((16, WIDTH), F32)]
    own_q, *blocks_q, small = call(line_sum, line_q, own_q, *plane_q, small)
    parts_q = [own_q, *links.to_line(blocks_q)]
    parts_r = [own_r, links.send(block_r, z=1)]
    rows = 48
    if links.outer > 1:
        small = small + sum(p[48:].astype(F32) for p in parts_q[1:])
        rest = rest + parts_r[1][48:].astype(F32)
        small, rest = lax.psum((small, rest), "dp", axis_index_groups=links.groups())
        parts_q = [links.outer_sum(sum(p[:48].astype(F32) for p in parts_q))]
        parts_r = [links.outer_sum(sum(p[:48].astype(F32) for p in parts_r))]
        rows = parts_q[0].shape[0]
    *third, rest = call(
        functools.partial(step_mlp, len(parts_r), rows),
        [(a.shape, F32) for a in state] + [((16, wide_r), F32)],
        *parts_r, rest, *(Far(a) for a in state), far=range(6), time=2,
    )
    third, near = third[:6], third[6:]
    *parts_q, rest = lax.optimization_barrier((*parts_q, rest))
    fourth = call(
        functools.partial(step_attention, len(parts_q), rows),
        [(a.shape, F32) for a in state[6:]], *parts_q, rest, small, *near, scalars=idx,
        far=range(len(state) - 6), time=2,
    )
    return (
        block_out, grad_tokens, *fourth[0:3], *(a.T for a in fourth[3:6]), *third[0:3],
        *(a.T for a in third[3:6]), *fourth[6:12], *(a.T for a in fourth[12:15]), *fourth[15:],
    )


def solution(mesh):
    tokens = P(("dp", "head"), None)
    qkv, rows_head, rows_dp = P(None, "dp", "head"), P("head", "dp"), P("dp", "head")
    pair, unit, none = P(None, "head"), P("head"), P()
    matrices = (qkv, rows_head, rows_dp, rows_head)
    small = (pair, unit, pair, none)
    in_specs = (tokens, P("dp"), tokens, *matrices, *small)
    in_specs += tuple(s for spec in (*matrices, *small) for s in (spec, spec))
    out_specs = (tokens, tokens) + tuple(
        s for spec in (*matrices, *small) for s in (spec, spec, spec)
    )
    return jax.shard_map(
        functools.partial(per_device, Links(dict(mesh.shape))),
        mesh=mesh, in_specs=in_specs, out_specs=out_specs, check_vma=False,
    )
```

```python
import functools
import math

import jax
import jax.numpy as jnp
import numpy as np
from jax import lax
from jax.experimental import pallas as pl
from jax.experimental.pallas import tpu as pltpu
from jax.sharding import PartitionSpec as P

HEAD_DIM = 32
WINDOW = 7
SIDE = 14
SHIFT = 3
STEP = 10
CANVAS = SIDE * SIDE
PLACES = WINDOW * WINDOW
SLOT = 64
QUAD_ROWS = 4 * CANVAS
SPAN = 208
WIDTH = 384
GROUPS = 3
PACK = 4
HIDDEN = 1536
CHUNK = 512

NORM_EPS = 1e-05
BETA_ONE = 0.9
BETA_TWO = 0.999
ADAM_EPS = 1e-08
RATE_MATRIX = 0.1
RATE_SMALL = 0.5
DECAY_MATRIX = 0.05
MASKED = -1e30
LOG2E = math.log2(math.e)
SCALE = HEAD_DIM**-0.5
ROOT_HALF = 0.7071067811865476
INV_ROOT_TWO_PI = 1.0 / 2.5066282746310002
BF = jnp.bfloat16
F32 = jnp.float32


def slot_rows():
    rows = -np.ones((4, SLOT), np.int64)
    for win in range(4):
        for place in range(PLACES):
            row = (win // 2) * WINDOW + place // WINDOW
            col = (win % 2) * WINDOW + place % WINDOW
            rows[win, place] = ((row + SHIFT) % SIDE) * SIDE + (col + SHIFT) % SIDE
    return rows.reshape(-1)


def region_codes():
    def band(v):
        return 0 if v < SIDE - WINDOW else (1 if v < SIDE - SHIFT else 2)

    codes = np.full((4, SLOT), 999.0, np.float32)
    for win in range(4):
        for place in range(PLACES):
            row = (win // 2) * WINDOW + place // WINDOW
            col = (win % 2) * WINDOW + place % WINDOW
            codes[win, place] = 4 * (3 * band(row) + band(col))
    return codes.reshape(-1)


def tables():
    line = np.array([13 * (p // WINDOW) + p % WINDOW for p in range(PLACES)], np.float32)
    out = np.full((8, 4 * SLOT), -1000.0, np.float32)
    out[0] = slot_rows()
    out[0][out[0] < 0] = -1000.0
    out[1] = region_codes()
    out[2, :PLACES] = 43 + line
    out[3, :PLACES] = out[3, SLOT : SLOT + PLACES] = 84 - line
    out[4, :PLACES] = line
    return out, out.T.copy()


def onehot(shape, axis, places):
    index = lax.broadcasted_iota(jnp.int32, shape, axis).astype(F32)
    return jnp.where(index == places, 1.0, 0.0).astype(BF)


def dot_nn(a, b):
    return jnp.dot(a, b, preferred_element_type=F32)


def dot_nt(a, b):
    return lax.dot_general(a, b, (((1,), (1,)), ((), ())), preferred_element_type=F32)


def stats(values):
    centred = values - jnp.mean(values, axis=-1, keepdims=True)
    inv_std = lax.rsqrt(jnp.mean(centred * centred, axis=-1, keepdims=True) + NORM_EPS)
    return centred * inv_std, inv_std


def norm_back(grad_norm, hat, inv_std, gain_row):
    grad_hat = grad_norm * gain_row
    inner = grad_hat - jnp.mean(grad_hat, axis=-1, keepdims=True)
    return inv_std * (inner - hat * jnp.mean(grad_hat * hat, axis=-1, keepdims=True))


def owners(idx):
    z, y, x, c = idx[0], idx[1], idx[2], idx[3]
    for e in range(2):
        for k in range(4):
            for s in range(4):
                row = ((z ^ s) * 2 + (y ^ (k >> 1))) * 48
                yield e, k, s, pl.multiple_of(row, 16), (x ^ (k & 1)) * 2 + (c ^ e)


def spread(block):
    four = jnp.concatenate([block] * PACK, axis=1)
    rows = lax.broadcasted_iota(jnp.int32, four.shape, 0) // HEAD_DIM
    lanes = lax.broadcasted_iota(jnp.int32, four.shape, 1) // SLOT
    return jnp.where(rows == lanes, four, jnp.zeros_like(four))


def assemble(idx, refs, put, order=(0, 1, 2, 3)):
    for e, k, s, row, head in owners(idx):
        start = (k * 4 + order.index(s)) * 48
        put(row, head, refs[e][start : start + 48, :])


UNITS = [(win, g) for win in range(4) for g in range(GROUPS)]


def window(win):
    return slice(win * SLOT, (win + 1) * SLOT)


def feats(g):
    return slice(g * 128, (g + 1) * 128)


def own_blocks(parts):
    rows = []
    for g in range(GROUPS):
        for h in range(PACK):
            rows.append(
                jnp.concatenate(
                    [
                        parts[win, g][
                            h * HEAD_DIM : (h + 1) * HEAD_DIM, h * SLOT : (h + 1) * SLOT
                        ]
                        for win in range(4)
                    ],
                    axis=1,
                )
            )
    return jnp.concatenate(rows, axis=0)


def pack(qkv, out_t, expand, contract_t, qv, eb, table_t, first, second, own):
    first[...] = jnp.concatenate([qkv[0], qkv[1], qkv[2], out_t[...]], axis=1).astype(BF)
    second[:, 0:WIDTH] = expand[...].astype(BF)
    second[:, WIDTH:] = contract_t[...].astype(BF)
    own[...] = jnp.zeros(own.shape, BF)
    own[0:2, 0:96] = qv[...].astype(BF)
    own[2:3, :] = eb[...].reshape(1, -1).astype(BF)
    own[3:6, 0 : table_t.shape[1]] = table_t[...].astype(BF)


def prepare(
    idx, after, tok, gout, crop, rows_c, cols_c, par_h,
    na, xt, ut, u, tokv, goutv, got, code_row, code_col, par, down, across,
):
    down[...] = onehot((128, 2 * SLOT), 0, rows_c[3:4, 0 : 2 * SLOT])
    across[...] = onehot((256, SLOT), 0, rows_c[4:5, 0:SLOT])
    tokv[...] = tok[...]
    goutv[...] = gout[...]
    par[...] = jnp.concatenate([par_h[...], jnp.zeros((2, WIDTH), F32)], axis=0)
    lane = lax.broadcasted_iota(jnp.int32, (4 * SLOT, 128), 1)
    ones = jnp.where(lane == 0, 1.0, 0.0).astype(BF)
    to_slots = []
    for turn in range(4):
        ut[turn] = onehot((4 * SLOT, SPAN), 1, cols_c[:, 0:1] + 4.0 * turn)
        u[turn] = onehot((SPAN, 4 * SLOT), 0, rows_c[0:1, :] + 4.0 * turn)
        to_slots.append(ut[turn])
    head = idx[2] * 2 + idx[3]
    for block in range(na.shape[0] // 4):
        hat, _ = stats(tok[block * QUAD_ROWS : (block + 1) * QUAD_ROWS, :].astype(F32))
        n1 = (hat * par_h[0:1, :] + par_h[1:2, :]).astype(BF)
        sides = jnp.concatenate([n1, hat.astype(BF)], axis=1)
        crops = crop[pl.ds(head * (na.shape[0] // 4) + block, 1), :] & 3
        for turn in range(4):
            step, start = 4 * block + turn, 192 * turn
            both = dot_nn(to_slots[turn], sides[start : start + SPAN]).astype(BF)
            na[step] = jnp.concatenate([both[:, 0:WIDTH], ones], axis=1)
            xt[step] = jnp.concatenate([both[:, WIDTH:], ones], axis=1).T[0:400, :]
            quad = crops[:, start : start + SPAN]
            quad = jnp.broadcast_to(quad.astype(F32), (8, SPAN)).astype(BF)
            code_row[step] = dot_nt(quad, to_slots[turn]) + rows_c[1:2, :]
            code_col[step] = dot_nt(to_slots[turn], quad) + cols_c[:, 1:2]
    got[...] = gout[...].T


def spread_small(idx, own, by_c, cols_c, across, tb, bias, eb, sbuf):
    x, c = idx[2], idx[3]
    for ref, dc in ((own, 0), (by_c, 1)):
        for dx in range(2):
            sbuf[(x ^ dx) * 2 + (c ^ dc)] = ref[16 * dx : 16 * (dx + 1), :].astype(F32)
    pad = jnp.zeros((1, WIDTH), F32)
    qv = [jnp.concatenate([sbuf[h, r : r + 1, 0:96] for h in range(4)], axis=1) for r in (0, 1)]
    bias[0:16, :] = jnp.concatenate(
        [jnp.concatenate([qv[0], pad, qv[1]], axis=1), jnp.zeros((15, 3 * WIDTH), F32)], axis=0
    ).astype(BF)
    eb[...] = jnp.concatenate(
        [
            jnp.concatenate([sbuf[h, 2:3, :] for h in range(4)], axis=1),
            jnp.zeros((15, HIDDEN), F32),
        ],
        axis=0,
    ).astype(BF)
    up = onehot((SLOT, 128), 1, cols_c[0:SLOT, 2:3])
    for g in range(GROUPS):
        blocks = []
        for h in range(g * PACK, (g + 1) * PACK):
            row = sbuf[h // 3, 3 + h % 3 : 4 + h % 3, 0:256]
            lines = pltpu.roll(
                jnp.broadcast_to(row, (128, 256)), 129, axis=1, stride=1, stride_axis=0
            )
            keyed = dot_nn(up, lines.astype(BF)).astype(BF)
            blocks.append(dot_nn(keyed, across[...]))
        tb[g] = jnp.concatenate(blocks, axis=1) * LOG2E


BATCH = 4


def canvas_start(step):
    return pl.multiple_of((step // 4) * QUAD_ROWS + (step % 4) * 192, 16)


def attention_forward(
    idx, mine, other, nas, codes_row, codes_col, u, bias, tb,
    mrg, qt, kt, vv, pt, mt, wnat, outt, wout,
    wbuf, waug, wt,
):
    def put(row, head, value):
        wbuf[head, pl.ds(row, 48), :] = value

    assemble(idx, (mine, other), put)
    for j in range(3):
        waug[0:WIDTH, j * WIDTH : (j + 1) * WIDTH] = jnp.concatenate(
            [wbuf[h, :, 96 * j : 96 * (j + 1)] for h in range(4)], axis=1
        )
    out_t = jnp.concatenate([wbuf[h, :, 288:384] for h in range(4)], axis=1)
    outt[...] = out_t
    wout[...] = out_t.T
    waug[WIDTH : WIDTH + 16, :] = bias[...]
    waug[WIDTH + 16 : 512, :] = jnp.zeros((112, 3 * WIDTH), BF)
    wnat[...] = waug[0:WIDTH, :]
    wt[...] = waug[...].T

    def canvases(batch, carry):
        steps = [batch * BATCH + i for i in range(BATCH)]
        units = [(i, w, g) for i in range(BATCH) for w, g in UNITS]
        all_t = [dot_nt(wt[...], nas[s]).astype(BF) for s in steps]
        kv = [dot_nt(nas[s], wt[WIDTH:, :]).astype(BF) for s in steps]
        masks = {}
        for i, s in enumerate(steps):
            for win in range(4):
                row = jnp.concatenate([codes_row[s, 0:1, window(win)]] * PACK, axis=1)
                masks[i, win] = jnp.where(codes_col[s, window(win), 0:1] == row, 0.0, MASKED)
        scores = {
            (i, w, g): dot_nn(kv[i][window(w), feats(g)], spread(all_t[i][feats(g), window(w)]))
            for i, w, g in units
        }
        probs = {}
        for i, w, g in units:
            sc = scores[i, w, g] * (SCALE * LOG2E) + (tb[g] + masks[i, w])
            grown = jnp.exp2(sc - jnp.max(sc, axis=0, keepdims=True))
            probs[i, w, g] = (grown * (1.0 / jnp.sum(grown, axis=0, keepdims=True))).astype(BF)
        mixed = {
            (i, w, g): dot_nn(all_t[i][2 * WIDTH :][feats(g), window(w)], probs[i, w, g])
            for i, w, g in units
        }
        for i, s in enumerate(steps):
            turn, start = s % 4, canvas_start(s)
            merged_t = own_blocks({(w, g): mixed[i, w, g] for w, g in UNITS}).astype(BF)
            back = dot_nt(u[turn], merged_t).astype(BF)
            for w, g in UNITS:
                pt[s, w * GROUPS + g] = probs[i, w, g]
            mt[s] = merged_t
            qt[s] = all_t[i][0:WIDTH]
            kt[s] = all_t[i][WIDTH : 2 * WIDTH]
            vv[s] = kv[i][:, WIDTH:]
            begin = pl.ds(start, 16)
            mrg[begin, :] = back[0:16] + jnp.where(
                turn == 0, jnp.zeros((16, WIDTH), BF), mrg[begin, :]
            )
            mrg[pl.ds(pl.multiple_of(start + 16, 16), SPAN - 16), :] = back[16:]
        return carry

    lax.fori_loop(0, nas.shape[0] // BATCH, canvases, 0)


TILE = 784


def mlp_begin(mrg, tok, outt, par, mid, n2, n2t):
    lane = lax.broadcasted_iota(jnp.int32, (TILE, 128), 1)
    ones = jnp.where(lane == 0, 1.0, 0.0).astype(BF)

    def head_rows(t, carry):
        rows = pl.ds(pl.multiple_of(t * TILE, 16), TILE)
        middle = tok[rows, :].astype(F32) + dot_nt(mrg[rows, :], outt[...]) + par[4:5, :]
        mid[rows, :] = middle
        hat, _ = stats(middle)
        n2[rows, 0:WIDTH] = (hat * par[2:3, :] + par[3:4, :]).astype(BF)
        n2[rows, WIDTH:512] = ones
        return carry

    lax.fori_loop(0, tok.shape[0] // TILE, head_rows, 0)
    n2t[...] = n2[...].T[0:400, :]


HALF = 2 * WIDTH


def mlp_half(other, idx, weights, n2, n2t, got, gout, eb, *refs):
    if other:
        before_m, before_g, before_eb, *refs = refs
        acc_m, acc_g, grads_out, rows_out, *refs = refs
    else:
        acc_m, acc_g, grads_out, ebg, *refs = refs
    eaug, ct, hid, gpr, cg, eg, *refs = refs
    core = idx[3] ^ 1 if other else idx[3]
    for e, k, s, row, head in owners(idx):
        if e == 0:
            start = (k * 4 + (0, 2, 1, 3).index(s)) * 48
            lanes = pl.ds(pl.multiple_of((idx[2] ^ (k & 1)) * WIDTH, 128), WIDTH)
            eaug[pl.ds(row, 48), lanes] = weights[start : start + 48, 0:WIDTH]
            ct[pl.ds(row, 48), lanes] = weights[start : start + 48, WIDTH:]
    for x in range(2):
        lanes = pl.ds(pl.multiple_of((2 * x + core) * WIDTH, 128), WIDTH)
        eaug[WIDTH : WIDTH + 16, x * WIDTH : (x + 1) * WIDTH] = eb[:, lanes]
    eaug[WIDTH + 16 : 512, :] = jnp.zeros((112, HALF), BF)
    pre = dot_nn(n2[...], eaug[...])
    grad_hidden = dot_nn(gout[...], ct[...])
    phi = 0.5 + 0.5 * lax.erf(pre * ROOT_HALF)
    bell = jnp.exp2(pre * pre * (-0.5 * LOG2E)) * INV_ROOT_TWO_PI
    hidden = (pre * phi).astype(BF)
    grad_pre = (grad_hidden * (phi + pre * bell)).astype(BF)
    hid[...] = hidden
    gpr[...] = grad_pre
    if other:
        acc_m[...] = before_m[...] + dot_nt(hidden, ct[...])
        acc_g[...] = before_g[...] + dot_nt(grad_pre, eaug[0:WIDTH, :])
    else:
        acc_m[...] = dot_nt(hidden, ct[...])
        acc_g[...] = dot_nt(grad_pre, eaug[0:WIDTH, :])
    cg[...] = dot_nn(got[...], hid[...]).astype(BF)
    grads = dot_nn(n2t[...], gpr[...])
    eg[...] = grads[0:WIDTH].astype(BF)
    if not other:
        ebg[...] = grads[WIDTH : WIDTH + 8]
    for e, k, s, row, head in owners(idx):
        if e == 0:
            lanes = pl.ds(pl.multiple_of((idx[2] ^ (k & 1)) * WIDTH, 128), WIDTH)
            base = (k * 4 + s) * 48
            grads_out[base : base + 48, 0:WIDTH] = eg[pl.ds(row, 48), lanes]
            grads_out[base : base + 48, WIDTH:] = cg[pl.ds(row, 48), lanes]
    if other:
        (small,) = refs
        small[...] = jnp.zeros(small.shape, F32)
        for x in range(2):
            block = slice(x * WIDTH, (x + 1) * WIDTH)
            for place, part in ((core, grads[WIDTH : WIDTH + 1]), (idx[3], before_eb[0:1, :])):
                lanes = pl.ds(pl.multiple_of(place * WIDTH, 128), WIDTH)
                small[x : x + 1, lanes] = part[:, block]
        rows_out[...] = small[...].astype(BF)
        grads_out[768:784, :] = small[...].astype(BF)


def mlp_end(mid, acc_m, acc_g, gout, par, blk, gmid, sums):
    def tail_rows(t, carry):
        rows = pl.ds(pl.multiple_of(t * TILE, 16), TILE)
        middle = mid[rows, :]
        blk[rows, :] = (middle + acc_m[rows, :] + par[5:6, :]).astype(BF)
        hat, inv = stats(middle)
        g = acc_g[rows, :]
        top = gout[rows, :].astype(F32)
        grad_mid = top + norm_back(g, hat, inv, par[2:3, :])
        gmid[rows, :] = grad_mid
        parts = (g * hat, g, grad_mid, top)
        return tuple(c + jnp.sum(p, axis=0, keepdims=True) for c, p in zip(carry, parts))

    zero = jnp.zeros((1, WIDTH), F32)
    totals = lax.fori_loop(0, mid.shape[0] // TILE, tail_rows, (zero,) * 4)
    sums[...] = jnp.concatenate([zero, zero, *totals, zero, zero], axis=0)


def small_rows(wacc, table, wnat, sums, down, across, small):
    totals = wacc[WIDTH : WIDTH + 1, :]
    high = totals.astype(BF)
    split = [high, (totals - high.astype(F32)).astype(BF), jnp.zeros((6, 3 * WIDTH), BF)]
    offset_sum = jnp.sum(
        dot_nt(jnp.concatenate(split, axis=0), wnat[...]), axis=0, keepdims=True
    )
    products = (wnat[...].astype(F32) * wacc[0:WIDTH, :]).astype(BF)
    gain_sum = dot_nt(jnp.full((8, 3 * WIDTH), 1.0, BF), products)[0:1, :]
    rows = [gain_sum, offset_sum, sums[2:6, :], totals[:, 0:WIDTH], totals[:, 2 * WIDTH :]]
    lines = []
    for g in range(GROUPS):
        high = table[g].astype(BF)
        low = (table[g] - high.astype(F32)).astype(BF)
        both = jnp.concatenate([high, low], axis=0)
        heads = [both[:, h * SLOT : (h + 1) * SLOT] for h in range(PACK)]
        spaced = dot_nt(jnp.concatenate(heads, axis=0), across[...]).astype(BF)
        spaced = [spaced[h * 128 : (h + 1) * 128] for h in range(PACK)]
        spread_out = dot_nn(down[...], jnp.concatenate(spaced, axis=1))
        for h in range(PACK):
            shifted = pltpu.roll(
                spread_out[:, h * 256 : (h + 1) * 256], 0, axis=1, stride=1, stride_axis=0
            )
            lines.append(jnp.sum(shifted, axis=0, keepdims=True)[:, 0:192])
    rows += [jnp.concatenate(lines[2 * i : 2 * i + 2], axis=1) for i in range(6)]
    rows.append(jnp.zeros((2, WIDTH), F32))
    small[...] = jnp.concatenate(rows, axis=0).astype(BF)


def attention_backward(
    idx, gmid, qt, kt, vv, pt, mt, xt, wout, ut, par, wnat, sums, down, across,
    keep, send, gta, small,
    ntall, oacc, wacc, table,
):
    table[...] = jnp.zeros(table.shape, F32)
    oacc[...] = jnp.zeros(oacc.shape, F32)
    wacc[...] = jnp.zeros(wacc.shape, F32)

    def rows_of(parts):
        return jnp.concatenate(
            [jnp.concatenate([parts[w, g] for w in range(4)], axis=1) for g in range(GROUPS)],
            axis=0,
        )

    def canvases(batch, carry):
        steps = [batch * BATCH + i for i in range(BATCH)]
        units = [(i, w, g) for i in range(BATCH) for w, g in UNITS]
        gmw = [
            dot_nn(ut[s % 4], gmid[pl.ds(canvas_start(s), SPAN), :].astype(BF)).astype(BF)
            for s in steps
        ]
        gmt = [dot_nt(wout[...], v).astype(BF) for v in gmw]
        gm_s = {(i, w, g): spread(gmt[i][feats(g), window(w)]) for i, w, g in units}
        gp = {
            (i, w, g): dot_nn(vv[steps[i], window(w), feats(g)], gm_s[i, w, g])
            for i, w, g in units
        }
        gs = {}
        for i, w, g in units:
            probs = pt[steps[i], w * GROUPS + g].astype(F32)
            delta = jnp.sum(probs * gp[i, w, g], axis=0, keepdims=True)
            gs[i, w, g] = (probs * (gp[i, w, g] - delta)).astype(BF)
        q_s = {(i, w, g): spread(qt[steps[i], feats(g), window(w)]) for i, w, g in units}
        gq = {
            (i, w, g): dot_nn(kt[steps[i], feats(g), window(w)], gs[i, w, g])
            for i, w, g in units
        }
        gk = {(i, w, g): dot_nt(q_s[i, w, g], gs[i, w, g]) for i, w, g in units}
        gv = {
            (i, w, g): dot_nt(gm_s[i, w, g], pt[steps[i], w * GROUPS + g]) for i, w, g in units
        }
        g_all = []
        for i in range(BATCH):
            parts = [{(w, g): v[i, w, g] for w, g in UNITS} for v in (gq, gk, gv)]
            g_all.append(
                jnp.concatenate(
                    [
                        (own_blocks(parts[0]) * SCALE).astype(BF),
                        (rows_of(parts[1]) * SCALE).astype(BF),
                        rows_of(parts[2]).astype(BF),
                    ],
                    axis=0,
                )
            )
            gta[steps[i]] = g_all[i]
        wacc[...] += dot_nt(
            jnp.concatenate([xt[s] for s in steps], axis=1), jnp.concatenate(g_all, axis=1)
        )
        oacc[...] += dot_nn(
            jnp.concatenate([mt[s] for s in steps], axis=1), jnp.concatenate(gmw, axis=0)
        )
        for g in range(GROUPS):
            table[g] += sum(gs[i, w, g].astype(F32) for i in range(BATCH) for w in range(4))
        return carry

    lax.fori_loop(0, qt.shape[0] // BATCH, canvases, 0)
    columns = par[...].T
    grads = wacc[0:WIDTH, :] * columns[:, 0:1] + columns[:, 1:2] * wacc[WIDTH : WIDTH + 1, :]
    grads = grads.astype(BF)
    out_t = oacc[...].astype(BF).T
    for h in range(4):
        pieces = [grads[:, j * WIDTH + 96 * h : j * WIDTH + 96 * (h + 1)] for j in range(3)]
        pieces.append(out_t[:, 96 * h : 96 * (h + 1)])
        ntall[h] = jnp.concatenate(pieces, axis=1)
    for e, k, s, row, head in owners(idx):
        base = (k * 4 + s) * 48
        (keep, send)[e][base : base + 48, :] = ntall[head, pl.ds(row, 48), :]
    small_rows(wacc, table, wnat, sums, down, across, small)
    send[768:784, :] = small[...]


def tokens_end(n_state, tok, gmid, gta, wnat, u, par, *refs):
    state, (gtok, *near), arrived = refs[:n_state], refs[n_state:-1], refs[-1]
    copies = [
        pltpu.make_async_copy(source, target, arrived.at[i])
        for i, (source, target) in enumerate(zip(state, near))
    ]
    for copy in copies:
        copy.start()

    def block_rows(block, carry):
        ends = [
            dot_nt(u[turn], gta[4 * block + turn]).astype(BF) for turn in range(4)
        ]
        pieces = [ends[0][0:192]]
        for turn in range(1, 4):
            pieces += [ends[turn - 1][192:] + ends[turn][0:16], ends[turn][16:192]]
        g1 = dot_nt(jnp.concatenate([*pieces, ends[3][192:]], axis=0), wnat[...])
        rows = pl.ds(pl.multiple_of(block * QUAD_ROWS, 16), QUAD_ROWS)
        hat, inv = stats(tok[rows, :].astype(F32))
        gtok[rows, :] = gmid[rows, :] + norm_back(g1, hat, inv, par[0:1, :])
        return carry

    lax.fori_loop(0, gta.shape[0] // 4, block_rows, 0)
    for copy in copies:
        copy.wait()


def join(*refs):
    parts, out = refs[:-1], refs[-1]
    start = 0
    for part in parts:
        out[start : start + part.shape[0], :] = part[...]
        start += part.shape[0]


def plane_sum(keep, got, mine, theirs, own, send1, send2, send3, rest):
    small = mine[...].astype(F32) + theirs[...].astype(F32)
    rest[...] = small
    for k, ref in enumerate((own, send1, send2, send3)):
        block = slice(k * 192, (k + 1) * 192)
        value = keep[block, :].astype(F32) + got[block, :].astype(F32)
        ref[0:192, :] = value.astype(ref.dtype)
        if k:
            ref[192:, :] = small.astype(BF)


def line_sum(own, r1, r2, r3, mine, *refs):
    parts = (r1, r2, r3)
    small = mine[...] + sum(r[192:, :].astype(F32) for r in parts)
    refs[4][...] = small
    for s in range(4):
        block = slice(s * 48, (s + 1) * 48)
        value = own[block, :] + sum(r[block, :].astype(F32) for r in parts)
        if s == 0:
            refs[0][...] = value
        else:
            refs[s][0:48, :] = value.astype(BF)
            refs[s][48:, :] = small.astype(BF)


def half_sum(own, mine, *refs):
    parts, (keep, send, rest) = refs[:-3], refs[-3:]
    rows = own.shape[0]
    half = rows // 2
    total = own[...] + sum(r[0:rows, :].astype(F32) for r in parts)
    small = mine[...] + sum(r[rows:, :].astype(F32) for r in parts)
    keep[...] = total[0:half]
    send[0:half, :] = total[half:].astype(BF)
    send[half:, :] = small.astype(BF)
    rest[...] = small


def adamw(master, grad, moment, square, step_rate, decay_rate):
    moment_new = BETA_ONE * moment + (1.0 - BETA_ONE) * grad
    square_new = BETA_TWO * square + (1.0 - BETA_TWO) * grad * grad
    moment_hat = moment_new * (1.0 / (1.0 - BETA_ONE**STEP))
    square_hat = square_new * (1.0 / (1.0 - BETA_TWO**STEP))
    step = moment_hat / (jnp.sqrt(square_hat) + ADAM_EPS)
    if decay_rate:
        step = step + decay_rate * master
    return master - step_rate * step, moment_new, square_new


def update(refs, grad, outs, step_rate, decay_rate, at=...):
    master, moment, square = (r[at] for r in refs)
    news = adamw(master, grad, moment, square, step_rate, decay_rate)
    for out, new in zip(outs, news):
        out[at] = new


def step_mlp(n_parts, rows, *refs):
    parts, rest, refs = refs[:n_parts], refs[n_parts], refs[n_parts + 1 :]
    ins, outs, total_rest = refs[:6], refs[6:12], refs[12]
    total = sum(r[0:rows, :].astype(F32) for r in parts)
    total_rest[...] = rest[...] + sum(r[rows:, :].astype(F32) for r in parts[1:])
    update(ins[0:3], total[:, 0:WIDTH], outs[0:3], RATE_MATRIX, DECAY_MATRIX)
    update(ins[3:6], total[:, WIDTH:], outs[3:6], RATE_MATRIX, DECAY_MATRIX)


def step_attention(n_parts, rows, idx, *refs):
    parts, refs = refs[:n_parts], refs[n_parts:]
    half = (len(refs) - 2) // 2
    rest, small, ins, outs = refs[0], refs[1], refs[2 : half + 2], refs[half + 2 :]
    total = sum(r[0:rows, :].astype(F32) for r in parts)
    small = small[...] + sum(r[rows:, :].astype(F32) for r in parts[1:])
    head = idx[2] * 2 + idx[3]

    def pick(blocks):
        return sum(jnp.where(head == h, block, 0.0) for h, block in enumerate(blocks))

    for j in range(3):
        update(
            ins[0:3], total[:, 96 * j : 96 * (j + 1)], outs[0:3], RATE_MATRIX, DECAY_MATRIX, at=j
        )
    update(ins[3:6], total[:, 288:384], outs[3:6], RATE_MATRIX, DECAY_MATRIX)
    qv = pick([small[6:8, 96 * h : 96 * (h + 1)] for h in range(4)])
    update(ins[6:9], qv, outs[6:9], RATE_SMALL, 0.0)
    eb = pick([rest[h // 2 : h // 2 + 1, WIDTH * (h % 2) : WIDTH * (h % 2 + 1)] for h in range(4)])
    update(ins[9:12], eb.reshape(ins[9].shape), outs[9:12], RATE_SMALL, 0.0)
    table_rows = ins[12].shape[1]
    lines = [
        small[8 + n // 2 : 9 + n // 2, 192 * (n % 2) : 192 * (n % 2) + table_rows]
        for n in range(12)
    ]
    table = pick([jnp.concatenate(lines[3 * h : 3 * h + 3], axis=0) for h in range(4)])
    update(ins[12:15], table, outs[12:15], RATE_SMALL, 0.0)
    update(ins[15:18], small[0:6, :], outs[15:18], RATE_SMALL, 0.0)


class Links:
    def __init__(self, sizes):
        self.sizes = sizes
        self.outer = sizes["dp"] // 8

    def perm(self, z=0, y=0, x=0, c=0):
        pairs = []
        for flat in range(self.sizes["dp"] * self.sizes["head"]):
            head, dp = flat % 4, flat // 4
            inner, place = dp // self.outer, dp % self.outer
            inner ^= z * 2 + y
            pairs.append((flat, (inner * self.outer + place) * 4 + (head ^ (x * 2 + c))))
        return pairs

    def send(self, value, **flips):
        return lax.ppermute(value, ("dp", "head"), self.perm(**flips))

    def groups(self):
        return [[i * self.outer + j for j in range(self.outer)] for i in range(8)]

    def outer_gather(self, shard):
        if self.outer > 1:
            shard = lax.all_gather(
                shard, "dp", axis=0, tiled=True, axis_index_groups=self.groups()
            )
        return shard

    def gather_line(self, shard):
        return jnp.concatenate([shard] + [self.send(shard, z=s) for s in range(1, 4)], axis=0)

    def gather_plane(self, line):
        return [line] + [self.send(line, x=k & 1, y=k >> 1) for k in range(1, 4)]

    def gather_core(self, plane):
        rows = sum(p.shape[0] for p in plane)
        (plane,) = call(join, [((rows, plane[0].shape[1]), BF)], *plane)
        return plane, self.send(plane, c=1)

    def to_plane(self, blocks):
        return [self.send(b, x=k & 1, y=k >> 1) for k, b in enumerate(blocks, 1)]

    def to_line(self, blocks):
        return [self.send(b, z=s) for s, b in enumerate(blocks, 1)]

    def outer_sum(self, value):
        if self.outer > 1:
            value = lax.psum_scatter(
                value, "dp", scatter_dimension=0, tiled=True, axis_index_groups=self.groups()
            )
        return value


SMEM = pl.BlockSpec(memory_space=pltpu.SMEM)
VMEM = pl.BlockSpec(memory_space=pltpu.VMEM)
HBM = pl.BlockSpec(memory_space=pltpu.HBM)


class Far:
    def __init__(self, value, pinned=False):
        self.value, self.pinned = value, pinned


def placed(arg):
    if isinstance(arg, Far):
        return pltpu.with_memory_space_constraint(arg.value, pltpu.HBM)
    return pltpu.with_memory_space_constraint(arg, pltpu.VMEM)


def call(kernel, outs, *args, scratch=(), limit=10, scalars=None, far=(), time=1, same=()):
    lead = [] if scalars is None else [scalars]
    name = getattr(kernel, "__name__", None) or kernel.func.__name__
    return pl.pallas_call(
        kernel,
        in_specs=[SMEM] * len(lead)
        + [HBM if isinstance(a, Far) and a.pinned else VMEM for a in args],
        out_specs=[VMEM] * len(outs),
        out_shape=[(pltpu.HBM if i in far else pltpu.VMEM)(s, d) for i, (s, d) in enumerate(outs)],
        scratch_shapes=[
            pltpu.SemaphoreType.DMA((s,)) if isinstance(s, int) else pltpu.VMEM(*s)
            for s in scratch
        ],
        compiler_params=pltpu.CompilerParams(vmem_limit_bytes=limit * 2**20),
        cost_estimate=pl.CostEstimate(
            flops=int(time * 1.15e9), bytes_accessed=0, transcendentals=0
        ),
        input_output_aliases={i + len(lead): o for i, o in same},
        name=name,
    )(*lead, *(placed(a) for a in args))


def per_device(links, *args):
    (
        tokens, crop_ids, grad_out, qkv_w, out_w, exp_w, con_w, qv_b, exp_b, table_w, norm_p,
        qkv_m, qkv_s, out_m, out_s, exp_m, exp_s, con_m, con_s,
        qv_m, qv_s, eb_m, eb_s, tab_m, tab_s, norm_m, norm_s,
    ) = args
    rows_all = tokens.shape[0]
    canvases = rows_all // CANVAS
    head = lax.axis_index("head")
    dp = lax.axis_index("dp") // links.outer
    idx = jnp.stack([dp // 2, dp % 2, head // 2, head % 2]).astype(jnp.int32)
    slots = 4 * SLOT
    wide = (rows_all, WIDTH)
    square = (WIDTH, WIDTH)
    fm = (canvases, WIDTH, slots)
    tm = (canvases, slots, WIDTH)

    rows_own = exp_w.shape[0]
    first, second, own = call(
        pack,
        [((rows_own, WIDTH), BF), ((rows_own, 2 * WIDTH), BF), ((16, WIDTH), BF)],
        Far(qkv_w), Far(out_w.T), Far(exp_w), Far(con_w.T), Far(qv_b), Far(exp_b), Far(table_w.T),
    )
    first = links.outer_gather(first)
    line = links.gather_line(first)
    second = links.outer_gather(second)
    pair_s = jnp.concatenate([second, links.send(second, z=2)], axis=0)
    own = jnp.concatenate([own, links.send(own, x=1)], axis=0)
    line, own = lax.optimization_barrier((line, own))
    plane = links.gather_plane(line)
    by_c = links.send(own, c=1)
    crop_rows, _ = lax.optimization_barrier((crop_ids, line))
    crop_rows = crop_rows.reshape(-1, QUAD_ROWS)
    pair_s, crop_rows = lax.optimization_barrier((pair_s, crop_rows))
    line_s = jnp.concatenate([pair_s, links.send(pair_s, z=1)], axis=0)
    rows_c, cols_c = (jnp.asarray(t) for t in tables())
    to_slots = (4, slots, SPAN)
    nas, xt, ut, u, tok, gout, got, code_row, code_col, par, down, across = call(
        prepare,
        [
            ((canvases, slots, 512), BF), ((canvases, 400, slots), BF), (to_slots, BF),
            ((4, SPAN, slots), BF), (wide, BF), (wide, BF), ((WIDTH, rows_all), BF),
            ((canvases, 8, slots), F32), ((canvases, slots, 8), F32), ((8, WIDTH), F32),
            ((128, 2 * SLOT), BF), ((256, SLOT), BF),
        ],
        own, Far(tokens), Far(grad_out), Far(crop_rows), Far(rows_c), Far(cols_c),
        Far(norm_p), limit=12, scalars=idx, time=4,
    )
    by_c, nas = lax.optimization_barrier((by_c, nas))
    bias_t, bias16, eb16 = call(
        spread_small, [((GROUPS, SLOT, slots), F32), ((16, 3 * WIDTH), BF), ((16, HIDDEN), BF)],
        own, by_c, Far(cols_c), across, scratch=[((4, 16, WIDTH), F32)], scalars=idx, time=2,
    )
    *plane, line_s, bias_t = lax.optimization_barrier((*plane, line_s, bias_t))
    plane_s = links.gather_plane(line_s)
    firsts = links.gather_core(plane)
    merged, qt, kt, vv, pt, mt, wnat, outt, wout = call(
        attention_forward,
        [
            (wide, BF), (fm, BF), (fm, BF), (tm, BF), ((canvases, 12, SLOT, slots), BF), (fm, BF),
            ((WIDTH, 3 * WIDTH), BF), (square, BF), (square, BF),
        ],
        *firsts, nas, code_row, code_col, u, bias16, bias_t,
        scratch=[
            ((4, WIDTH, WIDTH), BF), ((512, 3 * WIDTH), BF), ((3 * WIDTH, 512), BF),
        ],
        limit=14, scalars=idx, time=11,
    )
    middle, n2, n2t = call(
        mlp_begin, [(wide, F32), ((rows_all, 512), BF), ((400, rows_all), BF)],
        merged, tok, outt, par, time=3,
    )
    n2, *plane_s = lax.optimization_barrier((n2, *plane_s))
    seconds = links.gather_core(plane_s)
    scratch = [
        ((512, HALF), BF), ((WIDTH, HALF), BF), ((rows_all, HALF), BF), ((rows_all, HALF), BF),
        ((WIDTH, HALF), BF), ((WIDTH, HALF), BF),
    ]
    acc_m, acc_g, keep_r, eb_grad = call(
        functools.partial(mlp_half, False),
        [(wide, F32), (wide, F32), ((768, HALF), BF), ((8, HALF), F32)],
        seconds[0], n2, n2t, got, gout, eb16, scratch=scratch, limit=17, scalars=idx, time=9,
    )
    acc_m, other_s = lax.optimization_barrier((acc_m, seconds[1]))
    acc_m, acc_g, send_r, rest = call(
        functools.partial(mlp_half, True),
        [(wide, F32), (wide, F32), ((784, HALF), BF), ((16, HALF), BF)],
        other_s, n2, n2t, got, gout, eb16, acc_m, acc_g, eb_grad,
        scratch=scratch + [((16, HALF), F32)], limit=17, scalars=idx, time=9, same=((6, 0), (7, 1)),
    )
    got_r = links.send(send_r, c=1)
    block_out, grad_mid, sums = call(
        mlp_end, [(wide, BF), (wide, F32), ((8, WIDTH), F32)], middle, acc_m, acc_g, gout, par,
        limit=10, far=(0,), time=3,
    )
    wide_r = 2 * WIDTH
    block_r = [((192, wide_r), F32)] + [((208, wide_r), BF)] * 3 + [((16, wide_r), F32)]
    got_r, grad_mid = lax.optimization_barrier((got_r, grad_mid))
    own_r, *blocks_r, rest = call(
        plane_sum, block_r, keep_r, got_r, rest, got_r[768:]
    )
    grad_mid, *blocks_r = lax.optimization_barrier((grad_mid, *blocks_r))
    plane_r = links.to_plane(blocks_r)
    state = [
        exp_w, exp_m, exp_s, con_w.T, con_m.T, con_s.T, qkv_w, qkv_m, qkv_s, out_w.T, out_m.T,
        out_s.T, qv_b, qv_m, qv_s, exp_b, eb_m, eb_s, table_w.T, tab_m.T, tab_s.T, norm_p, norm_m,
        norm_s,
    ]
    keep_q, send_q, g_all, small = call(
        attention_backward,
        [
            ((768, WIDTH), BF), ((784, WIDTH), BF), ((canvases, 3 * WIDTH, slots), BF),
            ((16, WIDTH), BF),
        ],
        grad_mid, qt, kt, vv, pt, mt, xt, wout, ut, par, wnat, sums, down, across,
        scratch=[
            ((4, WIDTH, WIDTH), BF), (square, F32), ((400, 3 * WIDTH), F32),
            ((GROUPS, SLOT, slots), F32),
        ],
        limit=20, scalars=idx, time=15,
    )
    *plane_r, send_q = lax.optimization_barrier((*plane_r, send_q))
    got_q = links.send(send_q, c=1)
    own_r, block_r, rest = call(
        half_sum, [((96, wide_r), F32), ((112, wide_r), BF), ((16, wide_r), F32)],
        own_r, rest, *plane_r,
    )
    block_q = [((192, WIDTH), F32)] + [((208, WIDTH), BF)] * 3 + [((16, WIDTH), F32)]
    own_q, *blocks_q, small = call(plane_sum, block_q, keep_q, got_q, small, got_q[768:])
    plane_q = links.to_plane(blocks_q)
    got_r = links.send(block_r, z=2)
    g_all = lax.optimization_barrier((g_all, *blocks_q))[0]
    grad_tokens, *near = call(
        functools.partial(tokens_end, len(state)),
        [(wide, F32)] + [(a.shape, F32) for a in state],
        tok, grad_mid, g_all, wnat, u, par, *(Far(a, pinned=True) for a in state),
        scratch=[len(state)], far=(0,), time=6,
    )
    got_r, grad_tokens = lax.optimization_barrier((got_r, grad_tokens))
    own_r, block_r, rest = call(
        half_sum, [((48, wide_r), F32), ((64, wide_r), BF), ((16, wide_r), F32)],
        own_r, rest, got_r,
    )
    line_q = [((48, WIDTH), F32)] + [((64, WIDTH), BF)] * 3 + [((16, WIDTH), F32)]
    own_q, *blocks_q, small = call(line_sum, line_q, own_q, *plane_q, small)
    parts_q = [own_q, *links.to_line(blocks_q)]
    parts_r = [own_r, links.send(block_r, z=1)]
    rows = 48
    if links.outer > 1:
        small = small + sum(p[48:].astype(F32) for p in parts_q[1:])
        rest = rest + parts_r[1][48:].astype(F32)
        small, rest = lax.psum((small, rest), "dp", axis_index_groups=links.groups())
        parts_q = [links.outer_sum(sum(p[:48].astype(F32) for p in parts_q))]
        parts_r = [links.outer_sum(sum(p[:48].astype(F32) for p in parts_r))]
        rows = parts_q[0].shape[0]
    *third, rest = call(
        functools.partial(step_mlp, len(parts_r), rows),
        [(a.shape, F32) for a in state[:6]] + [((16, wide_r), F32)],
        *parts_r, rest, *near[:6], far=range(6),
    )
    *parts_q, rest = lax.optimization_barrier((*parts_q, rest))
    fourth = call(
        functools.partial(step_attention, len(parts_q), rows),
        [(a.shape, F32) for a in state[6:]], *parts_q, rest, small, *near[6:], scalars=idx,
        far=range(len(state) - 6), time=2, limit=34,
    )
    return (
        block_out, grad_tokens, *fourth[0:3], *(a.T for a in fourth[3:6]), *third[0:3],
        *(a.T for a in third[3:6]), *fourth[6:12], *(a.T for a in fourth[12:15]), *fourth[15:],
    )


def solution(mesh):
    tokens = P(("dp", "head"), None)
    qkv, rows_head, rows_dp = P(None, "dp", "head"), P("head", "dp"), P("dp", "head")
    pair, unit, none = P(None, "head"), P("head"), P()
    matrices = (qkv, rows_head, rows_dp, rows_head)
    small = (pair, unit, pair, none)
    in_specs = (tokens, P("dp"), tokens, *matrices, *small)
    in_specs += tuple(s for spec in (*matrices, *small) for s in (spec, spec))
    out_specs = (tokens, tokens) + tuple(
        s for spec in (*matrices, *small) for s in (spec, spec, spec)
    )
    return jax.shard_map(
        functools.partial(per_device, Links(dict(mesh.shape))),
        mesh=mesh, in_specs=in_specs, out_specs=out_specs, check_vma=False,
    )
```
